32 devices in a mesh: item: 16 (over z, y, x), pipe: 2 (over core).
Axes of the slice: x: 2, y: 2, z: 4, core: 2. Of those that a mesh axis runs over, the one named last changes fastest.
Arguments:
- waveform: bfloat16 [512, 4096], P('item'), may hold values from -6 to 6
- lengths: int32 [512], P('item'), may hold values from 512 to 4096, as said below
- code_ids: int32 [512, 2048], P('item'), may hold values from 0 to 2047
- conv_w: float32 [2, 64, 192], P('pipe'), may hold values from -0.4375 to 0.4375
- point_w: float32 [2, 2, 64, 64], P('pipe'), may hold values from -0.75 to 0.75
- edge_w: float32 [2, 64, 4], P('pipe')
- codebook: float32 [2048, 64], P('pipe'), may hold values from -6 to 6
- conv_mom: float32 [2, 64, 192], P('pipe'), may hold values from -0.01953125 to 0.01953125
- point_mom: float32 [2, 2, 64, 64], P('pipe'), may hold values from -0.01953125 to 0.01953125
- edge_mom: float32 [2, 64, 4], P('pipe'), may hold values from -0.0390625 to 0.0390625
- code_mom: float32 [2048, 64], P('pipe'), may hold values from -1.5258789e-05 to 1.5258789e-05
- conv_avg: float32 [2, 64, 192], P('pipe'), may hold values from -0.4375 to 0.4375
- point_avg: float32 [2, 2, 64, 64], P('pipe'), may hold values from -0.75 to 0.75
- edge_avg: float32 [2, 64, 4], P('pipe')
- code_avg: float32 [2048, 64], P('pipe'), may hold values from -6 to 6
- rate_net: float32 [1], replicated, may hold values from 72.40774 to 144.81548
- rate_code: float32 [1], replicated, may hold values from 185363.8 to 370727.6
Outputs:
- loss_value: float32 [], replicated
- conv_new: float32 [2, 64, 192], P('pipe')
- conv_mom_new: float32 [2, 64, 192], P('pipe')
- conv_avg_new: float32 [2, 64, 192], P('pipe')
- conv_copy: bfloat16 [2, 64, 192], P('pipe')
- point_new: float32 [2, 2, 64, 64], P('pipe')
- point_mom_new: float32 [2, 2, 64, 64], P('pipe')
- point_avg_new: float32 [2, 2, 64, 64], P('pipe')
- point_copy: bfloat16 [2, 2, 64, 64], P('pipe')
- edge_new: float32 [2, 64, 4], P('pipe')
- edge_mom_new: float32 [2, 64, 4], P('pipe')
- edge_avg_new: float32 [2, 64, 4], P('pipe')
- edge_copy: bfloat16 [2, 64, 4], P('pipe')
- code_new: float32 [2048, 64], P('pipe')
- code_mom_new: float32 [2048, 64], P('pipe')
- code_avg_new: float32 [2048, 64], P('pipe')
- code_copy: bfloat16 [2048, 64], P('pipe')
The draws below stay inside these ranges and needn't reach their ends.
Inputs may be any that keep to these rules, and one draw needn't show every extreme that they name: `lengths`: valid frames of a clip, counted from its first frame. `code_ids`: a code number for every latent frame, padded ones too.
All inputs are finite; a program needn't handle non-finite values.
Results may differ from the reference program's by a relative error of at most 0.0087.
Values may be sent and summed in bfloat16 or wider, within the bound.
A program may use at most 512 MiB of HBM per device.

```python
import math
import jax
import jax.numpy as jnp
from jax import lax

CH = 64
DIM = 64
CODES = 2048
DILATION_SIZE = 3
FRAMES = 4096
CLIPS = 16
LAT = 2048
CLIPS_ALL = 512


def draw_lengths(key, part):
    clip_index = jnp.arange(CLIPS_ALL, dtype=jnp.int32)
    floor_len = FRAMES // 8 + clip_index * (5 * FRAMES // 8) // CLIPS_ALL
    jitter = jax.random.randint(key, (CLIPS_ALL,), 0, FRAMES // 4 + 1)
    values = floor_len + jitter
    values = values.at[0].set(FRAMES // 8).at[CLIPS_ALL - 1].set(FRAMES)
    return values.astype(jnp.int32)


def edge_common(key):
    noise = jax.random.normal(key, (2, CH, 4), jnp.float32)
    scales = jnp.array([0.5, (2.0 * CH) ** (-0.5)], jnp.float32)
    return noise * scales[:, None, None]


def draw_edge_w(key, part):
    return edge_common(jax.random.fold_in(key, 3))


def draw_edge_avg(key, part):
    return edge_common(jax.random.fold_in(key, 7))


def plant(values, rng, low, largest):
    place = [jax.random.randint(jax.random.fold_in(rng, axis), (), 0, length) for axis, length in enumerate(values.shape)]
    main_axis = values.shape.index(max(values.shape))
    beside = place[:main_axis] + [(place[main_axis] + 1) % values.shape[main_axis]] + place[main_axis + 1:]
    return values.at[tuple(place)].set(low).at[tuple(beside)].set(largest)


def steps_of(key, shape, cuts, smallest, top_value):
    def one(dim, blocks):
        steps = jax.random.uniform(jax.random.fold_in(jax.random.fold_in(key, 6), dim), (blocks,), jnp.float32, smallest / len(cuts), top_value / len(cuts))
        return jnp.repeat(jnp.exp(steps), shape[dim] // blocks).reshape((-1,) + (1,) * (len(shape) - dim - 1))

    gain = one(*cuts[0])
    for cut in cuts[1:]:
        gain = gain * one(*cut)
    return gain


def centred(own_key, dims, spread, most, split=(), kind=jnp.bfloat16):
    factor_of = steps_of(own_key, dims, split, -0.22, 0.18) if split else 1.0
    values = jax.random.normal(own_key, dims, jnp.float32) * spread * factor_of
    return jnp.minimum(jnp.maximum(values, -most), most).astype(kind)


def setup_inputs(seed: int = 0) -> dict:
    arg_keys = jax.random.split(jax.random.key(seed), 18)
    return {
        "waveform": centred(arg_keys[0], (CLIPS_ALL, FRAMES), 1.0, 6.0, ((0, 16),)),
        "lengths": draw_lengths(jax.random.fold_in(arg_keys[17], 71), 0),
        "code_ids": plant(jax.random.randint(arg_keys[2], (CLIPS_ALL, LAT), 0, CODES), jax.random.fold_in(arg_keys[2], 1), 0, CODES - 1).astype(jnp.int32),
        "conv_w": centred(arg_keys[3], (2, CH, 3 * CH), (3 * CH) ** -0.5, 0.4375, ((0, 2),), jnp.float32),
        "point_w": centred(arg_keys[4], (2, 2, CH, CH), CH ** -0.5, 0.75, ((0, 2),), jnp.float32),
        "edge_w": draw_edge_w(jax.random.fold_in(arg_keys[17], 71), 0),
        "codebook": centred(arg_keys[6], (CODES, DIM), 1.0, 6.0, ((0, 2),), jnp.float32),
        "conv_mom": centred(arg_keys[7], (2, CH, 3 * CH), (2.0 / (CLIPS_ALL * FRAMES) ** 0.5), 0.01953125, ((0, 2),), jnp.float32),
        "point_mom": centred(arg_keys[8], (2, 2, CH, CH), (2.0 / (CLIPS_ALL * FRAMES) ** 0.5), 0.01953125, ((0, 2),), jnp.float32),
        "edge_mom": centred(arg_keys[9], (2, CH, 4), (4.0 / (CLIPS_ALL * FRAMES) ** 0.5), 0.0390625, ((0, 2),), jnp.float32),
        "code_mom": centred(arg_keys[10], (CODES, DIM), (0.1 * (CLIPS_ALL * LAT // CODES) ** 0.5 / (CLIPS_ALL * FRAMES)), 1.52587890625e-05, ((0, 2),), jnp.float32),
        "conv_avg": centred(arg_keys[11], (2, CH, 3 * CH), (3 * CH) ** -0.5, 0.4375, ((0, 2),), jnp.float32),
        "point_avg": centred(arg_keys[12], (2, 2, CH, CH), CH ** -0.5, 0.75, ((0, 2),), jnp.float32),
        "edge_avg": draw_edge_avg(jax.random.fold_in(arg_keys[17], 71), 0),
        "code_avg": centred(arg_keys[14], (CODES, DIM), 1.0, 6.0, ((0, 2),), jnp.float32),
        "rate_net": jnp.clip(jnp.exp(jax.random.uniform(arg_keys[15], (1,), jnp.float32, math.log(72.40774), math.log(144.81548))), 72.40774, 144.81548),
        "rate_code": jnp.clip(jnp.exp(jax.random.uniform(arg_keys[16], (1,), jnp.float32, math.log(185363.8), math.log(370727.6))), 185363.8, 370727.6),
    }


HIGH_PRECISION = lax.Precision.HIGHEST
COMMIT = 0.02
MOMENTUM = 0.9
AVERAGE = 0.99

@jax.custom_vjp
def lowered_precision(v):
    return lax.optimization_barrier(v.astype(jnp.bfloat16)).astype(jnp.float32)

@jax.custom_vjp
def lowered_backward(v):
    return v

def low_keep(v):
    return (lowered_precision(v), None)

def low_pass(kept, grad):
    return (grad,)

def back_keep(v):
    return (v, None)

def back_low(kept, grad):
    return (lowered_precision(grad),)
lowered_precision.defvjp(low_keep, low_pass)
lowered_backward.defvjp(back_keep, back_low)

def shift_along(values, offset):
    if offset > 0:
        pad_zero = jnp.zeros(values.shape[:-1] + (offset,), values.dtype)
        return jnp.concatenate([values[..., offset:], pad_zero], -1)
    if offset < 0:
        pad_zero = jnp.zeros(values.shape[:-1] + (-offset,), values.dtype)
        return jnp.concatenate([pad_zero, values[..., :offset]], -1)
    return values

def spread_kernel_taps(values, reach):
    return jnp.concatenate([shift_along(values, -reach), values, shift_along(values, reach)], 1)

def input_taps(signal):
    phases = signal.reshape(signal.shape[0], -1, 2)
    even_part = phases[..., 0]
    odd_part = phases[..., 1]
    return jnp.stack([shift_along(odd_part, -1), even_part, odd_part, shift_along(even_part, 1)], 1)

def block_ref(entry_val, convolution_scaled, point_s):
    activation_unit = lowered_precision(jax.nn.relu(entry_val))
    inner_output_rows = lowered_backward(jnp.einsum('fw,ywi->yfi', lowered_precision(convolution_scaled), spread_kernel_taps(activation_unit, DILATION_SIZE), precision=HIGH_PRECISION))
    act_p = lowered_precision(jax.nn.relu(inner_output_rows))
    return entry_val + lowered_backward(jnp.einsum('fw,ywi->yfi', lowered_precision(point_s), act_p, precision=HIGH_PRECISION))

def encode_ref(convolution_scaled, point_s, edge_s, signal):
    hidden = lowered_backward(jnp.einsum('ck,bkt->bct', lowered_precision(edge_s), input_taps(signal), precision=HIGH_PRECISION))
    result = block_ref(hidden, convolution_scaled, point_s[0])
    return lowered_backward(lowered_precision(jnp.einsum('fw,ywi->yfi', lowered_precision(point_s[1]), lowered_precision(result), precision=HIGH_PRECISION)))

def decode_ref(convolution_scaled, point_s, edge_s, chosen, signal, frame_mask):
    dec_in = lowered_backward(jnp.einsum('fw,ywi->yfi', lowered_precision(point_s[0]), chosen, precision=HIGH_PRECISION))
    result = block_ref(dec_in, convolution_scaled, point_s[1])
    outs_four = lowered_backward(jnp.einsum('ck,bct->bkt', lowered_precision(edge_s), lowered_precision(result), precision=HIGH_PRECISION))
    even_out = outs_four[:, 1] + shift_along(outs_four[:, 3], -1)
    odd_out = outs_four[:, 2] + shift_along(outs_four[:, 0], 1)
    rebuilt = jnp.stack([even_out, odd_out], -1).reshape(signal.shape)
    error = jnp.where(frame_mask, rebuilt - signal, 0.0)
    return jnp.sum(error * error)

def lookup(table, ids):
    return jnp.swapaxes(jnp.take(table, ids, axis=0), 1, 2)

def nesterov(weight, grad, moment, average, rate):
    moment_new = MOMENTUM * moment + grad
    weight_new = weight - rate * (grad + MOMENTUM * moment_new)
    average_new = AVERAGE * average + (1.0 - AVERAGE) * weight_new
    return (weight_new, moment_new, average_new, weight_new.astype(jnp.bfloat16))

def reference(waveform, lengths, code_ids, conv_w, point_w, edge_w, codebook, conv_mom, point_mom, edge_mom, code_mom, conv_avg, point_avg, edge_avg, code_avg, rate_net, rate_code):
    groups = CLIPS_ALL // CLIPS
    signal_all = waveform.astype(jnp.float32).reshape(groups, CLIPS, FRAMES)
    len_all = lengths.reshape(groups, CLIPS)
    id_all = code_ids.reshape(groups, CLIPS, LAT)
    params = (conv_w, point_w, edge_w, codebook)

    def one_group(carry, batch):
        signal, lens, ids = batch
        frame_mask = jnp.arange(FRAMES)[None, :] < lens[:, None]
        lat_valid = 2 * jnp.arange(LAT)[None, :] < lens[:, None]
        masked = jnp.where(frame_mask, signal, 0.0)
        latent_val = encode_ref(conv_w[0], point_w[0], edge_w[0], masked)
        chosen_val = lookup(lowered_precision(codebook), ids)

        def loss_fn(conv_p, point_p, edge_p, code_p):
            latent = encode_ref(conv_p[0], point_p[0], edge_p[0], masked)
            chosen = lookup(lowered_precision(code_p), ids)
            gap = jnp.where(lat_valid[:, None, :], latent - chosen, 0.0)
            straight = latent + (chosen_val - latent_val)
            rebuilt_loss = decode_ref(conv_p[1], point_p[1], edge_p[1], straight, signal, frame_mask)
            return rebuilt_loss + COMMIT * jnp.sum(gap * gap)
        value, pullback = jax.vjp(loss_fn, *params)
        grads = pullback(jnp.ones_like(value))
        summed = tuple((a + b for a, b in zip(carry[0], grads)))
        return ((summed, carry[1] + value), None)
    start = (tuple((jnp.zeros_like(p) for p in params)), jnp.zeros((), jnp.float32))
    (grads, total), unused = lax.scan(one_group, start, (signal_all, len_all, id_all))
    count = jnp.sum(lengths).astype(jnp.float32)
    grads = tuple((g / count for g in grads))
    conv_out = nesterov(conv_w, grads[0], conv_mom, conv_avg, rate_net[0])
    point_out = nesterov(point_w, grads[1], point_mom, point_avg, rate_net[0])
    edge_out = nesterov(edge_w, grads[2], edge_mom, edge_avg, rate_net[0])
    code_out = nesterov(codebook, grads[3], code_mom, code_avg, rate_code[0])
    return (total / count, conv_out[0], conv_out[1], conv_out[2], conv_out[3], point_out[0], point_out[1], point_out[2], point_out[3], edge_out[0], edge_out[1], edge_out[2], edge_out[3], code_out[0], code_out[1], code_out[2], code_out[3])
```

```python
import functools

import jax
import jax.numpy as jnp
from jax import lax
from jax.experimental import pallas as pl
from jax.experimental.pallas import tpu as pltpu
from jax.sharding import PartitionSpec as P

REACH = 3
COMMIT = 0.02
MOMENTUM = 0.9
AVERAGE = 0.99

LANES = 128
TILE = 512
SLOTS = 8
LOW = 256
SPARE = 16
REAL = 8

F32 = jnp.float32
BF16 = jnp.bfloat16


def nn(a, b):
    return lax.dot_general(a, b, (((1,), (0,)), ((), ())), preferred_element_type=F32)


def nt(a, b):
    return lax.dot_general(a, b, (((1,), (1,)), ((), ())), preferred_element_type=F32)


def moved(ext, distance):
    width = ext.shape[1]
    turned = ext if distance == 0 else pltpu.roll(ext, (-distance) % width, 1)
    return turned[:, LANES : width - LANES]


def relu_bf(values):
    return jnp.maximum(values, 0.0).astype(BF16)


def stack(rows, times):
    return jnp.concatenate([rows] * times, axis=0)


def net_kernel(
    rank_ref,
    len_ref,
    wave_ref,
    ids_ref,
    conv_ref,
    conv_t_ref,
    point_ref,
    point_t_ref,
    edge_ref,
    edge_t_ref,
    table_ref,
    g_conv,
    g_point,
    g_edge,
    g_table,
    loss_ref,
    src_list,
    len_list,
    even_scr,
    odd_scr,
    code_scr,
    sig_r,
    msk_r,
    live_r,
    me_r,
    strips_r,
    onehot_r,
    hi_r,
    hidden_r,
    actu_e_r,
    chosen_r,
    decin_r,
    actu_d_r,
    actp_e_r,
    encres_r,
    actp_d_r,
    resb_r,
    gap_r,
    outs_r,
    dres_r,
    dinner_d_r,
    denc_r,
    dinner_e_r,
):
    clips, frames = wave_ref.shape
    half = frames // 2
    per_clip = half // LANES
    width = conv_ref.shape[1]
    groups = table_ref.shape[0] // width
    per_tile = TILE // LANES
    rank = rank_ref[0]

    for ref in (
        sig_r, msk_r, live_r, me_r, strips_r, onehot_r, hi_r, hidden_r, actu_e_r, chosen_r,
        decin_r, actu_d_r, actp_e_r, encres_r, actp_d_r, resb_r, gap_r, outs_r, dres_r,
        dinner_d_r, denc_r, dinner_e_r,
    ):

        @pl.loop(0, SLOTS)
        def _(slot, ref=ref):
            ref[:, pl.ds(pl.multiple_of(slot * TILE, TILE), TILE)] = jnp.zeros(
                (ref.shape[0], TILE), ref.dtype
            )

    for ref in (g_conv, g_point, g_edge, g_table, loss_ref):
        ref[...] = jnp.zeros(ref.shape, ref.dtype)

    row_at = lax.broadcasted_iota(jnp.int32, (2 * LANES, 2 * LANES), 0)
    col_at = lax.broadcasted_iota(jnp.int32, (2 * LANES, 2 * LANES), 1)
    wanted = jnp.where(col_at < LANES, 2 * col_at, 2 * (col_at - LANES) + 1)
    split = jnp.where(row_at == wanted, 1.0, 0.0).astype(BF16)
    for block in range(per_clip):
        parted = nn(wave_ref[:, block * 2 * LANES : (block + 1) * 2 * LANES], split)
        even_scr[block] = parted[:, :LANES]
        odd_scr[block] = parted[:, LANES:]
        code_scr[block] = ids_ref[:, block * LANES : (block + 1) * LANES]

    def put(index, source, length):
        src_list[index] = source
        len_list[index] = length

    put(0, 0, -frames)

    def add_clip(c, filled):
        clip = 2 * c + rank
        length = len_ref[clip]
        blocks = lax.shift_right_logical(
            lax.shift_right_logical(length + 1, 1) + (SPARE + LANES - 1), 7
        )

        def add_block(k, carry):
            put(filled + k, clip * 32 + k, length)
            return carry

        lax.fori_loop(0, blocks, add_block, 0)
        return filled + blocks

    filled = lax.fori_loop(0, clips // 2, add_clip, jnp.int32(1))
    tiles = lax.div(filled - 1 + per_tile - 1, jnp.int32(per_tile)) + 4

    def add_empty(k, carry):
        put(filled + k, 0, -frames)
        return carry

    lax.fori_loop(0, 6 * per_tile + 2, add_empty, 0)

    sub = lax.broadcasted_iota(jnp.int32, (8, LANES), 0)
    lane = lax.broadcasted_iota(jnp.int32, (8, LANES), 1)
    sub_ext = lax.broadcasted_iota(jnp.int32, (8, TILE + 2 * LANES), 0)
    sub_tile = lax.broadcasted_iota(jnp.int32, (8, TILE), 0)
    iota16 = lax.broadcasted_iota(jnp.int32, (16, TILE), 0).astype(F32).astype(BF16)

    def taps(ext):
        later = moved(ext, 1)
        earlier = moved(ext, -1)
        other = jnp.where(sub_tile == 0, later, jnp.where(sub_tile == 1, earlier, 0.0))
        return jnp.concatenate([moved(ext, 0), other], axis=0)

    @pl.loop(0, tiles)
    def _(i):
        def at(lag):
            return pl.multiple_of(lax.rem(i - lag + SLOTS, SLOTS) * TILE, TILE)

        def cur(ref, lag):
            return ref[:, pl.ds(at(lag), TILE)]

        def last_of(ref, lag):
            return ref[:, pl.ds(at(lag) + (TILE - LANES), LANES)]

        def first_of(ref, lag):
            return ref[:, pl.ds(at(lag), LANES)]

        def ext(ref, lag, following):
            return jnp.concatenate([last_of(ref, lag + 1), cur(ref, lag), following], axis=1)

        def keep(ref, lag, value):
            ref[:, pl.ds(at(lag), TILE)] = value

        e2_actu_e = (last_of(actu_e_r, 2), cur(actu_e_r, 1))
        e2_actu_d = (last_of(actu_d_r, 2), cur(actu_d_r, 1))
        e3_outs = (last_of(outs_r, 3), cur(outs_r, 2))
        e4_din = (last_of(dinner_d_r, 4), cur(dinner_d_r, 3))
        e5_din = (last_of(dinner_e_r, 5), cur(dinner_e_r, 4))
        chosen1, chosen3 = cur(chosen_r, 1), cur(chosen_r, 3)
        hidden1, decin1 = cur(hidden_r, 1), cur(decin_r, 1)
        onehot1, hi1, me1 = cur(onehot_r, 1), cur(hi_r, 1), cur(me_r, 1)
        actp_d2, resb2 = cur(actp_d_r, 2), cur(resb_r, 2)
        actu_d3, actp_e3, encres3, gap3, dres3 = (
            cur(actu_d_r, 3), cur(actp_e_r, 3), cur(encres_r, 3), cur(gap_r, 3), cur(dres_r, 3)
        )
        actu_e4, denc4, strips4 = cur(actu_e_r, 4), cur(denc_r, 4), cur(strips_r, 4)
        sig2 = ext(sig_r, 2, first_of(sig_r, 1))
        msk2 = ext(msk_r, 2, first_of(msk_r, 1))
        live2 = cur(live_r, 2)
        live2_ext = ext(live_r, 2, first_of(live_r, 1))

        sigs, msks, lives, mes, los, his = [], [], [], [], [], []
        for j in range(-1, per_tile + 1):
            index = i * per_tile + (j + 1)
            source, length = src_list[index], len_list[index]
            clip = lax.shift_right_logical(source, 5)
            block = jnp.bitwise_and(source, 31)
            here = (jnp.minimum(block, per_clip - 1), pl.ds(clip, 1), slice(None))
            t = block * LANES + lane
            even_ok = 2 * t < length
            odd_ok = 2 * t + 1 < length
            even = jnp.broadcast_to(even_scr[here], (8, LANES))
            odd = jnp.broadcast_to(odd_scr[here], (8, LANES))
            sigs.append(
                jnp.where((sub == 0) & even_ok, even, jnp.where((sub == 1) & odd_ok, odd, 0.0))
            )
            if 0 <= j < per_tile:
                valid = lax.shift_right_arithmetic(length + 1, 1)
                live = t < jnp.minimum(valid + REAL, half)
                code = jnp.broadcast_to(code_scr[here], (8, LANES))
                msks.append(
                    jnp.where(((sub == 0) & even_ok) | ((sub == 1) & odd_ok), 1.0, 0.0)
                )
                lives.append(jnp.where(live, 1.0, 0.0))
                mes.append(jnp.where(even_ok, 1.0, 0.0))
                los.append(jnp.where(live, jnp.bitwise_and(code, LOW - 1), -1).astype(F32))
                his.append(lax.shift_right_logical(code, 8).astype(F32))
        sig_ext = jnp.concatenate(sigs, axis=1)
        live0 = jnp.concatenate(lives, axis=1)
        strips = (taps(sig_ext) * stack(live0, 2)).astype(BF16)
        hidden = nn(edge_ref[0], strips)
        actu_e = relu_bf(hidden)

        low16 = stack(jnp.concatenate(los, axis=1), 2).astype(BF16) - iota16
        onehot = jnp.concatenate(
            [
                jnp.where(low16 == float(16 * r), jnp.ones((), BF16), jnp.zeros((), BF16))
                for r in range(LOW // 16)
            ],
            axis=0,
        )
        picked = nn(table_ref[...], onehot)
        hi0 = jnp.concatenate(his, axis=1)
        parts = [jnp.zeros((8, TILE), F32) for _ in range(width // 8)]
        for h in range(groups):
            here = hi0 == float(h)
            parts = [
                jnp.where(here, picked[h * width + 8 * r : h * width + 8 * r + 8], parts[r])
                for r in range(width // 8)
            ]
        chosen = jnp.concatenate(parts, axis=0).astype(BF16)
        decin = nn(point_ref[2], chosen)
        actu_d = relu_bf(decin)

        keep(sig_r, 0, moved(sig_ext, 0))
        keep(msk_r, 0, jnp.concatenate(msks, axis=1))
        keep(live_r, 0, live0)
        keep(me_r, 0, jnp.concatenate(mes, axis=1))
        keep(hi_r, 0, stack(hi0, 2).astype(BF16))
        keep(strips_r, 0, strips)
        keep(onehot_r, 0, onehot)
        keep(hidden_r, 0, hidden)
        keep(actu_e_r, 0, actu_e)
        keep(chosen_r, 0, chosen)
        keep(decin_r, 0, decin)
        keep(actu_d_r, 0, actu_d)

        def spread(pair, following):
            whole = jnp.concatenate([*pair, following], axis=1)
            return jnp.concatenate([moved(whole, d) for d in (-REACH, 0, REACH)], axis=0)

        def spread_back(pair, following):
            whole = jnp.concatenate([*pair, following], axis=1)
            return jnp.concatenate([moved(whole, d) for d in (REACH, 0, -REACH)], axis=0)

        actp_e = relu_bf(nn(conv_ref[0], spread(e2_actu_e, actu_e[:, :LANES])))
        encres = (hidden1 + nn(point_ref[0], actp_e)).astype(BF16)
        latent = nn(point_ref[1], encres).astype(BF16)
        gap = (latent.astype(F32) - chosen1.astype(F32)) * stack(me1, width // 8)
        gap_bf = gap.astype(BF16)
        square = gap * gap
        loss_rows = square[:8]
        for r in range(1, width // 8):
            loss_rows = loss_rows + square[8 * r : 8 * r + 8]
        terms = []
        for h in range(groups):
            here = hi1 == float(h)
            terms += [
                jnp.where(here, gap_bf[16 * r : 16 * r + 16], jnp.zeros((), BF16))
                for r in range(width // 16)
            ]
        g_table[...] += nt(jnp.concatenate(terms, axis=0), onehot1)

        actp_d = relu_bf(nn(conv_ref[1], spread(e2_actu_d, actu_d[:, :LANES])))
        resb = (decin1 + nn(point_ref[3], actp_d)).astype(BF16)
        outs = nn(edge_t_ref[1], resb)
        keep(actp_e_r, 1, actp_e)
        keep(encres_r, 1, encres)
        keep(gap_r, 1, gap * (2.0 * COMMIT))
        keep(actp_d_r, 1, actp_d)
        keep(resb_r, 1, resb)
        keep(outs_r, 1, outs)

        outs_ext = jnp.concatenate([*e3_outs, outs[:, :LANES]], axis=1) * stack(live2_ext, 2)
        shifted = outs_ext[8:]
        wide = TILE + 2 * LANES
        crossed = jnp.where(
            sub_ext == 0, pltpu.roll(shifted, 1, 1), pltpu.roll(shifted, wide - 1, 1)
        )
        error = (outs_ext[:8] + crossed - sig2) * msk2
        middle = moved(error, 0)
        loss_rows = COMMIT * loss_rows + middle * middle
        loss_sum = loss_rows[:, :LANES]
        for j in range(1, per_tile):
            loss_sum = loss_sum + loss_rows[:, j * LANES : (j + 1) * LANES]
        loss_ref[...] += loss_sum
        douts = (2.0 * taps(error) * stack(live2, 2)).astype(BF16)
        g_edge[1] += nt(resb2, douts)
        dres = nn(edge_ref[1], douts)
        dbranch = dres.astype(BF16)
        g_point[3] += nt(dbranch, actp_d2)
        dinner_d = jnp.where(actp_d2 > 0, nn(point_t_ref[3], dbranch).astype(BF16), 0)
        keep(dres_r, 2, dres)
        keep(dinner_d_r, 2, dinner_d)

        around = spread_back(e4_din, dinner_d[:, :LANES])
        g_conv[1] += nt(around, actu_d3)
        ddecin = (dres3 + jnp.where(actu_d3 > 0, nn(conv_t_ref[1], around), 0.0)).astype(BF16)
        g_point[2] += nt(ddecin, chosen3)
        dlatent = (nn(point_t_ref[2], ddecin) + gap3).astype(BF16)
        g_point[1] += nt(dlatent, encres3)
        denc = nn(point_t_ref[1], dlatent)
        dbranch_e = denc.astype(BF16)
        g_point[0] += nt(dbranch_e, actp_e3)
        dinner_e = jnp.where(actp_e3 > 0, nn(point_t_ref[0], dbranch_e).astype(BF16), 0)
        keep(denc_r, 3, denc)
        keep(dinner_e_r, 3, dinner_e)

        around_e = spread_back(e5_din, dinner_e[:, :LANES])
        g_conv[0] += nt(around_e, actu_e4)
        dhidden = (denc4 + jnp.where(actu_e4 > 0, nn(conv_t_ref[0], around_e), 0.0)).astype(BF16)
        g_edge[0] += nt(dhidden, strips4)


def net(rank, lengths, waveform, code_ids, conv, conv_t, point, point_t, edge, edge_t, table):
    clips, frames = waveform.shape
    width = conv.shape[1]
    columns = SLOTS * TILE
    listed = (clips // 2) * (frames // 2 // LANES + 1) + 8 * (TILE // LANES) + 8
    smem = pl.BlockSpec(memory_space=pltpu.SMEM)
    vmem = pl.BlockSpec(memory_space=pltpu.VMEM)

    def ring(rows, dtype):
        return pltpu.VMEM((rows, columns), dtype)

    return pl.pallas_call(
        net_kernel,
        out_shape=(
            jax.ShapeDtypeStruct((2, 3 * width, width), F32),
            jax.ShapeDtypeStruct((4, width, width), F32),
            jax.ShapeDtypeStruct((2, width, 16), F32),
            jax.ShapeDtypeStruct(table.shape, F32),
            jax.ShapeDtypeStruct((8, LANES), F32),
        ),
        in_specs=[smem, smem] + [vmem] * 9,
        out_specs=(vmem,) * 5,
        scratch_shapes=[
            pltpu.SMEM((listed,), jnp.int32),
            pltpu.SMEM((listed,), jnp.int32),
            pltpu.VMEM((frames // 2 // LANES, clips, LANES), F32),
            pltpu.VMEM((frames // 2 // LANES, clips, LANES), F32),
            pltpu.VMEM((frames // 2 // LANES, clips, LANES), jnp.int32),
            ring(8, F32),
            ring(8, F32),
            ring(8, F32),
            ring(8, F32),
            ring(16, BF16),
            ring(LOW, BF16),
            ring(16, BF16),
            ring(width, F32),
            ring(width, BF16),
            ring(width, BF16),
            ring(width, F32),
            ring(width, BF16),
            ring(width, BF16),
            ring(width, BF16),
            ring(width, BF16),
            ring(width, BF16),
            ring(width, F32),
            ring(16, F32),
            ring(width, F32),
            ring(width, BF16),
            ring(width, F32),
            ring(width, BF16),
        ],
        compiler_params=pltpu.CompilerParams(vmem_limit_bytes=48 * 2**20),
    )(rank, lengths, waveform, code_ids, conv, conv_t, point, point_t, edge, edge_t, table)


def nesterov(weight, grad, moment, average, rate):
    moment_new = MOMENTUM * moment + grad
    weight_new = weight - rate * (grad + MOMENTUM * moment_new)
    average_new = AVERAGE * average + (1.0 - AVERAGE) * weight_new
    return (weight_new, moment_new, average_new, weight_new.astype(jnp.bfloat16))


def per_device(
    waveform,
    lengths,
    code_ids,
    conv_w,
    point_w,
    edge_w,
    codebook,
    conv_mom,
    point_mom,
    edge_mom,
    code_mom,
    conv_avg,
    point_avg,
    edge_avg,
    code_avg,
    rate_net,
    rate_code,
):
    width = conv_w.shape[1]
    rank = lax.axis_index("pipe").reshape(1).astype(jnp.int32)
    own_rows = codebook.shape[0]

    def gathered(block):
        return lax.all_gather(block, "pipe", axis=0, tiled=True)

    own_table = codebook.astype(BF16).reshape(own_rows // LOW, LOW, width)
    own_table = jnp.swapaxes(own_table, 1, 2).reshape(own_rows // LOW * width, LOW)
    table = gathered(own_table)
    conv = gathered(conv_w.astype(BF16))
    point = gathered(point_w.astype(BF16).reshape(2, width, width))
    edge = gathered(edge_w.astype(BF16))
    conv_t = jnp.transpose(conv.reshape(2, width, 3, width), (0, 3, 2, 1)).reshape(conv.shape)
    point_t = jnp.swapaxes(point, 1, 2)
    gaps = jnp.zeros((2, width, 6), BF16)
    edge16 = jnp.concatenate([edge[:, :, 1:3], gaps, edge[:, :, 3:], edge[:, :, :1], gaps], -1)
    edge16_t = jnp.swapaxes(edge16, 1, 2)

    g_conv, g_point, g_edge, g_table, loss_rows = net(
        rank, lengths, waveform, code_ids, conv, conv_t, point, point_t, edge16, edge16_t, table
    )
    code_grad = lax.psum_scatter(g_table, "pipe", scatter_dimension=0, tiled=True)
    code_grad = lax.psum(code_grad, "item")
    net_grad = jnp.concatenate(
        [g_conv.reshape(2, -1), g_point.reshape(2, -1), g_edge.reshape(2, -1)], axis=1
    )
    net_grad = lax.psum_scatter(net_grad, "pipe", scatter_dimension=0, tiled=True)
    net_grad, count_all = lax.psum((net_grad[0], jnp.sum(lengths).astype(F32)), "item")
    loss_sum = lax.psum(jnp.sum(loss_rows), ("item", "pipe"))

    sizes = (3 * width * width, 2 * width * width)
    conv_grad = net_grad[: sizes[0]].reshape(3, width, width)
    conv_grad = jnp.transpose(conv_grad, (1, 0, 2)).reshape(1, width, 3 * width)
    point_grad = net_grad[sizes[0] : sizes[0] + sizes[1]].reshape(1, 2, width, width)
    edge_grad = net_grad[sizes[0] + sizes[1] :].reshape(1, width, 16)
    edge_grad = jnp.concatenate(
        [edge_grad[:, :, 9:10], edge_grad[:, :, :2], edge_grad[:, :, 8:9]], -1
    )
    code_grad = code_grad.reshape(own_rows // LOW, width, LOW)
    code_grad = jnp.swapaxes(code_grad, 1, 2).reshape(own_rows, width) * (-2.0 * COMMIT)
    conv_out = nesterov(conv_w, conv_grad / count_all, conv_mom, conv_avg, rate_net[0])
    point_out = nesterov(point_w, point_grad / count_all, point_mom, point_avg, rate_net[0])
    edge_out = nesterov(edge_w, edge_grad / count_all, edge_mom, edge_avg, rate_net[0])
    code_out = nesterov(codebook, code_grad / count_all, code_mom, code_avg, rate_code[0])
    return (loss_sum / count_all, *conv_out, *point_out, *edge_out, *code_out)


def solution(mesh):
    weights = (
        P("pipe", None, None),
        P("pipe", None, None, None),
        P("pipe", None, None),
        P("pipe", None),
    )
    return jax.shard_map(
        per_device,
        mesh=mesh,
        in_specs=(P("item", None), P("item"), P("item", None), *weights, *weights, *weights, P(), P()),
        out_specs=(P(),) + tuple(spec for spec in weights for _ in range(4)),
        check_vma=False,
    )
```

```python
import functools

import jax
import jax.numpy as jnp
from jax import lax
from jax.experimental import pallas as pl
from jax.experimental.pallas import tpu as pltpu
from jax.sharding import PartitionSpec as P

REACH = 3
COMMIT = 0.02
MOMENTUM = 0.9
AVERAGE = 0.99

LANES = 128
TILE = 512
SLOTS = 8
LOW = 256
SPARE = 16
REAL = 8

MESH = pl.DeviceIdType.MESH
F32 = jnp.float32
BF16 = jnp.bfloat16


def nn(a, b):
    return lax.dot_general(a, b, (((1,), (0,)), ((), ())), preferred_element_type=F32)


def nt(a, b):
    return lax.dot_general(a, b, (((1,), (1,)), ((), ())), preferred_element_type=F32)


def moved(ext, distance):
    width = ext.shape[1]
    turned = ext if distance == 0 else pltpu.roll(ext, (-distance) % width, 1)
    return turned[:, LANES : width - LANES]


def relu_bf(values):
    return jnp.maximum(values, 0.0).astype(BF16)


def stack(rows, times):
    return jnp.concatenate([rows] * times, axis=0)


def net_kernel(
    len_ref,
    wave_ref,
    ids_ref,
    weight_ref,
    payload_ref,
    stats_ref,
    g_conv,
    g_point,
    g_edge,
    g_table,
    loss_ref,
    src_list,
    len_list,
    even_scr,
    odd_scr,
    code_scr,
    sig_r,
    msk_r,
    live_r,
    me_r,
    strips_r,
    onehot_r,
    hi_r,
    hidden_r,
    actu_e_r,
    chosen_r,
    decin_r,
    actu_d_r,
    actp_e_r,
    encres_r,
    actp_d_r,
    resb_r,
    gap_r,
    outs_r,
    dres_r,
    dinner_d_r,
    denc_r,
    dinner_e_r,
):
    sets, per_clip = wave_ref.shape[:2]
    half = per_clip * LANES
    frames = 2 * half
    width = 64
    groups = 2 * (weight_ref.shape[1] - 4 * width - 16) // width
    table_rows = groups // 2 * width
    per_tile = TILE // LANES

    def weight(part, start, rows, first, columns):
        start += table_rows
        return weight_ref[part, start : start + rows, first : first + columns]

    conv = [weight(part, 0, width, 0, 3 * width) for part in range(2)]
    conv_t = [weight(part, width, width, 0, 3 * width) for part in range(2)]
    point = [weight(k // 2, 2 * width, width, k % 2 * width, width) for k in range(4)]
    point_t = [weight(k // 2, 2 * width, width, (2 + k % 2) * width, width) for k in range(4)]
    edge = [weight(part, 3 * width, width, 0, 16) for part in range(2)]
    edge_t = [weight(part, 4 * width, 16, 0, width) for part in range(2)]

    for ref in (
        sig_r, msk_r, live_r, me_r, strips_r, onehot_r, hi_r, hidden_r, actu_e_r, chosen_r,
        decin_r, actu_d_r, actp_e_r, encres_r, actp_d_r, resb_r, gap_r, outs_r, dres_r,
        dinner_d_r, denc_r, dinner_e_r,
    ):

        @pl.loop(0, SLOTS)
        def _(slot, ref=ref):
            ref[:, pl.ds(pl.multiple_of(slot * TILE, TILE), TILE)] = jnp.zeros(
                (ref.shape[0], TILE), ref.dtype
            )

    for ref in (g_conv, g_point, g_edge, g_table, loss_ref):
        ref[...] = jnp.zeros(ref.shape, ref.dtype)

    for k in range(sets):
        for block in range(per_clip):
            rows = slice(8 * k, 8 * k + 8)
            parted = wave_ref[k, block].astype(F32)
            even_scr[block, rows] = parted[:8]
            odd_scr[block, rows] = parted[8:]
            code_scr[block, rows] = ids_ref[k, block]

    def put(index, source, length):
        src_list[index] = source
        len_list[index] = length

    put(0, 0, -frames)

    def add_clip(c, carry):
        filled, count = carry
        length = len_ref[jnp.bitwise_and(c, 8), jnp.bitwise_and(c, 7)]
        blocks = lax.shift_right_logical(
            lax.shift_right_logical(length + 1, 1) + (SPARE + LANES - 1), 7
        )

        def add_block(k, carry):
            put(filled + k, c * 32 + k, length)
            return carry

        lax.fori_loop(0, blocks, add_block, 0)
        return filled + blocks, count + length

    filled, count = lax.fori_loop(0, 8 * sets, add_clip, (jnp.int32(1), jnp.int32(0)))
    tiles = lax.div(filled - 1 + per_tile - 1, jnp.int32(per_tile)) + 4

    def add_empty(k, carry):
        put(filled + k, 0, -frames)
        return carry

    lax.fori_loop(0, 6 * per_tile + 2, add_empty, 0)

    sub = lax.broadcasted_iota(jnp.int32, (8, LANES), 0)
    lane = lax.broadcasted_iota(jnp.int32, (8, LANES), 1)
    sub_ext = lax.broadcasted_iota(jnp.int32, (8, TILE + 2 * LANES), 0)
    sub_tile = lax.broadcasted_iota(jnp.int32, (8, TILE), 0)
    iota16 = lax.broadcasted_iota(jnp.int32, (16, TILE), 0).astype(F32).astype(BF16)

    table = jnp.concatenate([weight_ref[part, :table_rows] for part in range(2)], axis=0)

    def taps(ext):
        later = moved(ext, 1)
        earlier = moved(ext, -1)
        other = jnp.where(sub_tile == 0, later, jnp.where(sub_tile == 1, earlier, 0.0))
        return jnp.concatenate([moved(ext, 0), other], axis=0)

    @pl.loop(0, tiles)
    def _(i):
        def at(lag):
            return pl.multiple_of(lax.rem(i - lag + SLOTS, SLOTS) * TILE, TILE)

        def cur(ref, lag):
            return ref[:, pl.ds(at(lag), TILE)]

        def last_of(ref, lag):
            return ref[:, pl.ds(at(lag) + (TILE - LANES), LANES)]

        def first_of(ref, lag):
            return ref[:, pl.ds(at(lag), LANES)]

        def ext(ref, lag, following):
            return jnp.concatenate([last_of(ref, lag + 1), cur(ref, lag), following], axis=1)

        def keep(ref, lag, value):
            ref[:, pl.ds(at(lag), TILE)] = value

        e2_actu_e = (last_of(actu_e_r, 2), cur(actu_e_r, 1))
        e2_actu_d = (last_of(actu_d_r, 2), cur(actu_d_r, 1))
        e3_outs = (last_of(outs_r, 3), cur(outs_r, 2))
        e4_din = (last_of(dinner_d_r, 4), cur(dinner_d_r, 3))
        e5_din = (last_of(dinner_e_r, 5), cur(dinner_e_r, 4))
        chosen1, chosen3 = cur(chosen_r, 1), cur(chosen_r, 3)
        hidden1, decin1 = cur(hidden_r, 1), cur(decin_r, 1)
        onehot1, hi1, me1 = cur(onehot_r, 1), cur(hi_r, 1), cur(me_r, 1)
        actp_d2, resb2 = cur(actp_d_r, 2), cur(resb_r, 2)
        actu_d3, actp_e3, encres3, gap3, dres3 = (
            cur(actu_d_r, 3), cur(actp_e_r, 3), cur(encres_r, 3), cur(gap_r, 3), cur(dres_r, 3)
        )
        actu_e4, denc4, strips4 = cur(actu_e_r, 4), cur(denc_r, 4), cur(strips_r, 4)
        sig2 = ext(sig_r, 2, first_of(sig_r, 1))
        msk2 = ext(msk_r, 2, first_of(msk_r, 1))
        live2 = cur(live_r, 2)
        live2_ext = ext(live_r, 2, first_of(live_r, 1))

        sigs, msks, lives, mes, los, his = [], [], [], [], [], []
        for j in range(-1, per_tile + 1):
            index = i * per_tile + (j + 1)
            source, length = src_list[index], len_list[index]
            clip = lax.shift_right_logical(source, 5)
            block = jnp.bitwise_and(source, 31)
            here = (jnp.minimum(block, per_clip - 1), pl.ds(clip, 1), slice(None))
            t = block * LANES + lane
            even_ok = 2 * t < length
            odd_ok = 2 * t + 1 < length
            even = jnp.broadcast_to(even_scr[here], (8, LANES))
            odd = jnp.broadcast_to(odd_scr[here], (8, LANES))
            sigs.append(
                jnp.where((sub == 0) & even_ok, even, jnp.where((sub == 1) & odd_ok, odd, 0.0))
            )
            if 0 <= j < per_tile:
                valid = lax.shift_right_arithmetic(length + 1, 1)
                live = t < jnp.minimum(valid + REAL, half)
                code = jnp.broadcast_to(code_scr[here], (8, LANES))
                msks.append(
                    jnp.where(((sub == 0) & even_ok) | ((sub == 1) & odd_ok), 1.0, 0.0)
                )
                lives.append(jnp.where(live, 1.0, 0.0))
                mes.append(jnp.where(even_ok, 1.0, 0.0))
                los.append(jnp.where(live, jnp.bitwise_and(code, LOW - 1), -1).astype(F32))
                his.append(lax.shift_right_logical(code, 8).astype(F32))
        sig_ext = jnp.concatenate(sigs, axis=1)
        live0 = jnp.concatenate(lives, axis=1)
        strips = (taps(sig_ext) * stack(live0, 2)).astype(BF16)
        hidden = nn(edge[0], strips)
        actu_e = relu_bf(hidden)

        low16 = stack(jnp.concatenate(los, axis=1), 2).astype(BF16) - iota16
        onehot = jnp.concatenate(
            [
                jnp.where(low16 == float(16 * r), jnp.ones((), BF16), jnp.zeros((), BF16))
                for r in range(LOW // 16)
            ],
            axis=0,
        )
        picked = nn(table, onehot)
        hi0 = jnp.concatenate(his, axis=1)
        parts = [jnp.zeros((8, TILE), F32) for _ in range(width // 8)]
        for h in range(groups):
            here = hi0 == float(h)
            parts = [
                jnp.where(here, picked[h * width + 8 * r : h * width + 8 * r + 8], parts[r])
                for r in range(width // 8)
            ]
        chosen = jnp.concatenate(parts, axis=0).astype(BF16)
        decin = nn(point[2], chosen)
        actu_d = relu_bf(decin)

        keep(sig_r, 0, moved(sig_ext, 0))
        keep(msk_r, 0, jnp.concatenate(msks, axis=1))
        keep(live_r, 0, live0)
        keep(me_r, 0, jnp.concatenate(mes, axis=1))
        keep(hi_r, 0, stack(hi0, 2).astype(BF16))
        keep(strips_r, 0, strips)
        keep(onehot_r, 0, onehot)
        keep(hidden_r, 0, hidden)
        keep(actu_e_r, 0, actu_e)
        keep(chosen_r, 0, chosen)
        keep(decin_r, 0, decin)
        keep(actu_d_r, 0, actu_d)

        def spread(pair, following):
            whole = jnp.concatenate([*pair, following], axis=1)
            return jnp.concatenate([moved(whole, d) for d in (-REACH, 0, REACH)], axis=0)

        def spread_back(pair, following):
            whole = jnp.concatenate([*pair, following], axis=1)
            return jnp.concatenate([moved(whole, d) for d in (REACH, 0, -REACH)], axis=0)

        actp_e = relu_bf(nn(conv[0], spread(e2_actu_e, actu_e[:, :LANES])))
        encres = (hidden1 + nn(point[0], actp_e)).astype(BF16)
        latent = nn(point[1], encres).astype(BF16)
        gap = (latent.astype(F32) - chosen1.astype(F32)) * stack(me1, width // 8)
        gap_bf = gap.astype(BF16)
        square = gap * gap
        loss_rows = square[:8]
        for r in range(1, width // 8):
            loss_rows = loss_rows + square[8 * r : 8 * r + 8]
        terms = []
        for h in range(groups):
            here = hi1 == float(h)
            terms += [
                jnp.where(here, gap_bf[16 * r : 16 * r + 16], jnp.zeros((), BF16))
                for r in range(width // 16)
            ]
        g_table[...] += nt(jnp.concatenate(terms, axis=0), onehot1)

        actp_d = relu_bf(nn(conv[1], spread(e2_actu_d, actu_d[:, :LANES])))
        resb = (decin1 + nn(point[3], actp_d)).astype(BF16)
        outs = nn(edge_t[1], resb)
        keep(actp_e_r, 1, actp_e)
        keep(encres_r, 1, encres)
        keep(gap_r, 1, gap * (2.0 * COMMIT))
        keep(actp_d_r, 1, actp_d)
        keep(resb_r, 1, resb)
        keep(outs_r, 1, outs)

        outs_ext = jnp.concatenate([*e3_outs, outs[:, :LANES]], axis=1) * stack(live2_ext, 2)
        shifted = outs_ext[8:]
        wide = TILE + 2 * LANES
        crossed = jnp.where(
            sub_ext == 0, pltpu.roll(shifted, 1, 1), pltpu.roll(shifted, wide - 1, 1)
        )
        error = (outs_ext[:8] + crossed - sig2) * msk2
        middle = moved(error, 0)
        loss_rows = COMMIT * loss_rows + middle * middle
        loss_sum = loss_rows[:, :LANES]
        for j in range(1, per_tile):
            loss_sum = loss_sum + loss_rows[:, j * LANES : (j + 1) * LANES]
        loss_ref[...] += loss_sum
        douts = (2.0 * taps(error) * stack(live2, 2)).astype(BF16)
        g_edge[1] += nt(douts, resb2)
        dres = nn(edge[1], douts)
        dbranch = dres.astype(BF16)
        g_point[3] += nt(dbranch, actp_d2)
        dinner_d = jnp.where(actp_d2 > 0, nn(point_t[3], dbranch).astype(BF16), 0)
        keep(dres_r, 2, dres)
        keep(dinner_d_r, 2, dinner_d)

        around = spread_back(e4_din, dinner_d[:, :LANES])
        g_conv[1] += nt(around, actu_d3)
        ddecin = (dres3 + jnp.where(actu_d3 > 0, nn(conv_t[1], around), 0.0)).astype(BF16)
        g_point[2] += nt(ddecin, chosen3)
        dlatent = (nn(point_t[2], ddecin) + gap3).astype(BF16)
        g_point[1] += nt(dlatent, encres3)
        denc = nn(point_t[1], dlatent)
        dbranch_e = denc.astype(BF16)
        g_point[0] += nt(dbranch_e, actp_e3)
        dinner_e = jnp.where(actp_e3 > 0, nn(point_t[0], dbranch_e).astype(BF16), 0)
        keep(denc_r, 3, denc)
        keep(dinner_e_r, 3, dinner_e)

        around_e = spread_back(e5_din, dinner_e[:, :LANES])
        g_conv[0] += nt(around_e, actu_e4)
        dhidden = (denc4 + jnp.where(actu_e4 > 0, nn(conv_t[0], around_e), 0.0)).astype(BF16)
        g_edge[0] += nt(strips4, dhidden)

    first = jnp.where((sub == 0) & (lane == 0), count, 0).astype(F32)
    stats_ref[...] = jnp.concatenate([loss_ref[...], first], axis=0)
    rows = groups // 2 * width
    for part in range(2):
        payload_ref[part, :rows] = g_table[part * rows : (part + 1) * rows, :LANES]
        payload_ref[part, rows : 2 * rows] = g_table[part * rows : (part + 1) * rows, LANES:]
        conv_rows = [g_conv[part, k * width : (k + 1) * width] for k in range(3)]
        edge_rows = jnp.concatenate(
            [g_edge[part], jnp.zeros((width - 16, width), F32)], axis=0
        )
        after = 2 * rows
        for pair in (
            conv_rows[:2],
            (conv_rows[2], edge_rows),
            (g_point[2 * part], g_point[2 * part + 1]),
        ):
            payload_ref[part, after : after + width] = jnp.concatenate(pair, axis=1)
            after += width
        rest = payload_ref.shape[1] - after
        if rest:
            payload_ref[part, after:] = jnp.zeros((rest, LANES), F32)


def net(rows, lengths, wave, codes, weights):
    sets, per_clip = wave.shape[:2]
    clips = 8 * sets
    width = 64
    table_rows = 2 * (weights.shape[1] - 4 * width - 16)
    columns = SLOTS * TILE
    listed = clips * (per_clip + 1) + 8 * (TILE // LANES) + 8
    smem = pl.BlockSpec(memory_space=pltpu.SMEM)
    vmem = pl.BlockSpec(memory_space=pltpu.VMEM)

    def ring(rows, dtype):
        return pltpu.VMEM((rows, columns), dtype)

    return pl.pallas_call(
        net_kernel,
        out_shape=(
            jax.ShapeDtypeStruct((2, rows, LANES), F32),
            jax.ShapeDtypeStruct((16, LANES), F32),
        ),
        in_specs=[smem] + [vmem] * 3,
        out_specs=(vmem,) * 2,
        scratch_shapes=[
            pltpu.VMEM((2, 3 * width, width), F32),
            pltpu.VMEM((4, width, width), F32),
            pltpu.VMEM((2, 16, width), F32),
            pltpu.VMEM((table_rows, LOW), F32),
            pltpu.VMEM((8, LANES), F32),
            pltpu.SMEM((listed,), jnp.int32),
            pltpu.SMEM((listed,), jnp.int32),
            pltpu.VMEM((per_clip, clips, LANES), F32),
            pltpu.VMEM((per_clip, clips, LANES), F32),
            pltpu.VMEM((per_clip, clips, LANES), jnp.int32),
            ring(8, F32),
            ring(8, F32),
            ring(8, F32),
            ring(8, F32),
            ring(16, BF16),
            ring(LOW, BF16),
            ring(16, BF16),
            ring(width, F32),
            ring(width, BF16),
            ring(width, BF16),
            ring(width, F32),
            ring(width, BF16),
            ring(width, BF16),
            ring(width, BF16),
            ring(width, BF16),
            ring(width, BF16),
            ring(width, F32),
            ring(16, F32),
            ring(width, F32),
            ring(width, BF16),
            ring(width, F32),
            ring(width, BF16),
        ],
        compiler_params=pltpu.CompilerParams(vmem_limit_bytes=48 * 2**20),
    )(lengths, wave, codes, weights)


def remote(src, dst, send, recv, to):
    return pltpu.make_async_remote_copy(
        src_ref=src, dst_ref=dst, send_sem=send, recv_sem=recv, device_id=to, device_id_type=MESH
    )


def share_kernel(
    items,
    len_ref,
    wave_ref,
    ids_ref,
    conv_ref,
    point_ref,
    edge_ref,
    table_ref,
    len_out,
    wave_out,
    ids_out,
    weight_out,
    len_scr,
    wave_scr,
    ids_scr,
    weight_scr,
    sems,
):
    item = lax.axis_index("item")
    pipe = lax.axis_index("pipe")
    partner = (item, 1 - pipe)
    mirror = (items - 1 - item, pipe)
    per_clip = wave_out.shape[1]
    width = conv_ref.shape[1]
    table_rows = weight_scr.shape[1] - 4 * width - 16

    barrier = pltpu.get_barrier_semaphore()
    for other in (partner, mirror):
        pl.semaphore_signal(barrier, inc=1, device_id=other, device_id_type=MESH)

    row_at = lax.broadcasted_iota(jnp.int32, (2 * LANES, 2 * LANES), 0)
    col_at = lax.broadcasted_iota(jnp.int32, (2 * LANES, 2 * LANES), 1)
    wanted = jnp.where(col_at < LANES, 2 * col_at, 2 * (col_at - LANES) + 1)
    split = jnp.where(row_at == wanted, 1.0, 0.0).astype(BF16)
    on_first = pipe == 0
    lane = lax.broadcasted_iota(jnp.int32, (8, LANES), 1)
    kept = jnp.zeros((8, LANES), jnp.int32)
    given = kept
    for k in range(8):
        kept = jnp.where(lane == k, jnp.where(on_first, len_ref[k], len_ref[8 + k]), kept)
        given = jnp.where(lane == k, jnp.where(on_first, len_ref[24 + k], len_ref[16 + k]), given)
    len_out[:8] = kept
    len_scr[0] = given
    for block in range(per_clip):
        parted = nn(wave_ref[:, block * 2 * LANES : (block + 1) * 2 * LANES], split)
        codes = ids_ref[:, block * LANES : (block + 1) * LANES]
        even, odd = parted[:, :LANES], parted[:, LANES:]

        def chosen(values, first, second):
            return jnp.where(on_first, values[8 * first :][:8], values[8 * second :][:8])

        def both(first, second):
            return jnp.concatenate(
                [chosen(even, first, second), chosen(odd, first, second)], axis=0
            ).astype(BF16)

        wave_out[0, block] = both(0, 1)
        wave_scr[0, block] = both(3, 2)
        ids_out[0, block] = chosen(codes, 0, 1)
        ids_scr[0, block] = chosen(codes, 3, 2)

    pl.semaphore_wait(barrier, 2)
    copies = [
        remote(ref.at[0], ref.at[1], sems.at[2 * k], sems.at[2 * k + 1], mirror)
        for k, ref in enumerate((len_scr, wave_scr, ids_scr))
    ]
    for copy in copies:
        copy.start()

    groups = table_rows // width
    for h in range(groups):
        weight_scr[0, h * width : (h + 1) * width] = table_ref[:, h * LOW : (h + 1) * LOW].astype(
            BF16
        )
    blank = jnp.zeros((width, LOW - 3 * width), F32)
    conv = conv_ref[0]
    conv_t = [conv[:, k * width : (k + 1) * width].T for k in range(3)]
    points = [point_ref[0, 0], point_ref[0, 1]]
    edge = edge_ref[0]
    empty = jnp.zeros((6, width), F32)
    edge_t = jnp.concatenate([edge[1:3], empty, edge[3:], edge[:1], empty], axis=0)
    edge_square = jnp.concatenate([edge_t, jnp.zeros((width - 16, width), F32)], axis=0).T
    after = table_rows
    for pieces in (
        [conv, blank],
        conv_t + [blank],
        points + [value.T for value in points],
        [edge_square, jnp.zeros((width, LOW - width), F32)],
        [edge_t, jnp.zeros((16, LOW - width), F32)],
    ):
        value = jnp.concatenate(pieces, axis=1).astype(BF16)
        weight_scr[0, after : after + value.shape[0]] = value
        after += value.shape[0]
    over = remote(weight_scr.at[0], weight_scr.at[1], sems.at[6], sems.at[7], partner)
    over.start()
    weight_out[pipe] = weight_scr[0]
    over.wait()
    weight_out[1 - pipe] = weight_scr[1]
    for copy in copies:
        copy.wait()
    len_out[8:] = len_scr[1]
    wave_out[1] = wave_scr[1]
    ids_out[1] = ids_scr[1]


def shared(items, lengths, waveform, code_ids, conv, point, edge, table):
    per_clip = code_ids.shape[1] // LANES
    width = conv.shape[1]
    weight_rows = table.shape[1] // LOW * width + 4 * width + 16
    smem = pl.BlockSpec(memory_space=pltpu.SMEM)
    vmem = pl.BlockSpec(memory_space=pltpu.VMEM)
    wave_shape = (2, per_clip, 16, LANES)
    ids_shape = (2, per_clip, 8, LANES)
    weight_shape = (2, weight_rows, LOW)
    return pl.pallas_call(
        functools.partial(share_kernel, items),
        out_shape=(
            jax.ShapeDtypeStruct((16, LANES), jnp.int32),
            jax.ShapeDtypeStruct(wave_shape, BF16),
            jax.ShapeDtypeStruct(ids_shape, jnp.int32),
            jax.ShapeDtypeStruct(weight_shape, BF16),
        ),
        in_specs=[smem] + [vmem] * 6,
        out_specs=(vmem,) * 4,
        scratch_shapes=[
            pltpu.VMEM((2, 8, LANES), jnp.int32),
            pltpu.VMEM(wave_shape, BF16),
            pltpu.VMEM(ids_shape, jnp.int32),
            pltpu.VMEM(weight_shape, BF16),
            pltpu.SemaphoreType.DMA((8,)),
        ],
        compiler_params=pltpu.CompilerParams(
            collective_id=0, has_side_effects=True, vmem_limit_bytes=16 * 2**20
        ),
    )(lengths, waveform, code_ids, conv, point, edge, table)


def sum_kernel(
    items,
    payload_ref,
    stats_ref,
    sum_ref,
    stats_out,
    crossed,
    crossed_stats,
    part,
    part_stats,
    landed,
    landed_stats,
    whole,
    cross_sem,
    out_send,
    out_recv,
    stats_send,
    stats_recv,
    back_send,
    back_recv,
):
    item = lax.axis_index("item")
    pipe = lax.axis_index("pipe")
    partner = (item, 1 - pipe)
    piece = part.shape[1]

    def peer(d):
        return lax.rem(item + d, items)

    barrier = pltpu.get_barrier_semaphore()
    pl.semaphore_signal(barrier, inc=1, device_id=partner, device_id_type=MESH)

    @pl.loop(1, items)
    def _(d):
        pl.semaphore_signal(barrier, inc=1, device_id=(peer(d), pipe), device_id_type=MESH)

    pl.semaphore_wait(barrier, items)

    over = remote(payload_ref.at[1 - pipe], crossed, cross_sem.at[0], cross_sem.at[1], partner)
    over_stats = remote(stats_ref, crossed_stats, cross_sem.at[2], cross_sem.at[3], partner)
    over.start()
    over_stats.start()
    over_stats.wait()
    part_stats[...] = stats_ref[...] + crossed_stats[...]
    over.wait()

    def out_copy(to):
        return remote(
            part.at[to], landed.at[item], out_send.at[to], out_recv.at[item], (to, pipe)
        )

    def out_copy_stats(to):
        return remote(
            part_stats, landed_stats.at[item], stats_send.at[to], stats_recv.at[item], (to, pipe)
        )

    def add_up(k):
        rows = pl.ds(pl.multiple_of(k * piece, piece), piece)
        return payload_ref[pipe, rows] + crossed[rows]

    @pl.loop(1, items)
    def _(d):
        to = peer(d)
        part[to] = add_up(to).astype(BF16)
        out_copy(to).start()
        out_copy_stats(to).start()

    total = add_up(item)

    def take(d, carry):
        total, stats = carry
        source = peer(items - d)
        remote(
            part.at[source], landed.at[source], out_send.at[source], out_recv.at[source],
            (source, pipe),
        ).wait_recv()
        remote(
            part_stats, landed_stats.at[source], stats_send.at[source], stats_recv.at[source],
            (source, pipe),
        ).wait_recv()
        return total + landed[source].astype(F32), stats + landed_stats[source]

    total, stats = lax.fori_loop(1, items, take, (total, part_stats[...]))
    whole[item] = total.astype(BF16)
    stats_out[...] = stats

    def back_copy(place, slot, to):
        return remote(
            whole.at[place], whole.at[place], back_send.at[slot], back_recv.at[place], (to, pipe)
        )

    @pl.loop(1, items)
    def _(d):
        to = peer(d)
        back_copy(item, to, to).start()

    own = pl.ds(pl.multiple_of(item * piece, piece), piece)
    sum_ref[own] = total.astype(BF16).astype(F32)

    @pl.loop(1, items)
    def _(d):
        source = peer(items - d)
        back_copy(source, source, source).wait_recv()
        rows = pl.ds(pl.multiple_of(source * piece, piece), piece)
        sum_ref[rows] = whole[source].astype(F32)

    @pl.loop(1, items)
    def _(d):
        to = peer(d)
        out_copy(to).wait_send()
        out_copy_stats(to).wait_send()
        back_copy(item, to, to).wait_send()


def summed(items, payload, stats):
    rows = payload.shape[1]
    piece = rows // items
    vmem = pl.BlockSpec(memory_space=pltpu.VMEM)
    sems = pltpu.SemaphoreType.DMA((items,))
    return pl.pallas_call(
        functools.partial(sum_kernel, items),
        out_shape=(
            jax.ShapeDtypeStruct((rows, LANES), F32),
            jax.ShapeDtypeStruct(stats.shape, F32),
        ),
        in_specs=[vmem] * 2,
        out_specs=(vmem,) * 2,
        scratch_shapes=[
            pltpu.VMEM((rows, LANES), F32),
            pltpu.VMEM(stats.shape, F32),
            pltpu.VMEM((items, piece, LANES), BF16),
            pltpu.VMEM(stats.shape, F32),
            pltpu.VMEM((items, piece, LANES), BF16),
            pltpu.VMEM((items,) + stats.shape, F32),
            pltpu.VMEM((items, piece, LANES), BF16),
            pltpu.SemaphoreType.DMA((4,)),
        ]
        + [sems] * 6,
        compiler_params=pltpu.CompilerParams(
            collective_id=1, has_side_effects=True, vmem_limit_bytes=16 * 2**20
        ),
    )(payload, stats)


def update_kernel(*refs):
    rate_net, rate_code, sum_ref, stats_ref = refs[:4]
    states = refs[4:16]
    loss_ref = refs[16]
    results = refs[17:]
    width = states[0].shape[1]
    count = jnp.sum(stats_ref[8:], keepdims=True)
    loss_ref[0] = jnp.sum(stats_ref[:8]) / jnp.sum(stats_ref[8:])
    scale = 1.0 / count

    def step(kind, place, grad, rate):
        weight_ref, moment_ref, average_ref = (states[4 * j + kind] for j in range(3))
        new_ref, moment_new_ref, average_new_ref, copy_ref = results[4 * kind : 4 * kind + 4]
        grad = grad * scale
        moment = MOMENTUM * moment_ref[place] + grad
        weight = weight_ref[place] - rate * (grad + MOMENTUM * moment)
        new_ref[place] = weight
        moment_new_ref[place] = moment
        average_new_ref[place] = AVERAGE * average_ref[place] + (1.0 - AVERAGE) * weight
        copy_ref[place] = weight.astype(BF16)

    groups = states[3].shape[1] // LOW
    rows = groups * width
    for h in range(groups):
        for side in range(LOW // LANES):
            start = h * LOW + side * LANES
            grad = sum_ref[side * rows + h * width : side * rows + (h + 1) * width]
            place = (slice(None), slice(start, start + LANES))
            step(3, place, grad * (-2.0 * COMMIT), rate_code[0])
    first, second, third = (
        sum_ref[2 * rows + k * width : 2 * rows + (k + 1) * width] for k in range(3)
    )
    rate = rate_net[0]
    step(0, 0, jnp.concatenate([first, second[:, :width]], axis=1), rate)
    step(1, (0, 0), third[:, :width], rate)
    step(1, (0, 1), third[:, width:], rate)
    edge = [second[k : k + 1, width:] for k in (9, 0, 1, 8)]
    step(2, 0, jnp.concatenate(edge, axis=0), rate)


def updated(rates, sums, stats, states):
    smem = pl.BlockSpec(memory_space=pltpu.SMEM)
    shapes = [jax.ShapeDtypeStruct((1,), F32)]
    for weight in states[:4]:
        shapes += [jax.ShapeDtypeStruct(weight.shape, F32)] * 3
        shapes += [jax.ShapeDtypeStruct(weight.shape, BF16)]
    def block(value):
        return pl.BlockSpec(value.shape, lambda i: (0,) * len(value.shape))

    return pl.pallas_call(
        update_kernel,
        grid=(1,),
        out_shape=tuple(shapes),
        in_specs=[smem] * 2 + [block(value) for value in (sums, stats, *states)],
        out_specs=(smem,) + tuple(block(value) for value in shapes[1:]),
        compiler_params=pltpu.CompilerParams(vmem_limit_bytes=24 * 2**20),
    )(*rates, sums, stats, *states)


def per_device(
    waveform,
    lengths,
    code_ids,
    conv_w,
    point_w,
    edge_w,
    codebook,
    conv_mom,
    point_mom,
    edge_mom,
    code_mom,
    conv_avg,
    point_avg,
    edge_avg,
    code_avg,
    rate_net,
    rate_code,
):
    width = conv_w.shape[1]
    items = lax.axis_size("item")
    edge_w, edge_mom, edge_avg = (jnp.swapaxes(v, 1, 2) for v in (edge_w, edge_mom, edge_avg))
    codebook, code_mom, code_avg = (v.T for v in (codebook, code_mom, code_avg))
    rows = 2 * (codebook.shape[1] // LOW) * width + 3 * width
    piece = -(-rows // (16 * items)) * 16
    own_inputs = shared(items, lengths, waveform, code_ids, conv_w, point_w, edge_w, codebook)
    payload, stats = net(piece * items, *own_inputs)
    sums, stats = summed(items, payload, stats)
    states = (
        conv_w, point_w, edge_w, codebook,
        conv_mom, point_mom, edge_mom, code_mom,
        conv_avg, point_avg, edge_avg, code_avg,
    )
    loss, *rest = updated((rate_net, rate_code), sums, stats, states)
    edges = (jnp.swapaxes(v, 1, 2) for v in rest[8:12])
    return (loss.reshape(()), *rest[:8], *edges, *(v.T for v in rest[12:]))


def solution(mesh):
    weights = (
        P("pipe", None, None),
        P("pipe", None, None, None),
        P("pipe", None, None),
        P("pipe", None),
    )
    return jax.shard_map(
        per_device,
        mesh=mesh,
        in_specs=(P("item", None), P("item"), P("item", None), *weights, *weights, *weights, P(), P()),
        out_specs=(P(),) + tuple(spec for spec in weights for _ in range(4)),
        check_vma=False,
    )
```

```python
import functools

import jax
import jax.numpy as jnp
from jax import lax
from jax.experimental import pallas as pl
from jax.experimental.pallas import tpu as pltpu
from jax.sharding import PartitionSpec as P

REACH = 3
COMMIT = 0.02
MOMENTUM = 0.9
AVERAGE = 0.99

LANES = 128
TILE = 512
SLOTS = 8
LAG = TILE // LANES + 1
DEPTH = -(-4 * LAG * LANES // TILE)
LOW = 256
SPARE = 16
REAL = 8

MESH = pl.DeviceIdType.MESH
F32 = jnp.float32
BF16 = jnp.bfloat16


def nn(a, b):
    return lax.dot_general(a, b, (((1,), (0,)), ((), ())), preferred_element_type=F32)


def nt(a, b):
    return lax.dot_general(a, b, (((1,), (1,)), ((), ())), preferred_element_type=F32)


def moved(ext, distance):
    width = ext.shape[1]
    turned = ext if distance == 0 else pltpu.roll(ext, (-distance) % width, 1)
    return turned[:, LANES : width - LANES]


def relu_bf(values):
    return jnp.maximum(values, 0.0).astype(BF16)


def stack(rows, times):
    return jnp.concatenate([rows] * times, axis=0)


def net_kernel(
    len_ref,
    wave_ref,
    ids_ref,
    weight_ref,
    payload_ref,
    stats_ref,
    g_conv,
    g_point,
    g_edge,
    g_table,
    loss_ref,
    even_scr,
    odd_scr,
    code_scr,
    sig_r,
    msk_r,
    live_r,
    me_r,
    low_r,
    high_r,
    hi_r,
    strips_r,
    onehot_r,
    hidden_r,
    actu_e_r,
    chosen_r,
    decin_r,
    actu_d_r,
    actp_e_r,
    encres_r,
    actp_d_r,
    resb_r,
    gap_r,
    gapb_r,
    outs_r,
    dres_r,
    dinner_d_r,
    denc_r,
    dinner_e_r,
):
    sets, per_clip = wave_ref.shape[:2]
    half = per_clip * LANES
    frames = 2 * half
    width = 64
    groups = 2 * (weight_ref.shape[1] - 4 * width - 16) // width
    table_rows = groups // 2 * width
    per_tile = TILE // LANES

    def weight(part, start, rows, first, columns):
        start += table_rows
        return weight_ref[part, start : start + rows, first : first + columns]

    conv = [weight(part, 0, width, 0, 3 * width) for part in range(2)]
    conv_t = [weight(part, width, width, 0, 3 * width) for part in range(2)]
    point = [weight(k // 2, 2 * width, width, k % 2 * width, width) for k in range(4)]
    point_t = [weight(k // 2, 2 * width, width, (2 + k % 2) * width, width) for k in range(4)]
    edge = [weight(part, 3 * width, width, 0, 16) for part in range(2)]
    edge_t = [weight(part, 4 * width, 16, 0, width) for part in range(2)]

    rings = (
        sig_r, msk_r, live_r, me_r, low_r, high_r, hi_r, strips_r, onehot_r, hidden_r, actu_e_r,
        chosen_r, decin_r, actu_d_r, actp_e_r, encres_r, actp_d_r, resb_r, gap_r, gapb_r, outs_r,
        dres_r, dinner_d_r, denc_r, dinner_e_r,
    )
    slots = SLOTS * per_tile

    @pl.loop(slots - 4 * LAG - 2, slots)
    def _(slot):
        for ref in rings:
            ref[slot] = jnp.zeros(ref.shape[1:], ref.dtype)

    for ref in (g_conv, g_point, g_edge, g_table, loss_ref):
        ref[...] = jnp.zeros(ref.shape, ref.dtype)

    for k in range(sets):
        for block in range(per_clip):
            rows = slice(8 * k, 8 * k + 8)
            parted = wave_ref[k, block].astype(F32)
            even_scr[block, rows] = parted[:8]
            odd_scr[block, rows] = parted[8:]
            code_scr[block, rows] = ids_ref[k, block]

    clips = 8 * sets

    def blocks_of(length):
        valid = lax.shift_right_arithmetic(length + 1, 1)
        return lax.shift_right_arithmetic(valid + (SPARE + LANES - 1), 7)

    def length_of(clip):
        return len_ref[jnp.bitwise_and(clip, 8), jnp.bitwise_and(clip, 7)]

    def add_clip(c, carry):
        length = length_of(c)
        return carry[0] + blocks_of(length), carry[1] + length

    blocks, count = lax.fori_loop(0, clips, add_clip, (jnp.int32(0), jnp.int32(0)))
    tiles = lax.div(blocks + per_tile - 1, jnp.int32(per_tile)) + DEPTH

    sub = lax.broadcasted_iota(jnp.int32, (8, LANES), 0)
    lane = lax.broadcasted_iota(jnp.int32, (8, LANES), 1)
    sub_ext = lax.broadcasted_iota(jnp.int32, (8, TILE + 2 * LANES), 0)
    sub_tile = lax.broadcasted_iota(jnp.int32, (8, TILE), 0)
    iota16 = lax.broadcasted_iota(jnp.int32, (16, TILE), 0).astype(F32).astype(BF16)

    table = jnp.concatenate([weight_ref[part, :table_rows] for part in range(2)], axis=0)

    def taps(ext):
        later = moved(ext, 1)
        earlier = moved(ext, -1)
        other = jnp.where(sub_tile == 0, later, jnp.where(sub_tile == 1, earlier, 0.0))
        return jnp.concatenate([moved(ext, 0), other], axis=0)

    def fetch(state, slot):
        clip, place = state
        real = clip < clips
        length = jnp.where(real, length_of(clip), -frames)
        row = pl.ds(jnp.minimum(clip, clips - 1), 1)
        here = (jnp.minimum(place, per_clip - 1), row, slice(None))
        t = place * LANES + lane
        even_ok = 2 * t < length
        odd_ok = 2 * t + 1 < length
        even = jnp.broadcast_to(even_scr[here], (8, LANES))
        odd = jnp.broadcast_to(odd_scr[here], (8, LANES))
        code = jnp.broadcast_to(code_scr[here], (8, LANES))
        live = t < jnp.minimum(lax.shift_right_arithmetic(length + 1, 1) + REAL, half)
        low = jnp.where(live, jnp.bitwise_and(code, LOW - 1), -1).astype(F32)
        high = lax.shift_right_logical(code, 8).astype(F32)
        sig_r[slot] = jnp.where(
            (sub == 0) & even_ok, even, jnp.where((sub == 1) & odd_ok, odd, 0.0)
        )
        msk_r[slot] = jnp.where(((sub == 0) & even_ok) | ((sub == 1) & odd_ok), 1.0, 0.0)
        live_r[slot] = jnp.where(live, 1.0, 0.0)
        me_r[slot] = jnp.where(even_ok, 1.0, 0.0)
        low_r[slot] = stack(low, 2).astype(BF16)
        high_r[slot] = high
        hi_r[slot] = stack(high, 2).astype(BF16)
        done = place + 1 >= blocks_of(length)
        clip = jnp.where(done, jnp.minimum(clip + 1, clips), clip)
        return clip, jnp.where(done, 0, place + 1)

    state = (jnp.int32(0), jnp.int32(0))
    for b in range(per_tile + 1):
        state = fetch(state, b)

    def tile_step(i, state):
        def block(lag, b):
            return jnp.bitwise_and(i * per_tile - lag + b, slots - 1)

        def load(ref, lag, first=0, last=per_tile):
            return jnp.concatenate([ref[block(lag, b)] for b in range(first, last)], axis=1)

        def load_ext(ref, lag):
            return load(ref, lag, -1, per_tile + 1)

        stores = []

        def keep(ref, lag, value):
            stores.append((ref, lag, value))

        def spread(ext, way):
            return jnp.concatenate([moved(ext, d * way) for d in (-REACH, 0, REACH)], axis=0)

        def first_step():
            lag = 0
            sig_ext, live0 = load_ext(sig_r, lag), load(live_r, lag)
            hi0 = load(high_r, lag)
            low16 = load(low_r, lag) - iota16
            strips = (taps(sig_ext) * stack(live0, 2)).astype(BF16)
            onehot = jnp.concatenate(
                [
                    jnp.where(low16 == float(16 * r), jnp.ones((), BF16), jnp.zeros((), BF16))
                    for r in range(LOW // 16)
                ],
                axis=0,
            )
            keep(strips_r, lag, strips)
            keep(onehot_r, lag, onehot)
            yield
            picked = nn(table, onehot)
            hidden = nn(edge[0], strips)
            yield
            parts = [jnp.zeros((8, TILE), F32) for _ in range(width // 8)]
            for h in range(groups):
                here = hi0 == float(h)
                parts = [
                    jnp.where(here, picked[h * width + 8 * r : h * width + 8 * r + 8], parts[r])
                    for r in range(width // 8)
                ]
            chosen = jnp.concatenate(parts, axis=0).astype(BF16)
            keep(chosen_r, lag, chosen)
            keep(hidden_r, lag, hidden)
            keep(actu_e_r, lag, relu_bf(hidden))
            yield
            decin = nn(point[2], chosen)
            yield
            keep(decin_r, lag, decin)
            keep(actu_d_r, lag, relu_bf(decin))

        def second_step():
            lag = LAG
            actu_e, actu_d = load_ext(actu_e_r, lag), load_ext(actu_d_r, lag)
            hidden, decin = load(hidden_r, lag), load(decin_r, lag)
            chosen, me = load(chosen_r, lag), load(me_r, lag)
            yield
            inner_e = nn(conv[0], spread(actu_e, 1))
            inner_d = nn(conv[1], spread(actu_d, 1))
            yield
            actp_e = relu_bf(inner_e)
            actp_d = relu_bf(inner_d)
            keep(actp_e_r, lag, actp_e)
            keep(actp_d_r, lag, actp_d)
            yield
            branch_e = nn(point[0], actp_e)
            branch_d = nn(point[3], actp_d)
            yield
            encres = (hidden + branch_e).astype(BF16)
            resb = (decin + branch_d).astype(BF16)
            keep(encres_r, lag, encres)
            keep(resb_r, lag, resb)
            yield
            latent = nn(point[1], encres)
            outs = nn(edge_t[1], resb)
            yield
            keep(outs_r, lag, outs)
            gap = (latent.astype(BF16).astype(F32) - chosen.astype(F32)) * stack(me, width // 8)
            keep(gap_r, lag, gap * (2.0 * COMMIT))
            keep(gapb_r, lag, gap.astype(BF16))
            square = gap * gap
            rows = square[:8]
            for r in range(1, width // 8):
                rows = rows + square[8 * r : 8 * r + 8]
            add_loss(COMMIT * rows)

        def scatter_step():
            lag = LAG + per_tile
            onehot, hi, gap = load(onehot_r, lag), load(hi_r, lag), load(gapb_r, lag)
            yield
            terms = []
            for h in range(groups):
                here = hi == float(h)
                terms += [
                    jnp.where(here, gap[16 * r : 16 * r + 16], jnp.zeros((), BF16))
                    for r in range(width // 16)
                ]
            found = nt(jnp.concatenate(terms, axis=0), onehot)
            yield
            g_table[...] += found

        def add_loss(rows):
            total = rows[:, :LANES]
            for j in range(1, per_tile):
                total = total + rows[:, j * LANES : (j + 1) * LANES]
            loss_ref[...] += total

        def third_step():
            lag = 2 * LAG
            outs_ext, live_ext = load_ext(outs_r, lag), load_ext(live_r, lag)
            sig_ext, msk_ext = load_ext(sig_r, lag), load_ext(msk_r, lag)
            actp, resb = load(actp_d_r, lag), load(resb_r, lag)
            outs_ext = outs_ext * stack(live_ext, 2)
            shifted = outs_ext[8:]
            wide = TILE + 2 * LANES
            crossed = jnp.where(
                sub_ext == 0, pltpu.roll(shifted, 1, 1), pltpu.roll(shifted, wide - 1, 1)
            )
            error = (outs_ext[:8] + crossed - sig_ext) * msk_ext
            middle = moved(error, 0)
            douts = (2.0 * taps(error) * stack(moved(live_ext, 0), 2)).astype(BF16)
            yield
            dres = nn(edge[1], douts)
            yield
            dbranch = dres.astype(BF16)
            keep(dres_r, lag, dres)
            add_loss(middle * middle)
            yield
            dinner = nn(point_t[3], dbranch)
            yield
            keep(dinner_d_r, lag, jnp.where(actp > 0, dinner.astype(BF16), 0))
            yield
            g_point[3] += nt(dbranch, actp)
            g_edge[1] += nt(douts, resb)

        def fourth_step():
            lag = 3 * LAG
            around = spread(load_ext(dinner_d_r, lag), -1)
            actu, decin, chosen = load(actu_d_r, lag), load(decin_r, lag), load(chosen_r, lag)
            actp, encres = load(actp_e_r, lag), load(encres_r, lag)
            gap, dres = load(gap_r, lag), load(dres_r, lag)
            yield
            du = nn(conv_t[1], around)
            yield
            ddecin = (dres + jnp.where(decin > 0, du, 0.0)).astype(BF16)
            yield
            back = nn(point_t[2], ddecin)
            yield
            dlatent = (back + gap).astype(BF16)
            yield
            denc = nn(point_t[1], dlatent)
            yield
            dbranch = denc.astype(BF16)
            keep(denc_r, lag, denc)
            yield
            dinner = nn(point_t[0], dbranch)
            g_conv[1] += nt(around, actu)
            yield
            keep(dinner_e_r, lag, jnp.where(actp > 0, dinner.astype(BF16), 0))
            yield
            g_point[2] += nt(ddecin, chosen)
            g_point[1] += nt(dlatent, encres)
            g_point[0] += nt(dbranch, actp)

        def fifth_step():
            lag = 4 * LAG
            around = spread(load_ext(dinner_e_r, lag), -1)
            actu, hidden = load(actu_e_r, lag), load(hidden_r, lag)
            denc, strips = load(denc_r, lag), load(strips_r, lag)
            yield
            du = nn(conv_t[0], around)
            yield
            dhidden = (denc + jnp.where(hidden > 0, du, 0.0)).astype(BF16)
            yield
            g_conv[0] += nt(around, actu)
            yield
            g_edge[0] += nt(strips, dhidden)

        steps = [
            f()
            for f in (
                first_step, fourth_step, second_step, scatter_step, third_step, fifth_step
            )
        ]
        while steps:
            left = []
            for step in steps:
                try:
                    next(step)
                    left.append(step)
                except StopIteration:
                    pass
            steps = left
        for ref, lag, value in stores:
            for b in range(per_tile):
                ref[block(lag, b)] = value[:, b * LANES : (b + 1) * LANES]
        for b in range(per_tile):
            state = fetch(state, block(-LAG, b))
        return state

    lax.fori_loop(0, tiles, tile_step, state)

    first = jnp.where((sub == 0) & (lane == 0), count, 0).astype(F32)
    stats_ref[...] = jnp.concatenate([loss_ref[...], first], axis=0)
    rows = groups // 2 * width
    for part in range(2):
        payload_ref[part, :rows] = g_table[part * rows : (part + 1) * rows, :LANES]
        payload_ref[part, rows : 2 * rows] = g_table[part * rows : (part + 1) * rows, LANES:]
        conv_rows = [g_conv[part, k * width : (k + 1) * width] for k in range(3)]
        edge_rows = jnp.concatenate(
            [g_edge[part], jnp.zeros((width - 16, width), F32)], axis=0
        )
        after = 2 * rows
        for pair in (
            conv_rows[:2],
            (conv_rows[2], edge_rows),
            (g_point[2 * part], g_point[2 * part + 1]),
        ):
            payload_ref[part, after : after + width] = jnp.concatenate(pair, axis=1)
            after += width
        rest = payload_ref.shape[1] - after
        if rest:
            payload_ref[part, after:] = jnp.zeros((rest, LANES), F32)


def net(rows, lengths, wave, codes, weights):
    sets, per_clip = wave.shape[:2]
    clips = 8 * sets
    width = 64
    table_rows = 2 * (weights.shape[1] - 4 * width - 16)
    slots = SLOTS * TILE // LANES
    smem = pl.BlockSpec(memory_space=pltpu.SMEM)
    vmem = pl.BlockSpec(memory_space=pltpu.VMEM)

    def ring(rows, dtype):
        return pltpu.VMEM((slots, rows, LANES), dtype)

    return pl.pallas_call(
        net_kernel,
        out_shape=(
            jax.ShapeDtypeStruct((2, rows, LANES), F32),
            jax.ShapeDtypeStruct((16, LANES), F32),
        ),
        in_specs=[smem] + [vmem] * 3,
        out_specs=(vmem,) * 2,
        scratch_shapes=[
            pltpu.VMEM((2, 3 * width, width), F32),
            pltpu.VMEM((4, width, width), F32),
            pltpu.VMEM((2, 16, width), F32),
            pltpu.VMEM((table_rows, LOW), F32),
            pltpu.VMEM((8, LANES), F32),
            pltpu.VMEM((per_clip, clips, LANES), F32),
            pltpu.VMEM((per_clip, clips, LANES), F32),
            pltpu.VMEM((per_clip, clips, LANES), jnp.int32),
            ring(8, F32),
            ring(8, F32),
            ring(8, F32),
            ring(8, F32),
            ring(16, BF16),
            ring(8, F32),
            ring(16, BF16),
            ring(16, BF16),
            ring(LOW, BF16),
            ring(width, F32),
            ring(width, BF16),
            ring(width, BF16),
            ring(width, F32),
            ring(width, BF16),
            ring(width, BF16),
            ring(width, BF16),
            ring(width, BF16),
            ring(width, BF16),
            ring(width, F32),
            ring(width, BF16),
            ring(16, F32),
            ring(width, F32),
            ring(width, BF16),
            ring(width, F32),
            ring(width, BF16),
        ],
        compiler_params=pltpu.CompilerParams(vmem_limit_bytes=48 * 2**20),
    )(lengths, wave, codes, weights)


def remote(src, dst, send, recv, to):
    return pltpu.make_async_remote_copy(
        src_ref=src, dst_ref=dst, send_sem=send, recv_sem=recv, device_id=to, device_id_type=MESH
    )


def share_kernel(
    items,
    len_ref,
    wave_ref,
    ids_ref,
    conv_ref,
    point_ref,
    edge_ref,
    table_ref,
    len_out,
    wave_out,
    ids_out,
    weight_out,
    len_scr,
    wave_scr,
    ids_scr,
    weight_scr,
    sems,
):
    item = lax.axis_index("item")
    pipe = lax.axis_index("pipe")
    partner = (item, 1 - pipe)
    mirror = (items - 1 - item, pipe)
    per_clip = wave_out.shape[1]
    width = conv_ref.shape[1]
    table_rows = weight_scr.shape[1] - 4 * width - 16

    barrier = pltpu.get_barrier_semaphore()
    for other in (partner, mirror):
        pl.semaphore_signal(barrier, inc=1, device_id=other, device_id_type=MESH)

    row_at = lax.broadcasted_iota(jnp.int32, (2 * LANES, 2 * LANES), 0)
    col_at = lax.broadcasted_iota(jnp.int32, (2 * LANES, 2 * LANES), 1)
    wanted = jnp.where(col_at < LANES, 2 * col_at, 2 * (col_at - LANES) + 1)
    split = jnp.where(row_at == wanted, 1.0, 0.0).astype(BF16)
    on_first = pipe == 0
    lane = lax.broadcasted_iota(jnp.int32, (8, LANES), 1)
    kept = jnp.zeros((8, LANES), jnp.int32)
    given = kept
    for k in range(8):
        kept = jnp.where(lane == k, jnp.where(on_first, len_ref[k], len_ref[8 + k]), kept)
        given = jnp.where(lane == k, jnp.where(on_first, len_ref[24 + k], len_ref[16 + k]), given)
    len_out[:8] = kept
    len_scr[0] = given
    for block in range(per_clip):
        parted = nn(wave_ref[:, block * 2 * LANES : (block + 1) * 2 * LANES], split)
        codes = ids_ref[:, block * LANES : (block + 1) * LANES]
        even, odd = parted[:, :LANES], parted[:, LANES:]

        def chosen(values, first, second):
            return jnp.where(on_first, values[8 * first :][:8], values[8 * second :][:8])

        def both(first, second):
            return jnp.concatenate(
                [chosen(even, first, second), chosen(odd, first, second)], axis=0
            ).astype(BF16)

        wave_out[0, block] = both(0, 1)
        wave_scr[0, block] = both(3, 2)
        ids_out[0, block] = chosen(codes, 0, 1)
        ids_scr[0, block] = chosen(codes, 3, 2)

    pl.semaphore_wait(barrier, 2)
    copies = [
        remote(ref.at[0], ref.at[1], sems.at[2 * k], sems.at[2 * k + 1], mirror)
        for k, ref in enumerate((len_scr, wave_scr, ids_scr))
    ]
    for copy in copies:
        copy.start()

    groups = table_rows // width
    for h in range(groups):
        weight_scr[0, h * width : (h + 1) * width] = table_ref[:, h * LOW : (h + 1) * LOW].astype(
            BF16
        )
    blank = jnp.zeros((width, LOW - 3 * width), F32)
    conv = conv_ref[0]
    conv_t = [conv[:, k * width : (k + 1) * width].T for k in range(3)]
    points = [point_ref[0, 0], point_ref[0, 1]]
    edge = edge_ref[0]
    empty = jnp.zeros((6, width), F32)
    edge_t = jnp.concatenate([edge[1:3], empty, edge[3:], edge[:1], empty], axis=0)
    edge_square = jnp.concatenate([edge_t, jnp.zeros((width - 16, width), F32)], axis=0).T
    after = table_rows
    for pieces in (
        [conv, blank],
        conv_t + [blank],
        points + [value.T for value in points],
        [edge_square, jnp.zeros((width, LOW - width), F32)],
        [edge_t, jnp.zeros((16, LOW - width), F32)],
    ):
        value = jnp.concatenate(pieces, axis=1).astype(BF16)
        weight_scr[0, after : after + value.shape[0]] = value
        after += value.shape[0]
    over = remote(weight_scr.at[0], weight_scr.at[1], sems.at[6], sems.at[7], partner)
    over.start()
    weight_out[pipe] = weight_scr[0]
    over.wait()
    weight_out[1 - pipe] = weight_scr[1]
    for copy in copies:
        copy.wait()
    len_out[8:] = len_scr[1]
    wave_out[1] = wave_scr[1]
    ids_out[1] = ids_scr[1]


def shared(items, lengths, waveform, code_ids, conv, point, edge, table):
    per_clip = code_ids.shape[1] // LANES
    width = conv.shape[1]
    weight_rows = table.shape[1] // LOW * width + 4 * width + 16
    smem = pl.BlockSpec(memory_space=pltpu.SMEM)
    vmem = pl.BlockSpec(memory_space=pltpu.VMEM)
    wave_shape = (2, per_clip, 16, LANES)
    ids_shape = (2, per_clip, 8, LANES)
    weight_shape = (2, weight_rows, LOW)
    return pl.pallas_call(
        functools.partial(share_kernel, items),
        out_shape=(
            jax.ShapeDtypeStruct((16, LANES), jnp.int32),
            jax.ShapeDtypeStruct(wave_shape, BF16),
            jax.ShapeDtypeStruct(ids_shape, jnp.int32),
            jax.ShapeDtypeStruct(weight_shape, BF16),
        ),
        in_specs=[smem] + [vmem] * 6,
        out_specs=(vmem,) * 4,
        scratch_shapes=[
            pltpu.VMEM((2, 8, LANES), jnp.int32),
            pltpu.VMEM(wave_shape, BF16),
            pltpu.VMEM(ids_shape, jnp.int32),
            pltpu.VMEM(weight_shape, BF16),
            pltpu.SemaphoreType.DMA((8,)),
        ],
        compiler_params=pltpu.CompilerParams(
            collective_id=0, has_side_effects=True, vmem_limit_bytes=16 * 2**20
        ),
    )(lengths, waveform, code_ids, conv, point, edge, table)


def sum_kernel(
    items,
    payload_ref,
    stats_ref,
    sum_ref,
    stats_out,
    crossed,
    crossed_stats,
    part,
    part_stats,
    landed,
    landed_stats,
    whole,
    cross_sem,
    out_send,
    out_recv,
    stats_send,
    stats_recv,
    back_send,
    back_recv,
):
    item = lax.axis_index("item")
    pipe = lax.axis_index("pipe")
    partner = (item, 1 - pipe)
    piece = part.shape[1]

    def peer(d):
        return lax.rem(item + d, items)

    barrier = pltpu.get_barrier_semaphore()
    pl.semaphore_signal(barrier, inc=1, device_id=partner, device_id_type=MESH)

    @pl.loop(1, items)
    def _(d):
        pl.semaphore_signal(barrier, inc=1, device_id=(peer(d), pipe), device_id_type=MESH)

    pl.semaphore_wait(barrier, items)

    over = remote(payload_ref.at[1 - pipe], crossed, cross_sem.at[0], cross_sem.at[1], partner)
    over_stats = remote(stats_ref, crossed_stats, cross_sem.at[2], cross_sem.at[3], partner)
    over.start()
    over_stats.start()
    over_stats.wait()
    part_stats[...] = stats_ref[...] + crossed_stats[...]
    over.wait()

    def out_copy(to):
        return remote(
            part.at[to], landed.at[item], out_send.at[to], out_recv.at[item], (to, pipe)
        )

    def out_copy_stats(to):
        return remote(
            part_stats, landed_stats.at[item], stats_send.at[to], stats_recv.at[item], (to, pipe)
        )

    def add_up(k):
        rows = pl.ds(pl.multiple_of(k * piece, piece), piece)
        return payload_ref[pipe, rows] + crossed[rows]

    @pl.loop(1, items)
    def _(d):
        to = peer(d)
        part[to] = add_up(to).astype(BF16)
        out_copy(to).start()
        out_copy_stats(to).start()

    total = add_up(item)

    def take(d, carry):
        total, stats = carry
        source = peer(items - d)
        remote(
            part.at[source], landed.at[source], out_send.at[source], out_recv.at[source],
            (source, pipe),
        ).wait_recv()
        remote(
            part_stats, landed_stats.at[source], stats_send.at[source], stats_recv.at[source],
            (source, pipe),
        ).wait_recv()
        return total + landed[source].astype(F32), stats + landed_stats[source]

    total, stats = lax.fori_loop(1, items, take, (total, part_stats[...]))
    whole[item] = total.astype(BF16)
    stats_out[...] = stats

    def back_copy(place, slot, to):
        return remote(
            whole.at[place], whole.at[place], back_send.at[slot], back_recv.at[place], (to, pipe)
        )

    @pl.loop(1, items)
    def _(d):
        to = peer(d)
        back_copy(item, to, to).start()

    own = pl.ds(pl.multiple_of(item * piece, piece), piece)
    sum_ref[own] = total.astype(BF16).astype(F32)

    @pl.loop(1, items)
    def _(d):
        source = peer(items - d)
        back_copy(source, source, source).wait_recv()
        rows = pl.ds(pl.multiple_of(source * piece, piece), piece)
        sum_ref[rows] = whole[source].astype(F32)

    @pl.loop(1, items)
    def _(d):
        to = peer(d)
        out_copy(to).wait_send()
        out_copy_stats(to).wait_send()
        back_copy(item, to, to).wait_send()


def summed(items, payload, stats):
    rows = payload.shape[1]
    piece = rows // items
    vmem = pl.BlockSpec(memory_space=pltpu.VMEM)
    sems = pltpu.SemaphoreType.DMA((items,))
    return pl.pallas_call(
        functools.partial(sum_kernel, items),
        out_shape=(
            jax.ShapeDtypeStruct((rows, LANES), F32),
            jax.ShapeDtypeStruct(stats.shape, F32),
        ),
        in_specs=[vmem] * 2,
        out_specs=(vmem,) * 2,
        scratch_shapes=[
            pltpu.VMEM((rows, LANES), F32),
            pltpu.VMEM(stats.shape, F32),
            pltpu.VMEM((items, piece, LANES), BF16),
            pltpu.VMEM(stats.shape, F32),
            pltpu.VMEM((items, piece, LANES), BF16),
            pltpu.VMEM((items,) + stats.shape, F32),
            pltpu.VMEM((items, piece, LANES), BF16),
            pltpu.SemaphoreType.DMA((4,)),
        ]
        + [sems] * 6,
        compiler_params=pltpu.CompilerParams(
            collective_id=1, has_side_effects=True, vmem_limit_bytes=16 * 2**20
        ),
    )(payload, stats)


def update_kernel(*refs):
    rate_net, rate_code, sum_ref, stats_ref = refs[:4]
    states = refs[4:16]
    loss_ref = refs[16]
    results = refs[17:]
    width = states[0].shape[1]
    count = jnp.sum(stats_ref[8:], keepdims=True)
    loss_ref[0] = jnp.sum(stats_ref[:8]) / jnp.sum(stats_ref[8:])
    scale = 1.0 / count

    def step(kind, place, grad, rate):
        weight_ref, moment_ref, average_ref = (states[4 * j + kind] for j in range(3))
        new_ref, moment_new_ref, average_new_ref, copy_ref = results[4 * kind : 4 * kind + 4]
        grad = grad * scale
        moment = MOMENTUM * moment_ref[place] + grad
        weight = weight_ref[place] - rate * (grad + MOMENTUM * moment)
        new_ref[place] = weight
        moment_new_ref[place] = moment
        average_new_ref[place] = AVERAGE * average_ref[place] + (1.0 - AVERAGE) * weight
        copy_ref[place] = weight.astype(BF16)

    groups = states[3].shape[1] // LOW
    rows = groups * width
    for h in range(groups):
        for side in range(LOW // LANES):
            start = h * LOW + side * LANES
            grad = sum_ref[side * rows + h * width : side * rows + (h + 1) * width]
            place = (slice(None), slice(start, start + LANES))
            step(3, place, grad * (-2.0 * COMMIT), rate_code[0])
    first, second, third = (
        sum_ref[2 * rows + k * width : 2 * rows + (k + 1) * width] for k in range(3)
    )
    rate = rate_net[0]
    step(0, 0, jnp.concatenate([first, second[:, :width]], axis=1), rate)
    step(1, (0, 0), third[:, :width], rate)
    step(1, (0, 1), third[:, width:], rate)
    edge = [second[k : k + 1, width:] for k in (9, 0, 1, 8)]
    step(2, 0, jnp.concatenate(edge, axis=0), rate)


def updated(rates, sums, stats, states):
    smem = pl.BlockSpec(memory_space=pltpu.SMEM)
    shapes = [jax.ShapeDtypeStruct((1,), F32)]
    for weight in states[:4]:
        shapes += [jax.ShapeDtypeStruct(weight.shape, F32)] * 3
        shapes += [jax.ShapeDtypeStruct(weight.shape, BF16)]
    def block(value):
        return pl.BlockSpec(value.shape, lambda i: (0,) * len(value.shape))

    return pl.pallas_call(
        update_kernel,
        grid=(1,),
        out_shape=tuple(shapes),
        in_specs=[smem] * 2 + [block(value) for value in (sums, stats, *states)],
        out_specs=(smem,) + tuple(block(value) for value in shapes[1:]),
        compiler_params=pltpu.CompilerParams(vmem_limit_bytes=24 * 2**20),
    )(*rates, sums, stats, *states)


def per_device(
    waveform,
    lengths,
    code_ids,
    conv_w,
    point_w,
    edge_w,
    codebook,
    conv_mom,
    point_mom,
    edge_mom,
    code_mom,
    conv_avg,
    point_avg,
    edge_avg,
    code_avg,
    rate_net,
    rate_code,
):
    width = conv_w.shape[1]
    items = lax.axis_size("item")
    edge_w, edge_mom, edge_avg = (jnp.swapaxes(v, 1, 2) for v in (edge_w, edge_mom, edge_avg))
    codebook, code_mom, code_avg = (v.T for v in (codebook, code_mom, code_avg))
    rows = 2 * (codebook.shape[1] // LOW) * width + 3 * width
    piece = -(-rows // (16 * items)) * 16
    own_inputs = shared(items, lengths, waveform, code_ids, conv_w, point_w, edge_w, codebook)
    payload, stats = net(piece * items, *own_inputs)
    sums, stats = summed(items, payload, stats)
    states = (
        conv_w, point_w, edge_w, codebook,
        conv_mom, point_mom, edge_mom, code_mom,
        conv_avg, point_avg, edge_avg, code_avg,
    )
    loss, *rest = updated((rate_net, rate_code), sums, stats, states)
    edges = (jnp.swapaxes(v, 1, 2) for v in rest[8:12])
    return (loss.reshape(()), *rest[:8], *edges, *(v.T for v in rest[12:]))


def solution(mesh):
    weights = (
        P("pipe", None, None),
        P("pipe", None, None, None),
        P("pipe", None, None),
        P("pipe", None),
    )
    return jax.shard_map(
        per_device,
        mesh=mesh,
        in_specs=(P("item", None), P("item"), P("item", None), *weights, *weights, *weights, P(), P()),
        out_specs=(P(),) + tuple(spec for spec in weights for _ in range(4)),
        check_vma=False,
    )
```

```python
import functools

import jax
import jax.numpy as jnp
from jax import lax
from jax.experimental import pallas as pl
from jax.experimental.pallas import tpu as pltpu
from jax.sharding import PartitionSpec as P

REACH = 3
COMMIT = 0.02
MOMENTUM = 0.9
AVERAGE = 0.99

LANES = 128
TILE = 512
SLOTS = 8
LAG = TILE // LANES + 1
DEPTH = -(-4 * LAG * LANES // TILE)
LOW = 256
SPARE = 16
REAL = 8

MESH = pl.DeviceIdType.MESH
F32 = jnp.float32
BF16 = jnp.bfloat16


def nn(a, b):
    return lax.dot_general(a, b, (((1,), (0,)), ((), ())), preferred_element_type=F32)


def nt(a, b):
    return lax.dot_general(a, b, (((1,), (1,)), ((), ())), preferred_element_type=F32)


def moved(ext, distance):
    width = ext.shape[1]
    turned = ext if distance == 0 else pltpu.roll(ext, (-distance) % width, 1)
    return turned[:, LANES : width - LANES]


def relu_bf(values):
    return jnp.maximum(values, 0.0).astype(BF16)


def stack(rows, times):
    return jnp.concatenate([rows] * times, axis=0)


def net_kernel(
    len_src,
    wave_src,
    ids_src,
    weight_src,
    payload_ref,
    stats_ref,
    len_ref,
    wave_ref,
    ids_ref,
    weight_ref,
    load_sems,
    g_mix,
    g_point,
    g_edge,
    g_table,
    loss_ref,
    even_scr,
    odd_scr,
    code_scr,
    sig_r,
    msk_r,
    live_r,
    me_r,
    low_r,
    high_r,
    hi_r,
    strips_r,
    onehot_r,
    actu_e_r,
    chosen_r,
    actu_d_r,
    actp_e_r,
    encres_r,
    actp_d_r,
    resb_r,
    gapb_r,
    outs_r,
    douts_r,
    dbranch_d_r,
    dinner_d_r,
    dlatent_r,
    dbranch_e_r,
    dinner_e_r,
):
    pairs = (
        (len_src, len_ref), (wave_src, wave_ref), (ids_src, ids_ref), (weight_src, weight_ref)
    )
    loads = [
        pltpu.make_async_copy(source, place, load_sems.at[k])
        for k, (source, place) in enumerate(pairs)
    ]
    for load in loads:
        load.start()
    sets, per_clip = wave_ref.shape[:2]
    half = per_clip * LANES
    frames = 2 * half
    width = 64
    groups = 2 * (weight_ref.shape[1] - 4 * width - 16) // width
    table_rows = groups // 2 * width
    per_tile = TILE // LANES

    rings = (
        sig_r, msk_r, live_r, me_r, low_r, high_r, hi_r, strips_r, onehot_r, actu_e_r, chosen_r,
        actu_d_r, actp_e_r, encres_r, actp_d_r, resb_r, gapb_r, outs_r, douts_r, dbranch_d_r,
        dinner_d_r, dlatent_r, dbranch_e_r, dinner_e_r,
    )
    slots = SLOTS * per_tile

    @pl.loop(slots - 4 * LAG - 2, slots)
    def _(slot):
        for ref in rings:
            ref[slot] = jnp.zeros(ref.shape[1:], ref.dtype)

    for ref in (g_mix, g_point, g_edge, g_table, loss_ref):
        ref[...] = jnp.zeros(ref.shape, ref.dtype)

    for load in loads:
        load.wait()

    def weight(part, start, rows, first, columns):
        start += table_rows
        return weight_ref[part, start : start + rows, first : first + columns]

    conv = [weight(part, 0, width, 0, 3 * width) for part in range(2)]
    conv_t = [weight(part, width, width, 0, 3 * width) for part in range(2)]
    point = [weight(k // 2, 2 * width, width, k % 2 * width, width) for k in range(4)]
    point_t = [weight(k // 2, 2 * width, width, (2 + k % 2) * width, width) for k in range(4)]
    edge = [weight(part, 3 * width, width, 0, 16) for part in range(2)]
    edge_t = [weight(part, 4 * width, 16, 0, width) for part in range(2)]

    def beside(*parts):
        return jnp.concatenate(parts, axis=1)

    same = lax.broadcasted_iota(jnp.int32, (width, width), 0) == lax.broadcasted_iota(
        jnp.int32, (width, width), 1
    )
    share = jnp.where(same, 2.0 * COMMIT, 0.0)
    share_bf = share.astype(BF16)
    share_rest = (share - share_bf.astype(F32)).astype(BF16)
    result_e = beside(point[0], edge[0])
    result_d = beside(point[3], point[2])
    back_d = beside(conv_t[1], edge[1])
    back_latent = beside(point_t[2], share_bf, share_rest)
    back_e = beside(conv_t[0], point_t[1])

    for k in range(sets):
        for block in range(per_clip):
            rows = slice(8 * k, 8 * k + 8)
            parted = wave_ref[k, block].astype(F32)
            even_scr[block, rows] = parted[:8]
            odd_scr[block, rows] = parted[8:]
            code_scr[block, rows] = ids_ref[k, block]

    clips = 8 * sets

    def blocks_of(length):
        valid = lax.shift_right_arithmetic(length + 1, 1)
        return lax.shift_right_arithmetic(valid + (SPARE + LANES - 1), 7)

    def length_of(clip):
        return len_ref[jnp.bitwise_and(clip, 8), jnp.bitwise_and(clip, 7)]

    def add_clip(c, carry):
        length = length_of(c)
        return carry[0] + blocks_of(length), carry[1] + length

    blocks, count = lax.fori_loop(0, clips, add_clip, (jnp.int32(0), jnp.int32(0)))
    tiles = lax.div(blocks + per_tile - 1, jnp.int32(per_tile)) + DEPTH

    sub = lax.broadcasted_iota(jnp.int32, (8, LANES), 0)
    lane = lax.broadcasted_iota(jnp.int32, (8, LANES), 1)
    sub_ext = lax.broadcasted_iota(jnp.int32, (8, TILE + 2 * LANES), 0)
    sub_tile = lax.broadcasted_iota(jnp.int32, (8, TILE), 0)
    iota16 = lax.broadcasted_iota(jnp.int32, (16, TILE), 0).astype(F32).astype(BF16)

    table = jnp.concatenate([weight_ref[part, :table_rows] for part in range(2)], axis=0)

    def taps(ext):
        later = moved(ext, 1)
        earlier = moved(ext, -1)
        other = jnp.where(sub_tile == 0, later, jnp.where(sub_tile == 1, earlier, 0.0))
        return jnp.concatenate([moved(ext, 0), other], axis=0)

    def fetch(state, slot):
        clip, place = state
        real = clip < clips
        length = jnp.where(real, length_of(clip), -frames)
        row = pl.ds(jnp.minimum(clip, clips - 1), 1)
        here = (jnp.minimum(place, per_clip - 1), row, slice(None))
        t = place * LANES + lane
        even_ok = 2 * t < length
        odd_ok = 2 * t + 1 < length
        even = jnp.broadcast_to(even_scr[here], (8, LANES))
        odd = jnp.broadcast_to(odd_scr[here], (8, LANES))
        code = jnp.broadcast_to(code_scr[here], (8, LANES))
        live = t < jnp.minimum(lax.shift_right_arithmetic(length + 1, 1) + REAL, half)
        low = jnp.where(live, jnp.bitwise_and(code, LOW - 1), -1).astype(F32)
        high = lax.shift_right_logical(code, 8).astype(F32)
        sig_r[slot] = jnp.where(
            (sub == 0) & even_ok, even, jnp.where((sub == 1) & odd_ok, odd, 0.0)
        )
        msk_r[slot] = jnp.where(((sub == 0) & even_ok) | ((sub == 1) & odd_ok), 1.0, 0.0)
        live_r[slot] = jnp.where(live, 1.0, 0.0)
        me_r[slot] = jnp.where(even_ok, 1.0, 0.0)
        low_r[slot] = stack(low, 2).astype(BF16)
        high_r[slot] = high
        hi_r[slot] = stack(high, 2).astype(BF16)
        done = place + 1 >= blocks_of(length)
        clip = jnp.where(done, jnp.minimum(clip + 1, clips), clip)
        return clip, jnp.where(done, 0, place + 1)

    state = (jnp.int32(0), jnp.int32(0))
    for b in range(per_tile + 1):
        state = fetch(state, b)

    def tile_step(names, i, state):
        def block(lag, b):
            return jnp.bitwise_and(i * per_tile - lag + b, slots - 1)

        def load(ref, lag, first=0, last=per_tile):
            return jnp.concatenate([ref[block(lag, b)] for b in range(first, last)], axis=1)

        def load_ext(ref, lag):
            return load(ref, lag, -1, per_tile + 1)

        stores = []

        def keep(ref, lag, value):
            stores.append((ref, lag, value))

        def spread(ext, way):
            return jnp.concatenate([moved(ext, d * way) for d in (-REACH, 0, REACH)], axis=0)

        def first_step():
            lag = 0
            sig_ext, live0 = load_ext(sig_r, lag), load(live_r, lag)
            hi0 = load(high_r, lag)
            low16 = load(low_r, lag) - iota16
            strips = (taps(sig_ext) * stack(live0, 2)).astype(BF16)
            onehot = jnp.concatenate(
                [
                    jnp.where(low16 == float(16 * r), jnp.ones((), BF16), jnp.zeros((), BF16))
                    for r in range(LOW // 16)
                ],
                axis=0,
            )
            keep(strips_r, lag, strips)
            keep(onehot_r, lag, onehot)
            yield
            picked = nn(table, onehot)
            hidden = nn(edge[0], strips)
            yield
            parts = [jnp.zeros((8, TILE), F32) for _ in range(width // 8)]
            for h in range(groups):
                here = hi0 == float(h)
                parts = [
                    jnp.where(here, picked[h * width + 8 * r : h * width + 8 * r + 8], parts[r])
                    for r in range(width // 8)
                ]
            chosen = jnp.concatenate(parts, axis=0).astype(BF16)
            keep(chosen_r, lag, chosen)
            keep(actu_e_r, lag, relu_bf(hidden))
            yield
            decin = nn(point[2], chosen)
            yield
            keep(actu_d_r, lag, relu_bf(decin))

        def second_step():
            lag = LAG
            actu_e, actu_d = load_ext(actu_e_r, lag), load_ext(actu_d_r, lag)
            strips, chosen, me = load(strips_r, lag), load(chosen_r, lag), load(me_r, lag)
            yield
            inner_e = nn(conv[0], spread(actu_e, 1))
            inner_d = nn(conv[1], spread(actu_d, 1))
            yield
            actp_e = relu_bf(inner_e)
            actp_d = relu_bf(inner_d)
            keep(actp_e_r, lag, actp_e)
            keep(actp_d_r, lag, actp_d)
            yield
            sum_e = nn(result_e, jnp.concatenate([actp_e, strips], axis=0))
            sum_d = nn(result_d, jnp.concatenate([actp_d, chosen], axis=0))
            yield
            encres = sum_e.astype(BF16)
            resb = sum_d.astype(BF16)
            keep(encres_r, lag, encres)
            keep(resb_r, lag, resb)
            yield
            latent = nn(point[1], encres)
            outs = nn(edge_t[1], resb)
            yield
            keep(outs_r, lag, outs)
            gap = (latent.astype(BF16).astype(F32) - chosen.astype(F32)) * stack(me, width // 8)
            keep(gapb_r, lag, gap.astype(BF16))
            square = gap * gap
            rows = square[:8]
            for r in range(1, width // 8):
                rows = rows + square[8 * r : 8 * r + 8]
            add_loss(COMMIT * rows)

        def scatter_step():
            lag = LAG + per_tile
            onehot, hi, gap = load(onehot_r, lag), load(hi_r, lag), load(gapb_r, lag)
            yield
            terms = []
            for h in range(groups):
                here = hi == float(h)
                terms += [
                    jnp.where(here, gap[16 * r : 16 * r + 16], jnp.zeros((), BF16))
                    for r in range(width // 16)
                ]
            found = nt(jnp.concatenate(terms, axis=0), onehot)
            yield
            g_table[...] += found

        def add_loss(rows):
            total = rows[:, :LANES]
            for j in range(1, per_tile):
                total = total + rows[:, j * LANES : (j + 1) * LANES]
            loss_ref[...] += total

        def third_step():
            lag = 2 * LAG
            outs_ext, live_ext = load_ext(outs_r, lag), load_ext(live_r, lag)
            sig_ext, msk_ext = load_ext(sig_r, lag), load_ext(msk_r, lag)
            actp, resb = load(actp_d_r, lag), load(resb_r, lag)
            outs_ext = outs_ext * stack(live_ext, 2)
            shifted = outs_ext[8:]
            wide = TILE + 2 * LANES
            crossed = jnp.where(
                sub_ext == 0, pltpu.roll(shifted, 1, 1), pltpu.roll(shifted, wide - 1, 1)
            )
            error = (outs_ext[:8] + crossed - sig_ext) * msk_ext
            middle = moved(error, 0)
            douts = (2.0 * taps(error) * stack(moved(live_ext, 0), 2)).astype(BF16)
            yield
            dres = nn(edge[1], douts)
            yield
            dbranch = dres.astype(BF16)
            keep(douts_r, lag, douts)
            keep(dbranch_d_r, lag, dbranch)
            add_loss(middle * middle)
            yield
            dinner = nn(point_t[3], dbranch)
            yield
            keep(dinner_d_r, lag, jnp.where(actp > 0, dinner.astype(BF16), 0))
            yield
            g_point[1] += nt(dbranch, actp)
            g_edge[1] += nt(douts, resb)

        def fourth_step():
            lag = 3 * LAG
            around = spread(load_ext(dinner_d_r, lag), -1)
            actu, chosen, douts = load(actu_d_r, lag), load(chosen_r, lag), load(douts_r, lag)
            actp = load(actp_e_r, lag)
            gap, dbranch_d = load(gapb_r, lag), load(dbranch_d_r, lag)
            yield
            both = nn(back_d, jnp.concatenate([around, douts], axis=0))
            yield
            ddecin = jnp.where(actu > 0, both.astype(BF16), dbranch_d)
            yield
            back = nn(back_latent, jnp.concatenate([ddecin, gap, gap], axis=0))
            yield
            dlatent = back.astype(BF16)
            keep(dlatent_r, lag, dlatent)
            yield
            denc = nn(point_t[1], dlatent)
            yield
            dbranch = denc.astype(BF16)
            keep(dbranch_e_r, lag, dbranch)
            yield
            dinner = nn(point_t[0], dbranch)
            yield
            keep(dinner_e_r, lag, jnp.where(actp > 0, dinner.astype(BF16), 0))
            yield
            g_mix[1] += nt(
                jnp.concatenate([actu, chosen], axis=0), jnp.concatenate([around, ddecin], axis=0)
            )
            g_point[0] += nt(dbranch, actp)

        def fifth_step():
            lag = 4 * LAG
            around = spread(load_ext(dinner_e_r, lag), -1)
            actu, strips = load(actu_e_r, lag), load(strips_r, lag)
            dlatent, dbranch = load(dlatent_r, lag), load(dbranch_e_r, lag)
            encres = load(encres_r, lag)
            yield
            both = nn(back_e, jnp.concatenate([around, dlatent], axis=0))
            yield
            dhidden = jnp.where(actu > 0, both.astype(BF16), dbranch)
            yield
            g_mix[0] += nt(
                jnp.concatenate([actu, encres], axis=0), jnp.concatenate([around, dlatent], axis=0)
            )
            yield
            g_edge[0] += nt(strips, dhidden)

        known = {
            1: first_step,
            4: fourth_step,
            2: second_step,
            0: scatter_step,
            3: third_step,
            5: fifth_step,
        }
        steps = [f() for name, f in known.items() if name in names]
        while steps:
            left = []
            for step in steps:
                try:
                    next(step)
                    left.append(step)
                except StopIteration:
                    pass
            steps = left
        for ref, lag, value in stores:
            for b in range(per_tile):
                ref[block(lag, b)] = value[:, b * LANES : (b + 1) * LANES]
        if 1 in names:
            for b in range(per_tile):
                state = fetch(state, block(-LAG, b))
        return state

    ranges = (
        ((1, 2), 0, 2),
        (range(6), 2, tiles - 2),
        ((4, 5), tiles - 2, tiles - 1),
        ((5,), tiles - 1, tiles),
    )
    for names, begin, end in ranges:
        state = lax.fori_loop(begin, end, functools.partial(tile_step, names), state)

    loss_row = jnp.sum(loss_ref[...], axis=0, keepdims=True)
    count_row = jnp.where(lane == 0, count, 0).astype(F32)
    stats_ref[...] = jnp.where(
        jnp.bitwise_and(sub, 1) == 0, jnp.broadcast_to(loss_row, (8, LANES)), count_row
    )
    rows = groups // 2 * width
    for part in range(2):
        payload_ref[part, :rows] = g_table[part * rows : (part + 1) * rows, :LANES]
        payload_ref[part, rows : 2 * rows] = g_table[part * rows : (part + 1) * rows, LANES:]
        conv_rows = [g_mix[part, :width, k * width : (k + 1) * width].T for k in range(3)]
        mixed = g_mix[part, width:, 3 * width :].T
        edge_rows = jnp.concatenate(
            [g_edge[part], jnp.zeros((width - 16, width), F32)], axis=0
        )
        after = 2 * rows
        for pair in (
            conv_rows[:2],
            (conv_rows[2], edge_rows),
            (mixed, g_point[1]) if part else (g_point[0], mixed),
        ):
            payload_ref[part, after : after + width] = jnp.concatenate(pair, axis=1)
            after += width
        rest = payload_ref.shape[1] - after
        if rest:
            payload_ref[part, after:] = jnp.zeros((rest, LANES), F32)


def net(rows, lengths, wave, codes, weights):
    sets, per_clip = wave.shape[:2]
    clips = 8 * sets
    width = 64
    table_rows = 2 * (weights.shape[1] - 4 * width - 16)
    slots = SLOTS * TILE // LANES
    vmem = pl.BlockSpec(memory_space=pltpu.VMEM)

    def ring(rows, dtype):
        return pltpu.VMEM((slots, rows, LANES), dtype)

    return pl.pallas_call(
        net_kernel,
        out_shape=(
            jax.ShapeDtypeStruct((2, rows, LANES), F32),
            jax.ShapeDtypeStruct((8, LANES), F32),
        ),
        in_specs=[pl.BlockSpec(memory_space=pl.ANY)] * 4,
        out_specs=(vmem,) * 2,
        scratch_shapes=[
            pltpu.SMEM(lengths.shape, lengths.dtype),
            pltpu.VMEM(wave.shape, wave.dtype),
            pltpu.VMEM(codes.shape, codes.dtype),
            pltpu.VMEM(weights.shape, weights.dtype),
            pltpu.SemaphoreType.DMA((4,)),
            pltpu.VMEM((2, 2 * width, 4 * width), F32),
            pltpu.VMEM((2, width, width), F32),
            pltpu.VMEM((2, 16, width), F32),
            pltpu.VMEM((table_rows, LOW), F32),
            pltpu.VMEM((8, LANES), F32),
            pltpu.VMEM((per_clip, clips, LANES), F32),
            pltpu.VMEM((per_clip, clips, LANES), F32),
            pltpu.VMEM((per_clip, clips, LANES), jnp.int32),
            *(ring(8, F32) for _ in range(4)),
            ring(16, BF16),
            ring(8, F32),
            *(ring(16, BF16) for _ in range(2)),
            ring(LOW, BF16),
            *(ring(width, BF16) for _ in range(8)),
            ring(16, F32),
            ring(16, BF16),
            *(ring(width, BF16) for _ in range(5)),
        ],
        compiler_params=pltpu.CompilerParams(vmem_limit_bytes=60 * 2**20),
    )(lengths, wave, codes, weights)


def remote(src, dst, send, recv, to):
    return pltpu.make_async_remote_copy(
        src_ref=src, dst_ref=dst, send_sem=send, recv_sem=recv, device_id=to, device_id_type=MESH
    )


def share_kernel(items, *refs):
    sources, (len_out, wave_out, ids_out, weight_out), inputs = refs[:7], refs[7:11], refs[11:18]
    len_ref, wave_ref, ids_ref, conv_ref, point_ref, edge_ref, table_ref = inputs
    len_scr, wave_scr, ids_scr, weight_scr, sems, load_sems = refs[18:]
    loads = [
        pltpu.make_async_copy(source, place, load_sems.at[k])
        for k, (source, place) in enumerate(zip(sources, inputs))
    ]
    for load in loads:
        load.start()
    item = lax.axis_index("item")
    pipe = lax.axis_index("pipe")
    partner = (item, 1 - pipe)
    mirror = (items - 1 - item, pipe)
    per_clip = wave_out.shape[1]
    width = conv_ref.shape[1]
    table_rows = weight_scr.shape[1] - 4 * width - 16

    barrier = pltpu.get_barrier_semaphore()
    for other in (partner, mirror):
        pl.semaphore_signal(barrier, inc=1, device_id=other, device_id_type=MESH)

    row_at = lax.broadcasted_iota(jnp.int32, (2 * LANES, 2 * LANES), 0)
    col_at = lax.broadcasted_iota(jnp.int32, (2 * LANES, 2 * LANES), 1)
    wanted = jnp.where(col_at < LANES, 2 * col_at, 2 * (col_at - LANES) + 1)
    split = jnp.where(row_at == wanted, 1.0, 0.0).astype(BF16)
    on_first = pipe == 0
    for load in loads[:3]:
        load.wait()
    lane = lax.broadcasted_iota(jnp.int32, (8, LANES), 1)
    kept = jnp.zeros((8, LANES), jnp.int32)
    given = kept
    for k in range(8):
        kept = jnp.where(lane == k, jnp.where(on_first, len_ref[k], len_ref[8 + k]), kept)
        given = jnp.where(lane == k, jnp.where(on_first, len_ref[24 + k], len_ref[16 + k]), given)
    len_out[:8] = kept
    len_scr[0] = given
    clips = wave_ref.shape[0]
    strips = [wave_ref[:, k * 2 * LANES : (k + 1) * 2 * LANES] for k in range(per_clip)]
    parted = nn(jnp.concatenate(strips, axis=0), split)

    def chosen(values, first, second):
        return jnp.where(on_first, values[8 * first :][:8], values[8 * second :][:8])

    def both(values, first, second):
        pair = [
            chosen(side, first, second) for side in (values[:, :LANES], values[:, LANES:])
        ]
        return jnp.concatenate(pair, axis=0).astype(BF16)

    codes = [ids_ref[:, k * LANES : (k + 1) * LANES] for k in range(per_clip)]
    for k in range(per_clip):
        values = parted[clips * k : clips * (k + 1)]
        wave_scr[0, k] = both(values, 3, 2)
        wave_out[0, k] = both(values, 0, 1)
        ids_out[0, k] = chosen(codes[k], 0, 1)
    for k in range(per_clip // 2):
        pair = [chosen(codes[2 * k + j], 3, 2) for j in range(2)]
        ids_scr[0, k] = jnp.concatenate(pair, axis=0).astype(jnp.int16)

    pl.semaphore_wait(barrier, 2)
    copies = [
        remote(ref.at[0], ref.at[1], sems.at[2 * k], sems.at[2 * k + 1], mirror)
        for k, ref in enumerate((len_scr, wave_scr, ids_scr))
    ]
    for copy in copies:
        copy.start()

    for load in loads[3:]:
        load.wait()
    groups = table_rows // width
    for h in range(groups):
        weight_scr[0, h * width : (h + 1) * width] = table_ref[:, h * LOW : (h + 1) * LOW].astype(
            BF16
        )
    blank = jnp.zeros((width, LOW - 3 * width), F32)
    conv = conv_ref[0]
    conv_t = [conv[:, k * width : (k + 1) * width].T for k in range(3)]
    points = [point_ref[0, 0], point_ref[0, 1]]
    edge = edge_ref[0]
    empty = jnp.zeros((6, width), F32)
    edge_t = jnp.concatenate([edge[1:3], empty, edge[3:], edge[:1], empty], axis=0)
    edge_square = jnp.concatenate([edge_t, jnp.zeros((width - 16, width), F32)], axis=0).T
    after = table_rows
    for pieces in (
        [conv, blank],
        conv_t + [blank],
        points + [value.T for value in points],
        [edge_square, jnp.zeros((width, LOW - width), F32)],
        [edge_t, jnp.zeros((16, LOW - width), F32)],
    ):
        value = jnp.concatenate(pieces, axis=1).astype(BF16)
        weight_scr[0, after : after + value.shape[0]] = value
        after += value.shape[0]
    over = remote(weight_scr.at[0], weight_scr.at[1], sems.at[6], sems.at[7], partner)
    over.start()
    weight_out[pipe] = weight_scr[0]
    over.wait()
    weight_out[1 - pipe] = weight_scr[1]
    for copy in copies:
        copy.wait()
    len_out[8:] = len_scr[1]
    wave_out[1] = wave_scr[1]
    for k in range(per_clip // 2):
        pair = ids_scr[1, k].astype(jnp.int32)
        ids_out[1, 2 * k], ids_out[1, 2 * k + 1] = pair[:8], pair[8:]


def shared(items, lengths, waveform, code_ids, conv, point, edge, table):
    per_clip = code_ids.shape[1] // LANES
    width = conv.shape[1]
    weight_rows = table.shape[1] // LOW * width + 4 * width + 16
    vmem = pl.BlockSpec(memory_space=pltpu.VMEM)
    wave_shape = (2, per_clip, 16, LANES)
    ids_shape = (2, per_clip, 8, LANES)
    weight_shape = (2, weight_rows, LOW)
    return pl.pallas_call(
        functools.partial(share_kernel, items),
        out_shape=(
            jax.ShapeDtypeStruct((16, LANES), jnp.int32),
            jax.ShapeDtypeStruct(wave_shape, BF16),
            jax.ShapeDtypeStruct(ids_shape, jnp.int32),
            jax.ShapeDtypeStruct(weight_shape, BF16),
        ),
        in_specs=[pl.BlockSpec(memory_space=pl.ANY)] * 7,
        out_specs=(vmem,) * 4,
        scratch_shapes=[pltpu.SMEM(lengths.shape, jnp.int32)]
        + [
            pltpu.VMEM(value.shape, value.dtype)
            for value in (waveform, code_ids, conv, point, edge, table)
        ]
        + [
            pltpu.VMEM((2, 8, LANES), jnp.int32),
            pltpu.VMEM(wave_shape, BF16),
            pltpu.VMEM((2, per_clip // 2, 16, LANES), jnp.int16),
            pltpu.VMEM(weight_shape, BF16),
            pltpu.SemaphoreType.DMA((8,)),
            pltpu.SemaphoreType.DMA((7,)),
        ],
        compiler_params=pltpu.CompilerParams(
            collective_id=0, has_side_effects=True, vmem_limit_bytes=60 * 2**20
        ),
    )(lengths, waveform, code_ids, conv, point, edge, table)


def sum_kernel(
    items,
    payload_ref,
    stats_ref,
    sum_ref,
    stats_out,
    crossed,
    crossed_stats,
    part,
    landed,
    whole,
    stats_sem,
    cross_send,
    cross_recv,
    out_send,
    out_recv,
    back_send,
    back_recv,
):
    item = lax.axis_index("item")
    pipe = lax.axis_index("pipe")
    partner = (item, 1 - pipe)
    piece = part.shape[1]

    def peer(d):
        if items & (items - 1):
            return lax.rem(item + d, items)
        return jnp.bitwise_and(item + d, items - 1)

    def rows_of(k):
        return pl.ds(pl.multiple_of(k * piece, piece), piece)

    barrier = pltpu.get_barrier_semaphore()
    pl.semaphore_signal(barrier, inc=1, device_id=partner, device_id_type=MESH)

    @pl.loop(1, items)
    def _(d):
        pl.semaphore_signal(barrier, inc=1, device_id=(peer(d), pipe), device_id_type=MESH)

    pl.semaphore_wait(barrier, items)

    def cross_copy(k):
        return remote(
            payload_ref.at[1 - pipe, rows_of(k)], crossed.at[rows_of(k)],
            cross_send.at[k], cross_recv.at[k], partner,
        )

    over_stats = remote(stats_ref, crossed_stats, stats_sem.at[0], stats_sem.at[1], partner)

    @pl.loop(1, items + 1)
    def _(d):
        cross_copy(peer(d)).start()

    over_stats.start()

    def out_copy(to, place):
        return remote(
            part.at[to], landed.at[place], out_send.at[to], out_recv.at[place], (to, pipe)
        )

    @pl.loop(1, items)
    def _(d):
        to = peer(d)
        cross_copy(to).wait_recv()
        part[to] = (payload_ref[pipe, rows_of(to)] + crossed[rows_of(to)]).astype(BF16)
        out_copy(to, item).start()

    cross_copy(item).wait_recv()
    total = payload_ref[pipe, rows_of(item)] + crossed[rows_of(item)]
    over_stats.wait()
    stats = stats_ref[...] + crossed_stats[...]
    high = stats.astype(BF16).astype(F32)
    middle = (stats - high).astype(BF16).astype(F32)
    low = stats - high - middle
    sub = lax.broadcasted_iota(jnp.int32, (8, LANES), 0)
    message = jnp.where(sub < 2, high, jnp.where(sub < 4, middle, jnp.where(sub < 6, low, 0.0)))
    whole[item, piece:] = jnp.concatenate([message, jnp.zeros_like(message)], axis=0).astype(BF16)

    def take(d, total):
        source = peer(items - d)
        out_copy(source, source).wait_recv()
        return total + landed[source].astype(F32)

    total = lax.fori_loop(1, items, take, total)
    whole[item, :piece] = total.astype(BF16)

    def back_copy(place, to):
        return remote(
            whole.at[place], whole.at[place], back_send.at[to], back_recv.at[place], (to, pipe)
        )

    @pl.loop(1, items)
    def _(d):
        back_copy(item, peer(d)).start()

    sum_ref[rows_of(item)] = whole[item, :piece].astype(F32)

    def gather(d, stats):
        source = peer(items - d)
        back_copy(source, source).wait_recv()
        sum_ref[rows_of(source)] = whole[source, :piece].astype(F32)
        return stats + whole[source, piece:].astype(F32)[:8]

    stats_out[...] = lax.fori_loop(1, items, gather, whole[item, piece:].astype(F32)[:8])

    @pl.loop(1, items)
    def _(d):
        to = peer(d)
        cross_copy(to).wait_send()
        out_copy(to, item).wait_send()
        back_copy(item, to).wait_send()

    cross_copy(item).wait_send()


def summed(items, payload, stats):
    rows = payload.shape[1]
    piece = rows // items
    vmem = pl.BlockSpec(memory_space=pltpu.VMEM)
    sems = pltpu.SemaphoreType.DMA((items,))
    return pl.pallas_call(
        functools.partial(sum_kernel, items),
        out_shape=(
            jax.ShapeDtypeStruct((rows, LANES), F32),
            jax.ShapeDtypeStruct(stats.shape, F32),
        ),
        in_specs=[vmem] * 2,
        out_specs=(vmem,) * 2,
        scratch_shapes=[
            pltpu.VMEM((rows, LANES), F32),
            pltpu.VMEM(stats.shape, F32),
            pltpu.VMEM((items, piece, LANES), BF16),
            pltpu.VMEM((items, piece, LANES), BF16),
            pltpu.VMEM((items, piece + 16, LANES), BF16),
            pltpu.SemaphoreType.DMA((2,)),
        ]
        + [sems] * 6,
        compiler_params=pltpu.CompilerParams(
            collective_id=1, has_side_effects=True, vmem_limit_bytes=16 * 2**20
        ),
    )(payload, stats)


def update_kernel(*refs):
    rate_net, rate_code, sum_ref, stats_ref = refs[:4]
    states = refs[4:16]
    loss_ref = refs[16]
    results = refs[17:]
    width = states[0].shape[1]
    odd = jnp.bitwise_and(lax.broadcasted_iota(jnp.int32, stats_ref.shape, 0), 1) == 1
    counts = jnp.where(odd, stats_ref[...], 0.0)
    loss_ref[0] = jnp.sum(jnp.where(odd, 0.0, stats_ref[...])) / jnp.sum(counts)
    scale = 1.0 / jnp.sum(counts, keepdims=True)

    def step(kind, place, grad, rate):
        weight_ref, moment_ref, average_ref = (states[4 * j + kind] for j in range(3))
        new_ref, moment_new_ref, average_new_ref, copy_ref = results[4 * kind : 4 * kind + 4]
        grad = grad * scale
        moment = MOMENTUM * moment_ref[place] + grad
        weight = weight_ref[place] - rate * (grad + MOMENTUM * moment)
        new_ref[place] = weight
        moment_new_ref[place] = moment
        average_new_ref[place] = AVERAGE * average_ref[place] + (1.0 - AVERAGE) * weight
        copy_ref[place] = weight.astype(BF16)

    groups = states[3].shape[1] // LOW
    rows = groups * width
    for h in range(groups):
        for side in range(LOW // LANES):
            start = h * LOW + side * LANES
            grad = sum_ref[side * rows + h * width : side * rows + (h + 1) * width]
            place = (slice(None), slice(start, start + LANES))
            step(3, place, grad * (-2.0 * COMMIT), rate_code[0])
    first, second, third = (
        sum_ref[2 * rows + k * width : 2 * rows + (k + 1) * width] for k in range(3)
    )
    rate = rate_net[0]
    step(0, 0, jnp.concatenate([first, second[:, :width]], axis=1), rate)
    step(1, (0, 0), third[:, :width], rate)
    step(1, (0, 1), third[:, width:], rate)
    edge = [second[k : k + 1, width:] for k in (9, 0, 1, 8)]
    step(2, 0, jnp.concatenate(edge, axis=0), rate)


def updated(rates, sums, stats, states):
    smem = pl.BlockSpec(memory_space=pltpu.SMEM)
    shapes = [jax.ShapeDtypeStruct((1,), F32)]
    for weight in states[:4]:
        shapes += [jax.ShapeDtypeStruct(weight.shape, F32)] * 3
        shapes += [jax.ShapeDtypeStruct(weight.shape, BF16)]
    def block(value):
        return pl.BlockSpec(value.shape, lambda i: (0,) * len(value.shape))

    return pl.pallas_call(
        update_kernel,
        grid=(1,),
        out_shape=tuple(shapes),
        in_specs=[smem] * 2 + [block(value) for value in (sums, stats, *states)],
        out_specs=(smem,) + tuple(block(value) for value in shapes[1:]),
        compiler_params=pltpu.CompilerParams(vmem_limit_bytes=24 * 2**20),
    )(*rates, sums, stats, *states)


def per_device(
    waveform,
    lengths,
    code_ids,
    conv_w,
    point_w,
    edge_w,
    codebook,
    conv_mom,
    point_mom,
    edge_mom,
    code_mom,
    conv_avg,
    point_avg,
    edge_avg,
    code_avg,
    rate_net,
    rate_code,
):
    width = conv_w.shape[1]
    items = lax.axis_size("item")
    edge_w, edge_mom, edge_avg = (jnp.swapaxes(v, 1, 2) for v in (edge_w, edge_mom, edge_avg))
    codebook, code_mom, code_avg = (v.T for v in (codebook, code_mom, code_avg))
    rows = 2 * (codebook.shape[1] // LOW) * width + 3 * width
    piece = -(-rows // (16 * items)) * 16
    own_inputs = shared(items, lengths, waveform, code_ids, conv_w, point_w, edge_w, codebook)
    payload, stats = net(piece * items, *own_inputs)
    sums, stats = summed(items, payload, stats)
    states = (
        conv_w, point_w, edge_w, codebook,
        conv_mom, point_mom, edge_mom, code_mom,
        conv_avg, point_avg, edge_avg, code_avg,
    )
    loss, *rest = updated((rate_net, rate_code), sums, stats, states)
    edges = (jnp.swapaxes(v, 1, 2) for v in rest[8:12])
    return (loss.reshape(()), *rest[:8], *edges, *(v.T for v in rest[12:]))


def solution(mesh):
    weights = (
        P("pipe", None, None),
        P("pipe", None, None, None),
        P("pipe", None, None),
        P("pipe", None),
    )
    return jax.shard_map(
        per_device,
        mesh=mesh,
        in_specs=(P("item", None), P("item"), P("item", None), *weights, *weights, *weights, P(), P()),
        out_specs=(P(),) + tuple(spec for spec in weights for _ in range(4)),
        check_vma=False,
    )
```

```python
import functools

import jax
import jax.numpy as jnp
from jax import lax
from jax.experimental import pallas as pl
from jax.experimental.pallas import tpu as pltpu
from jax.sharding import PartitionSpec as P

REACH = 3
COMMIT = 0.02
MOMENTUM = 0.9
AVERAGE = 0.99

LANES = 128
TILE = 512
SLOTS = 8
LAG = TILE // LANES + 1
HEAD = 2
DEPTH = -(-4 * LAG * LANES // TILE)
LOW = 256
SPARE = 8
REAL = 4

MESH = pl.DeviceIdType.MESH
ORDER = (1, 6, 2, 3, 4, 0, 5, 7, 1, 6, 2, 3, 4, 0, 5, 7, 1, 6, 2, 3, 4, 0, 5, 7, 1, 6, 2, 3, 0, 5, 7, 1, 6, 2, 3, 5, 7, 6, 2, 3, 5, 7, 6, 2, 3, 5, 7, 6, 2, 5, 6, 5, 6, 6, 6)
F32 = jnp.float32
BF16 = jnp.bfloat16


def nn(a, b):
    return lax.dot_general(a, b, (((1,), (0,)), ((), ())), preferred_element_type=F32)


def nt(a, b):
    return lax.dot_general(a, b, (((1,), (1,)), ((), ())), preferred_element_type=F32)


def moved(ext, distance):
    width = ext.shape[1]
    turned = ext if distance == 0 else pltpu.roll(ext, (-distance) % width, 1)
    return turned[:, LANES : width - LANES]


def relu_bf(values):
    return jnp.maximum(values, 0.0).astype(BF16)


def stack(rows, times):
    return jnp.concatenate([rows] * times, axis=0)


def net_kernel(
    len_src,
    wave_src,
    ids_src,
    weight_src,
    payload_ref,
    len_ref,
    wave_ref,
    ids_ref,
    weight_ref,
    load_sems,
    g_mix,
    g_point,
    g_edge,
    g_table,
    loss_ref,
    even_scr,
    odd_scr,
    code_scr,
    sig_r,
    msk_r,
    live_r,
    me_r,
    low_r,
    high_r,
    hi_r,
    strips_r,
    onehot_r,
    actu_e_r,
    chosen_r,
    actu_d_r,
    actp_e_r,
    encres_r,
    actp_d_r,
    resb_r,
    gapb_r,
    outs_r,
    douts_r,
    dbranch_d_r,
    dinner_d_r,
    dlatent_r,
    dbranch_e_r,
    dinner_e_r,
):
    pairs = (
        (len_src, len_ref), (wave_src, wave_ref), (ids_src, ids_ref), (weight_src, weight_ref)
    )
    loads = [
        pltpu.make_async_copy(source, place, load_sems.at[k])
        for k, (source, place) in enumerate(pairs)
    ]
    for load in loads:
        load.start()
    sets, per_clip = wave_ref.shape[:2]
    half = per_clip * LANES
    frames = 2 * half
    width = 64
    groups = 2 * (weight_ref.shape[1] - 4 * width - 16) // width
    table_rows = groups // 2 * width
    per_tile = TILE // LANES

    rings = (
        sig_r, msk_r, live_r, me_r, low_r, high_r, hi_r, strips_r, onehot_r, actu_e_r, chosen_r,
        actu_d_r, actp_e_r, encres_r, actp_d_r, resb_r, gapb_r, outs_r, douts_r, dbranch_d_r,
        dinner_d_r, dlatent_r, dbranch_e_r, dinner_e_r,
    )
    slots = SLOTS * per_tile

    @pl.loop(slots - (4 * LAG + 1 - HEAD * per_tile), slots)
    def _(slot):
        for ref in rings:
            ref[slot] = jnp.zeros(ref.shape[1:], ref.dtype)

    for ref in (g_mix, g_point, g_edge, g_table, loss_ref):
        ref[...] = jnp.zeros(ref.shape, ref.dtype)

    for load in loads:
        load.wait()

    def weight(part, start, rows, first, columns):
        start += table_rows
        return weight_ref[part, start : start + rows, first : first + columns]

    conv = [weight(part, 0, width, 0, 3 * width) for part in range(2)]
    conv_t = [weight(part, width, width, 0, 3 * width) for part in range(2)]
    point = [weight(k // 2, 2 * width, width, k % 2 * width, width) for k in range(4)]
    point_t = [weight(k // 2, 2 * width, width, (2 + k % 2) * width, width) for k in range(4)]
    edge = [weight(part, 3 * width, width, 0, 16) for part in range(2)]
    edge_t = [weight(part, 4 * width, 16, 0, width) for part in range(2)]

    def beside(*parts):
        return jnp.concatenate(parts, axis=1)

    same = lax.broadcasted_iota(jnp.int32, (width, width), 0) == lax.broadcasted_iota(
        jnp.int32, (width, width), 1
    )
    share = jnp.where(same, 2.0 * COMMIT, 0.0)
    share_bf = share.astype(BF16)
    share_rest = (share - share_bf.astype(F32)).astype(BF16)
    result_e = beside(point[0], edge[0])
    result_d = beside(point[3], point[2])
    back_d = beside(conv_t[1], edge[1])
    back_latent = beside(point_t[2], share_bf, share_rest)
    blank = jnp.zeros((width, width), BF16)
    finish = jnp.concatenate([beside(point[1], blank), beside(blank[:16], edge_t[1])], axis=0)
    back_e = beside(conv_t[0], point_t[1])

    for k in range(sets):
        for block in range(per_clip):
            rows = slice(8 * k, 8 * k + 8)
            parted = wave_ref[k, block].astype(F32)
            even_scr[block, rows] = parted[:8]
            odd_scr[block, rows] = parted[8:]
            code_scr[block, rows] = ids_ref[k, block]

    clips = 8 * sets

    def blocks_of(length):
        valid = lax.shift_right_arithmetic(length + 1, 1)
        return lax.shift_right_arithmetic(valid + (SPARE + LANES - 1), 7)

    def length_of(clip):
        return len_ref[jnp.bitwise_and(clip, 8), jnp.bitwise_and(clip, 7)]

    def add_clip(c, carry):
        length = length_of(c)
        return carry[0] + blocks_of(length), carry[1] + length

    blocks, count = lax.fori_loop(0, clips, add_clip, (jnp.int32(0), jnp.int32(0)))
    tiles = lax.div(blocks + per_tile - 1, jnp.int32(per_tile)) + DEPTH

    sub = lax.broadcasted_iota(jnp.int32, (8, LANES), 0)
    lane = lax.broadcasted_iota(jnp.int32, (8, LANES), 1)
    sub_ext = lax.broadcasted_iota(jnp.int32, (8, TILE + 2 * LANES), 0)
    sub_tile = lax.broadcasted_iota(jnp.int32, (8, TILE), 0)
    iota16 = lax.broadcasted_iota(jnp.int32, (16, TILE), 0).astype(F32).astype(BF16)

    table = jnp.concatenate([weight_ref[part, :table_rows] for part in range(2)], axis=0)

    def taps(ext):
        later = moved(ext, 1)
        earlier = moved(ext, -1)
        other = jnp.where(sub_tile == 0, later, jnp.where(sub_tile == 1, earlier, 0.0))
        return jnp.concatenate([moved(ext, 0), other], axis=0)

    def fetch(state, slot):
        clip, place = state
        real = clip < clips
        length = jnp.where(real, length_of(clip), -frames)
        row = pl.ds(jnp.minimum(clip, clips - 1), 1)
        here = (jnp.minimum(place, per_clip - 1), row, slice(None))
        t = place * LANES + lane
        even_ok = 2 * t < length
        odd_ok = 2 * t + 1 < length
        even = jnp.broadcast_to(even_scr[here], (8, LANES))
        odd = jnp.broadcast_to(odd_scr[here], (8, LANES))
        code = jnp.broadcast_to(code_scr[here], (8, LANES))
        live = t < jnp.minimum(lax.shift_right_arithmetic(length + 1, 1) + REAL, half)
        low = jnp.where(live, jnp.bitwise_and(code, LOW - 1), -1).astype(F32)
        high = lax.shift_right_logical(code, 8).astype(F32)
        sig_r[slot] = jnp.where(
            (sub == 0) & even_ok, even, jnp.where((sub == 1) & odd_ok, odd, 0.0)
        )
        msk_r[slot] = jnp.where(((sub == 0) & even_ok) | ((sub == 1) & odd_ok), 1.0, 0.0)
        live_r[slot] = jnp.where(live, 1.0, 0.0)
        me_r[slot] = jnp.where(even_ok, 1.0, 0.0)
        low_r[slot] = stack(low, 2).astype(BF16)
        high_r[slot] = high
        hi_r[slot] = stack(high, 2).astype(BF16)
        done = place + 1 >= blocks_of(length)
        clip = jnp.where(done, jnp.minimum(clip + 1, clips), clip)
        return clip, jnp.where(done, 0, place + 1)

    state = (jnp.int32(0), jnp.int32(0))
    for b in range(per_tile + 1):
        state = fetch(state, b)

    def tile_step(names, i, state):
        def block(lag, b):
            return jnp.bitwise_and(i * per_tile - lag + b, slots - 1)

        def load(ref, lag, first=0, last=per_tile):
            return jnp.concatenate([ref[block(lag, b)] for b in range(first, last)], axis=1)

        def load_ext(ref, lag):
            return load(ref, lag, -1, per_tile + 1)

        def keep(ref, lag, value):
            for b in range(per_tile):
                ref[block(lag, b)] = value[:, b * LANES : (b + 1) * LANES]

        def spread(ext, way):
            return jnp.concatenate([moved(ext, d * way) for d in (-REACH, 0, REACH)], axis=0)

        def strips_step():
            sig_ext, live = load_ext(sig_r, 0), load(live_r, 0)
            yield
            strips = (taps(sig_ext) * stack(live, 2)).astype(BF16)
            keep(strips_r, 0, strips)
            yield
            hidden = nn(edge[0], strips)
            yield
            keep(actu_e_r, 0, relu_bf(hidden))

        def lookup_step():
            low16, hi = load(low_r, 0) - iota16, load(high_r, 0)
            onehot = jnp.concatenate(
                [
                    jnp.where(low16 == float(16 * r), jnp.ones((), BF16), jnp.zeros((), BF16))
                    for r in range(LOW // 16)
                ],
                axis=0,
            )
            keep(onehot_r, 0, onehot)
            yield
            picked = nn(table, onehot)
            yield
            parts = [jnp.zeros((8, TILE), F32) for _ in range(width // 8)]
            for h in range(groups):
                here = hi == float(h)
                parts = [
                    jnp.where(here, picked[h * width + 8 * r : h * width + 8 * r + 8], parts[r])
                    for r in range(width // 8)
                ]
            chosen = jnp.concatenate(parts, axis=0).astype(BF16)
            keep(chosen_r, 0, chosen)
            yield
            decin = nn(point[2], chosen)
            yield
            keep(actu_d_r, 0, relu_bf(decin))

        def encode_step():
            lag = LAG
            around = spread(load_ext(actu_e_r, lag), 1)
            yield
            inner = nn(conv[0], around)
            yield
            actp, strips = relu_bf(inner), load(strips_r, lag)
            keep(actp_e_r, lag, actp)
            yield
            result = nn(result_e, jnp.concatenate([actp, strips], axis=0))
            yield
            encres = result.astype(BF16)
            keep(encres_r, lag, encres)
            yield
            latent = nn(point[1], encres)
            chosen, me = load(chosen_r, lag), load(me_r, lag)
            yield
            gap = (latent.astype(BF16).astype(F32) - chosen.astype(F32)) * stack(me, width // 8)
            keep(gapb_r, lag, gap.astype(BF16))
            yield
            square = gap * gap
            rows = square[:8]
            for r in range(1, width // 8):
                rows = rows + square[8 * r : 8 * r + 8]
            add_loss(COMMIT * rows)

        def decode_step():
            lag = LAG
            around = spread(load_ext(actu_d_r, lag), 1)
            yield
            inner = nn(conv[1], around)
            yield
            actp, chosen = relu_bf(inner), load(chosen_r, lag)
            keep(actp_d_r, lag, actp)
            yield
            result = nn(result_d, jnp.concatenate([actp, chosen], axis=0))
            yield
            resb = result.astype(BF16)
            keep(resb_r, lag, resb)
            yield
            outs = nn(edge_t[1], resb)
            yield
            keep(outs_r, lag, outs)

        def scatter_step():
            lag = LAG + per_tile
            hi, gap = load(hi_r, lag), load(gapb_r, lag)
            terms = []
            for h in range(groups):
                here = hi == float(h)
                terms += [
                    jnp.where(here, gap[16 * r : 16 * r + 16], jnp.zeros((), BF16))
                    for r in range(width // 16)
                ]
            onehot = load(onehot_r, lag)
            yield
            found = nt(jnp.concatenate(terms, axis=0), onehot)
            yield
            g_table[...] += found

        def add_loss(rows):
            total = rows[:, :LANES]
            for j in range(1, per_tile):
                total = total + rows[:, j * LANES : (j + 1) * LANES]
            loss_ref[...] += total

        def error_step():
            lag = 2 * LAG
            outs_ext, live_ext = load_ext(outs_r, lag), load_ext(live_r, lag)
            sig_ext, msk_ext = load_ext(sig_r, lag), load_ext(msk_r, lag)
            outs_ext = outs_ext * stack(live_ext, 2)
            shifted = outs_ext[8:]
            wide = TILE + 2 * LANES
            crossed = jnp.where(
                sub_ext == 0, pltpu.roll(shifted, 1, 1), pltpu.roll(shifted, wide - 1, 1)
            )
            error = (outs_ext[:8] + crossed - sig_ext) * msk_ext
            middle = moved(error, 0)
            add_loss(middle * middle)
            yield
            douts = (2.0 * taps(error) * stack(moved(live_ext, 0), 2)).astype(BF16)
            keep(douts_r, lag, douts)
            yield
            dres = nn(edge[1], douts)
            yield
            dbranch = dres.astype(BF16)
            keep(dbranch_d_r, lag, dbranch)
            yield
            dinner = nn(point_t[3], dbranch)
            actp = load(actp_d_r, lag)
            yield
            keep(dinner_d_r, lag, jnp.where(actp > 0, dinner.astype(BF16), 0))
            yield
            found = nt(dbranch, actp)
            yield
            g_point[1] += found
            yield
            found = nt(douts, load(resb_r, lag))
            yield
            g_edge[1] += found

        def middle_step():
            lag = 3 * LAG
            around, douts = spread(load_ext(dinner_d_r, lag), -1), load(douts_r, lag)
            yield
            both = nn(back_d, jnp.concatenate([around, douts], axis=0))
            actu, dbranch_d = load(actu_d_r, lag), load(dbranch_d_r, lag)
            yield
            ddecin = jnp.where(actu > 0, both.astype(BF16), dbranch_d)
            gap = load(gapb_r, lag)
            yield
            back = nn(back_latent, jnp.concatenate([ddecin, gap, gap], axis=0))
            yield
            dlatent = back.astype(BF16)
            keep(dlatent_r, lag, dlatent)
            yield
            denc = nn(point_t[1], dlatent)
            yield
            dbranch = denc.astype(BF16)
            keep(dbranch_e_r, lag, dbranch)
            actp = load(actp_e_r, lag)
            yield
            dinner = nn(point_t[0], dbranch)
            yield
            keep(dinner_e_r, lag, jnp.where(actp > 0, dinner.astype(BF16), 0))
            yield
            found = nt(
                jnp.concatenate([actu, load(chosen_r, lag)], axis=0),
                jnp.concatenate([around, ddecin], axis=0),
            )
            yield
            g_mix[1] += found
            yield
            found = nt(dbranch, actp)
            yield
            g_point[0] += found

        def last_step():
            lag = 4 * LAG
            around = spread(load_ext(dinner_e_r, lag), -1)
            dlatent = load(dlatent_r, lag)
            yield
            both = nn(back_e, jnp.concatenate([around, dlatent], axis=0))
            actu, dbranch = load(actu_e_r, lag), load(dbranch_e_r, lag)
            yield
            dhidden = jnp.where(actu > 0, both.astype(BF16), dbranch)
            yield
            found = nt(
                jnp.concatenate([actu, load(encres_r, lag)], axis=0),
                jnp.concatenate([around, dlatent], axis=0),
            )
            yield
            g_mix[0] += found
            yield
            found = nt(load(strips_r, lag), dhidden)
            yield
            g_edge[0] += found

        functions = (
            strips_step,
            lookup_step,
            encode_step,
            decode_step,
            scatter_step,
            error_step,
            middle_step,
            last_step,
        )
        steps = {k: functions[k]() for k in names}
        for k in ORDER:
            if k in steps:
                next(steps[k], None)
        for step in steps.values():
            for _ in step:
                pass
        if 0 in names:
            for b in range(per_tile):
                state = fetch(state, block(-LAG, b))
        return state

    ranges = (
        ((0, 1, 2, 3), 0, HEAD),
        (range(8), HEAD, tiles - 2),
        ((6, 7), tiles - 2, tiles - 1),
        ((7,), tiles - 1, tiles),
    )
    for names, begin, end in ranges:
        state = lax.fori_loop(begin, end, functools.partial(tile_step, names), state)

    loss_row = jnp.sum(loss_ref[...], axis=0, keepdims=True)
    count_row = jnp.where(lane == 0, count, 0).astype(F32)
    stats = jnp.where(
        jnp.bitwise_and(sub, 1) == 0, jnp.broadcast_to(loss_row, (8, LANES)), count_row
    )
    rows = groups // 2 * width
    for part in range(2):
        payload_ref[part, :rows] = g_table[part * rows : (part + 1) * rows, :LANES]
        payload_ref[part, rows : 2 * rows] = g_table[part * rows : (part + 1) * rows, LANES:]
        conv_rows = [g_mix[part, :width, k * width : (k + 1) * width].T for k in range(3)]
        mixed = g_mix[part, width:, 3 * width :].T
        edge_rows = jnp.concatenate(
            [g_edge[part], jnp.zeros((width - 16, width), F32)], axis=0
        )
        after = 2 * rows
        for pair in (
            conv_rows[:2],
            (conv_rows[2], edge_rows),
            (mixed, g_point[1]) if part else (g_point[0], mixed),
        ):
            payload_ref[part, after : after + width] = jnp.concatenate(pair, axis=1)
            after += width
        payload_ref[part, after : after + 8] = stats
        after += 8
        rest = payload_ref.shape[1] - after
        if rest:
            payload_ref[part, after:] = jnp.zeros((rest, LANES), F32)


def net(rows, lengths, wave, codes, weights):
    sets, per_clip = wave.shape[:2]
    clips = 8 * sets
    width = 64
    table_rows = 2 * (weights.shape[1] - 4 * width - 16)
    slots = SLOTS * TILE // LANES
    vmem = pl.BlockSpec(memory_space=pltpu.VMEM)

    def ring(rows, dtype):
        return pltpu.VMEM((slots, rows, LANES), dtype)

    return pl.pallas_call(
        net_kernel,
        out_shape=jax.ShapeDtypeStruct((2, rows, LANES), F32),
        in_specs=[pl.BlockSpec(memory_space=pl.ANY)] * 4,
        out_specs=vmem,
        scratch_shapes=[
            pltpu.SMEM(lengths.shape, lengths.dtype),
            pltpu.VMEM(wave.shape, wave.dtype),
            pltpu.VMEM(codes.shape, codes.dtype),
            pltpu.VMEM(weights.shape, weights.dtype),
            pltpu.SemaphoreType.DMA((4,)),
            pltpu.VMEM((2, 2 * width, 4 * width), F32),
            pltpu.VMEM((2, width, width), F32),
            pltpu.VMEM((2, 16, width), F32),
            pltpu.VMEM((table_rows, LOW), F32),
            pltpu.VMEM((8, LANES), F32),
            pltpu.VMEM((per_clip, clips, LANES), F32),
            pltpu.VMEM((per_clip, clips, LANES), F32),
            pltpu.VMEM((per_clip, clips, LANES), jnp.int32),
            *(ring(8, F32) for _ in range(4)),
            ring(16, BF16),
            ring(8, F32),
            *(ring(16, BF16) for _ in range(2)),
            ring(LOW, BF16),
            *(ring(width, BF16) for _ in range(8)),
            ring(16, F32),
            ring(16, BF16),
            *(ring(width, BF16) for _ in range(5)),
        ],
        compiler_params=pltpu.CompilerParams(vmem_limit_bytes=60 * 2**20),
    )(lengths, wave, codes, weights)


def remote(src, dst, send, recv, to):
    return pltpu.make_async_remote_copy(
        src_ref=src, dst_ref=dst, send_sem=send, recv_sem=recv, device_id=to, device_id_type=MESH
    )


def share_kernel(items, *refs):
    sources, (len_out, wave_out, ids_out, weight_out), inputs = refs[:7], refs[7:11], refs[11:18]
    len_ref, wave_ref, ids_ref, conv_ref, point_ref, edge_ref, table_ref = inputs
    len_scr, wave_scr, ids_scr, weight_scr, sems, load_sems = refs[18:]
    loads = [
        pltpu.make_async_copy(source, place, load_sems.at[k])
        for k, (source, place) in enumerate(zip(sources, inputs))
    ]
    for load in loads:
        load.start()
    item = lax.axis_index("item")
    pipe = lax.axis_index("pipe")
    partner = (item, 1 - pipe)
    mirror = (items - 1 - item, pipe)
    per_clip = wave_out.shape[1]
    width = conv_ref.shape[1]
    table_rows = weight_scr.shape[1] - 4 * width - 16

    barrier = pltpu.get_barrier_semaphore()
    for other in (partner, mirror):
        pl.semaphore_signal(barrier, inc=1, device_id=other, device_id_type=MESH)

    row_at = lax.broadcasted_iota(jnp.int32, (2 * LANES, 2 * LANES), 0)
    col_at = lax.broadcasted_iota(jnp.int32, (2 * LANES, 2 * LANES), 1)
    wanted = jnp.where(col_at < LANES, 2 * col_at, 2 * (col_at - LANES) + 1)
    split = jnp.where(row_at == wanted, 1.0, 0.0).astype(BF16)
    on_first = pipe == 0
    for load in loads[:3]:
        load.wait()
    lane = lax.broadcasted_iota(jnp.int32, (8, LANES), 1)
    kept = jnp.zeros((8, LANES), jnp.int32)
    given = kept
    for k in range(8):
        kept = jnp.where(lane == k, jnp.where(on_first, len_ref[k], len_ref[8 + k]), kept)
        given = jnp.where(lane == k, jnp.where(on_first, len_ref[24 + k], len_ref[16 + k]), given)
    len_out[:8] = kept
    len_scr[0] = given
    clips = wave_ref.shape[0]
    strips = [wave_ref[:, k * 2 * LANES : (k + 1) * 2 * LANES] for k in range(per_clip)]
    parted = nn(jnp.concatenate(strips, axis=0), split)

    def chosen(values, first, second):
        return jnp.where(on_first, values[8 * first :][:8], values[8 * second :][:8])

    def both(values, first, second):
        pair = [
            chosen(side, first, second) for side in (values[:, :LANES], values[:, LANES:])
        ]
        return jnp.concatenate(pair, axis=0).astype(BF16)

    codes = [ids_ref[:, k * LANES : (k + 1) * LANES] for k in range(per_clip)]
    for k in range(per_clip):
        values = parted[clips * k : clips * (k + 1)]
        wave_scr[0, k] = both(values, 3, 2)
        wave_out[0, k] = both(values, 0, 1)
        ids_out[0, k] = chosen(codes[k], 0, 1)
    for k in range(per_clip // 2):
        pair = [chosen(codes[2 * k + j], 3, 2) for j in range(2)]
        ids_scr[0, k] = jnp.concatenate(pair, axis=0).astype(jnp.int16)

    pl.semaphore_wait(barrier, 2)
    copies = [
        remote(ref.at[0], ref.at[1], sems.at[2 * k], sems.at[2 * k + 1], mirror)
        for k, ref in enumerate((len_scr, wave_scr, ids_scr))
    ]
    for copy in copies:
        copy.start()

    for load in loads[3:]:
        load.wait()
    groups = table_rows // width
    for h in range(groups):
        weight_scr[0, h * width : (h + 1) * width] = table_ref[:, h * LOW : (h + 1) * LOW].astype(
            BF16
        )
    blank = jnp.zeros((width, LOW - 3 * width), F32)
    conv = conv_ref[0]
    conv_t = [conv[:, k * width : (k + 1) * width].T for k in range(3)]
    points = [point_ref[0, 0], point_ref[0, 1]]
    edge = edge_ref[0]
    empty = jnp.zeros((6, width), F32)
    edge_t = jnp.concatenate([edge[1:3], empty, edge[3:], edge[:1], empty], axis=0)
    edge_square = jnp.concatenate([edge_t, jnp.zeros((width - 16, width), F32)], axis=0).T
    after = table_rows
    for pieces in (
        [conv, blank],
        conv_t + [blank],
        points + [value.T for value in points],
        [edge_square, jnp.zeros((width, LOW - width), F32)],
        [edge_t, jnp.zeros((16, LOW - width), F32)],
    ):
        value = jnp.concatenate(pieces, axis=1).astype(BF16)
        weight_scr[0, after : after + value.shape[0]] = value
        after += value.shape[0]
    over = remote(weight_scr.at[0], weight_scr.at[1], sems.at[6], sems.at[7], partner)
    over.start()
    weight_out[pipe] = weight_scr[0]
    over.wait()
    weight_out[1 - pipe] = weight_scr[1]
    for copy in copies:
        copy.wait()
    len_out[8:] = len_scr[1]
    wave_out[1] = wave_scr[1]
    for k in range(per_clip // 2):
        pair = ids_scr[1, k].astype(jnp.int32)
        ids_out[1, 2 * k], ids_out[1, 2 * k + 1] = pair[:8], pair[8:]


def shared(items, lengths, waveform, code_ids, conv, point, edge, table):
    per_clip = code_ids.shape[1] // LANES
    width = conv.shape[1]
    weight_rows = table.shape[1] // LOW * width + 4 * width + 16
    vmem = pl.BlockSpec(memory_space=pltpu.VMEM)
    wave_shape = (2, per_clip, 16, LANES)
    ids_shape = (2, per_clip, 8, LANES)
    weight_shape = (2, weight_rows, LOW)
    return pl.pallas_call(
        functools.partial(share_kernel, items),
        out_shape=(
            jax.ShapeDtypeStruct((16, LANES), jnp.int32),
            jax.ShapeDtypeStruct(wave_shape, BF16),
            jax.ShapeDtypeStruct(ids_shape, jnp.int32),
            jax.ShapeDtypeStruct(weight_shape, BF16),
        ),
        in_specs=[pl.BlockSpec(memory_space=pl.ANY)] * 7,
        out_specs=(vmem,) * 4,
        scratch_shapes=[pltpu.SMEM(lengths.shape, jnp.int32)]
        + [
            pltpu.VMEM(value.shape, value.dtype)
            for value in (waveform, code_ids, conv, point, edge, table)
        ]
        + [
            pltpu.VMEM((2, 8, LANES), jnp.int32),
            pltpu.VMEM(wave_shape, BF16),
            pltpu.VMEM((2, per_clip // 2, 16, LANES), jnp.int16),
            pltpu.VMEM(weight_shape, BF16),
            pltpu.SemaphoreType.DMA((8,)),
            pltpu.SemaphoreType.DMA((7,)),
        ],
        compiler_params=pltpu.CompilerParams(
            collective_id=0, has_side_effects=True, vmem_limit_bytes=60 * 2**20
        ),
    )(lengths, waveform, code_ids, conv, point, edge, table)


def sum_kernel(
    items,
    stats_row,
    payload_ref,
    sum_ref,
    own,
    crossed,
    part,
    landed,
    whole,
    own_sem,
    cross_send,
    cross_recv,
    out_send,
    out_recv,
    back_send,
    back_recv,
):
    item = lax.axis_index("item")
    pipe = lax.axis_index("pipe")
    partner = (item, 1 - pipe)
    piece = part.shape[1]

    def peer(d):
        if items & (items - 1):
            return lax.rem(item + d, items)
        return jnp.bitwise_and(item + d, items - 1)

    def rows_of(k):
        return pl.ds(pl.multiple_of(k * piece, piece), piece)

    load = pltpu.make_async_copy(payload_ref.at[pipe], own, own_sem)
    load.start()
    barrier = pltpu.get_barrier_semaphore()
    pl.semaphore_signal(barrier, inc=1, device_id=partner, device_id_type=MESH)

    @pl.loop(1, items)
    def _(d):
        pl.semaphore_signal(barrier, inc=1, device_id=(peer(d), pipe), device_id_type=MESH)

    pl.semaphore_wait(barrier, items)

    def cross_copy(k):
        return remote(
            payload_ref.at[1 - pipe, rows_of(k)], crossed.at[rows_of(k)],
            cross_send.at[k], cross_recv.at[k], partner,
        )

    @pl.loop(1, items + 1)
    def _(d):
        cross_copy(peer(d)).start()

    load.wait()

    def out_copy(to, place):
        return remote(
            part.at[to], landed.at[place], out_send.at[to], out_recv.at[place], (to, pipe)
        )

    @pl.loop(1, items)
    def _(d):
        to = peer(d)
        cross_copy(to).wait_recv()
        part[to] = (own[rows_of(to)] + crossed[rows_of(to)]).astype(BF16)
        out_copy(to, item).start()

    cross_copy(item).wait_recv()
    total = own[rows_of(item)] + crossed[rows_of(item)]
    stats = own[stats_row : stats_row + 8] + crossed[stats_row : stats_row + 8]
    high = stats.astype(BF16).astype(F32)
    middle = (stats - high).astype(BF16).astype(F32)
    low = stats - high - middle
    sub = lax.broadcasted_iota(jnp.int32, (8, LANES), 0)
    message = jnp.where(sub < 2, high, jnp.where(sub < 4, middle, jnp.where(sub < 6, low, 0.0)))
    whole[item, piece:] = jnp.concatenate([message, jnp.zeros_like(message)], axis=0).astype(BF16)

    def take(d, total):
        source = peer(items - d)
        out_copy(source, source).wait_recv()
        return total + landed[source].astype(F32)

    total = lax.fori_loop(1, items, take, total)
    whole[item, :piece] = total.astype(BF16)

    def back_copy(place, to):
        return remote(
            whole.at[place], whole.at[place], back_send.at[to], back_recv.at[place], (to, pipe)
        )

    @pl.loop(1, items)
    def _(d):
        back_copy(item, peer(d)).start()

    sum_ref[rows_of(item)] = whole[item, :piece].astype(F32)

    @pl.loop(1, items)
    def _(d):
        to = peer(d)
        cross_copy(to).wait_send()
        out_copy(to, item).wait_send()

    cross_copy(item).wait_send()

    def gather(d, stats):
        source = peer(items - d)
        back_copy(source, source).wait_recv()
        sum_ref[rows_of(source)] = whole[source, :piece].astype(F32)
        return stats + whole[source, piece:].astype(F32)[:8]

    stats = lax.fori_loop(1, items, gather, whole[item, piece:].astype(F32)[:8])
    sum_ref[stats_row : stats_row + 8] = stats

    @pl.loop(1, items)
    def _(d):
        back_copy(item, peer(d)).wait_send()


def summed(items, stats_row, payload):
    rows = payload.shape[1]
    piece = rows // items
    vmem = pl.BlockSpec(memory_space=pltpu.VMEM)
    sems = pltpu.SemaphoreType.DMA((items,))
    return pl.pallas_call(
        functools.partial(sum_kernel, items, stats_row),
        out_shape=jax.ShapeDtypeStruct((rows, LANES), F32),
        in_specs=[pl.BlockSpec(memory_space=pl.ANY)],
        out_specs=vmem,
        scratch_shapes=[
            pltpu.VMEM((rows, LANES), F32),
            pltpu.VMEM((rows, LANES), F32),
            pltpu.VMEM((items, piece, LANES), BF16),
            pltpu.VMEM((items, piece, LANES), BF16),
            pltpu.VMEM((items, piece + 16, LANES), BF16),
            pltpu.SemaphoreType.DMA,
        ]
        + [sems] * 6,
        compiler_params=pltpu.CompilerParams(
            collective_id=1, has_side_effects=True, vmem_limit_bytes=16 * 2**20
        ),
    )(payload)


def update_kernel(*refs):
    rate_net, rate_code, sum_ref = refs[:3]
    states = refs[3:15]
    loss_ref = refs[15]
    results = refs[16:]
    width = states[0].shape[1]
    groups = states[3].shape[1] // LOW
    rows = groups * width
    stats_row = 2 * rows + 3 * width
    stats = sum_ref[stats_row : stats_row + 8]
    odd = jnp.bitwise_and(lax.broadcasted_iota(jnp.int32, stats.shape, 0), 1) == 1
    counts = jnp.where(odd, stats, 0.0)
    loss_ref[0] = jnp.sum(jnp.where(odd, 0.0, stats)) / jnp.sum(counts)
    scale = 1.0 / jnp.sum(counts, keepdims=True)

    def step(kind, place, grad, rate):
        weight_ref, moment_ref, average_ref = (states[4 * j + kind] for j in range(3))
        new_ref, moment_new_ref, average_new_ref, copy_ref = results[4 * kind : 4 * kind + 4]
        grad = grad * scale
        moment = MOMENTUM * moment_ref[place] + grad
        weight = weight_ref[place] - rate * (grad + MOMENTUM * moment)
        new_ref[place] = weight
        moment_new_ref[place] = moment
        average_new_ref[place] = AVERAGE * average_ref[place] + (1.0 - AVERAGE) * weight
        copy_ref[place] = weight.astype(BF16)

    for h in range(groups):
        for side in range(LOW // LANES):
            start = h * LOW + side * LANES
            grad = sum_ref[side * rows + h * width : side * rows + (h + 1) * width]
            place = (slice(None), slice(start, start + LANES))
            step(3, place, grad * (-2.0 * COMMIT), rate_code[0])
    first, second, third = (
        sum_ref[2 * rows + k * width : 2 * rows + (k + 1) * width] for k in range(3)
    )
    rate = rate_net[0]
    step(0, 0, jnp.concatenate([first, second[:, :width]], axis=1), rate)
    step(1, (0, 0), third[:, :width], rate)
    step(1, (0, 1), third[:, width:], rate)
    edge = [second[k : k + 1, width:] for k in (9, 0, 1, 8)]
    step(2, 0, jnp.concatenate(edge, axis=0), rate)


def updated(rates, sums, states):
    smem = pl.BlockSpec(memory_space=pltpu.SMEM)
    shapes = [jax.ShapeDtypeStruct((1,), F32)]
    for weight in states[:4]:
        shapes += [jax.ShapeDtypeStruct(weight.shape, F32)] * 3
        shapes += [jax.ShapeDtypeStruct(weight.shape, BF16)]
    def block(value):
        return pl.BlockSpec(value.shape, lambda i: (0,) * len(value.shape))

    return pl.pallas_call(
        update_kernel,
        grid=(1,),
        out_shape=tuple(shapes),
        in_specs=[smem] * 2 + [block(value) for value in (sums, *states)],
        out_specs=(smem,) + tuple(block(value) for value in shapes[1:]),
        compiler_params=pltpu.CompilerParams(vmem_limit_bytes=24 * 2**20),
    )(*rates, sums, *states)


def per_device(
    waveform,
    lengths,
    code_ids,
    conv_w,
    point_w,
    edge_w,
    codebook,
    conv_mom,
    point_mom,
    edge_mom,
    code_mom,
    conv_avg,
    point_avg,
    edge_avg,
    code_avg,
    rate_net,
    rate_code,
):
    width = conv_w.shape[1]
    items = lax.axis_size("item")
    edge_w, edge_mom, edge_avg = (jnp.swapaxes(v, 1, 2) for v in (edge_w, edge_mom, edge_avg))
    codebook, code_mom, code_avg = (v.T for v in (codebook, code_mom, code_avg))
    rows = 2 * (codebook.shape[1] // LOW) * width + 3 * width
    piece = -(-(rows + 8) // (16 * items)) * 16
    own_inputs = shared(items, lengths, waveform, code_ids, conv_w, point_w, edge_w, codebook)
    payload = net(piece * items, *own_inputs)
    sums = summed(items, rows, payload)
    states = (
        conv_w, point_w, edge_w, codebook,
        conv_mom, point_mom, edge_mom, code_mom,
        conv_avg, point_avg, edge_avg, code_avg,
    )
    loss, *rest = updated((rate_net, rate_code), sums, states)
    edges = (jnp.swapaxes(v, 1, 2) for v in rest[8:12])
    return (loss.reshape(()), *rest[:8], *edges, *(v.T for v in rest[12:]))


def solution(mesh):
    weights = (
        P("pipe", None, None),
        P("pipe", None, None, None),
        P("pipe", None, None),
        P("pipe", None),
    )
    return jax.shard_map(
        per_device,
        mesh=mesh,
        in_specs=(P("item", None), P("item"), P("item", None), *weights, *weights, *weights, P(), P()),
        out_specs=(P(),) + tuple(spec for spec in weights for _ in range(4)),
        check_vma=False,
    )
```

```python
import functools

import jax
import jax.numpy as jnp
from jax import lax
from jax.experimental import pallas as pl
from jax.experimental.pallas import tpu as pltpu
from jax.sharding import PartitionSpec as P

REACH = 3
COMMIT = 0.02
MOMENTUM = 0.9
AVERAGE = 0.99

LANES = 128
TILE = 512
SLOTS = 8
LAG = TILE // LANES + 1
HEAD = 2
DEPTH = -(-4 * LAG * LANES // TILE)
LOW = 256
SPARE = 8
REAL = 4

MESH = pl.DeviceIdType.MESH
ORDER = (1, 6, 3, 2, 4, 7, 5, 0, 1, 6, 3, 2, 4, 7, 5, 0, 1, 6, 3, 2, 4, 7, 5, 0, 1, 6, 3, 2, 7, 5, 0, 1, 6, 3, 2, 7, 5, 6, 2, 7, 5, 6, 7, 6, 6)
F32 = jnp.float32
BF16 = jnp.bfloat16


def nn(a, b):
    return lax.dot_general(a, b, (((1,), (0,)), ((), ())), preferred_element_type=F32)


def nt(a, b):
    return lax.dot_general(a, b, (((1,), (1,)), ((), ())), preferred_element_type=F32)


def moved(ext, distance):
    width = ext.shape[1]
    turned = ext if distance == 0 else pltpu.roll(ext, (-distance) % width, 1)
    return turned[:, LANES : width - LANES]


def relu_bf(values):
    return jnp.maximum(values, 0.0).astype(BF16)


def stack(rows, times):
    return jnp.concatenate([rows] * times, axis=0)


def net_kernel(
    len_src,
    wave_src,
    ids_src,
    weight_src,
    payload_ref,
    len_ref,
    wave_ref,
    ids_ref,
    weight_ref,
    load_sems,
    g_mix,
    g_outs,
    g_edge,
    g_table,
    loss_ref,
    even_scr,
    odd_scr,
    code_scr,
    sig_r,
    msk_r,
    live_r,
    me_r,
    low_r,
    high_r,
    hi_r,
    strips_r,
    onehot_r,
    actu_e_r,
    chosen_r,
    actu_d_r,
    actp_e_r,
    actp_d_r,
    gapb_r,
    outs_r,
    douts_r,
    dinner_d_r,
    dlatent_r,
    dinner_e_r,
):
    pairs = (
        (len_src, len_ref), (wave_src, wave_ref), (ids_src, ids_ref), (weight_src, weight_ref)
    )
    loads = [
        pltpu.make_async_copy(source, place, load_sems.at[k])
        for k, (source, place) in enumerate(pairs)
    ]
    for load in loads:
        load.start()
    sets, per_clip = wave_ref.shape[:2]
    half = per_clip * LANES
    frames = 2 * half
    width = 64
    groups = 2 * (weight_ref.shape[1] - 4 * width - 16) // width
    table_rows = groups // 2 * width
    per_tile = TILE // LANES

    rings = (
        sig_r, msk_r, live_r, me_r, low_r, high_r, hi_r, strips_r, onehot_r, actu_e_r, chosen_r,
        actu_d_r, actp_e_r, actp_d_r, gapb_r, outs_r, douts_r, dinner_d_r, dlatent_r, dinner_e_r,
    )
    slots = SLOTS * per_tile

    @pl.loop(slots - (4 * LAG + 1 - HEAD * per_tile), slots)
    def _(slot):
        for ref in rings:
            ref[slot] = jnp.zeros(ref.shape[1:], ref.dtype)

    for ref in (g_mix, g_outs, g_edge, g_table, loss_ref):
        ref[...] = jnp.zeros(ref.shape, ref.dtype)

    for load in loads:
        load.wait()

    def weight(part, start, rows, first, columns):
        start += table_rows
        return weight_ref[part, start : start + rows, first : first + columns]

    conv = [weight(part, 0, width, 0, 3 * width) for part in range(2)]
    conv_t = [weight(part, width, width, 0, 3 * width) for part in range(2)]
    point = [weight(k // 2, 2 * width, width, k % 2 * width, width) for k in range(4)]
    point_t = [weight(k // 2, 2 * width, width, (2 + k % 2) * width, width) for k in range(4)]
    edge = [weight(part, 3 * width, width, 0, 16) for part in range(2)]
    edge_t = [weight(part, 4 * width, 16, 0, width) for part in range(2)]

    def beside(*parts):
        return jnp.concatenate(parts, axis=1)

    same = lax.broadcasted_iota(jnp.int32, (width, width), 0) == lax.broadcasted_iota(
        jnp.int32, (width, width), 1
    )
    same_bf = jnp.where(same, 1.0, 0.0).astype(BF16)

    def halves(value):
        high = value.astype(BF16)
        return high, (value - high.astype(F32)).astype(BF16)

    latent_w = beside(*halves(nn(point[1], point[0])), *halves(nn(point[1], edge[0])))
    outs_w = jnp.concatenate(halves(nn(edge_t[1], beside(point[3], point[2]))), axis=0)
    inner_d_w = beside(*halves(nn(point_t[3], edge[1])))
    inner_e_w = beside(*halves(nn(point_t[0], point_t[1])))
    back_d = beside(conv_t[1], edge[1])
    back_latent = beside(point_t[2], same_bf)
    back_e = beside(conv_t[0], point_t[1])

    for k in range(sets):
        for block in range(per_clip):
            rows = slice(8 * k, 8 * k + 8)
            parted = wave_ref[k, block].astype(F32)
            even_scr[block, rows] = parted[:8]
            odd_scr[block, rows] = parted[8:]
            code_scr[block, rows] = ids_ref[k, block]

    clips = 8 * sets

    def blocks_of(length):
        valid = lax.shift_right_arithmetic(length + 1, 1)
        return lax.shift_right_arithmetic(valid + (SPARE + LANES - 1), 7)

    def length_of(clip):
        return len_ref[jnp.bitwise_and(clip, 8), jnp.bitwise_and(clip, 7)]

    def add_clip(c, carry):
        length = length_of(c)
        return carry[0] + blocks_of(length), carry[1] + length

    blocks, count = lax.fori_loop(0, clips, add_clip, (jnp.int32(0), jnp.int32(0)))
    tiles = lax.div(blocks + per_tile - 1, jnp.int32(per_tile)) + DEPTH

    sub = lax.broadcasted_iota(jnp.int32, (8, LANES), 0)
    lane = lax.broadcasted_iota(jnp.int32, (8, LANES), 1)
    sub_ext = lax.broadcasted_iota(jnp.int32, (8, TILE + 2 * LANES), 0)
    sub_tile = lax.broadcasted_iota(jnp.int32, (8, TILE), 0)
    iota16 = lax.broadcasted_iota(jnp.int32, (16, TILE), 0).astype(F32).astype(BF16)

    table = jnp.concatenate([weight_ref[part, :table_rows] for part in range(2)], axis=0)

    def taps(ext):
        later = moved(ext, 1)
        earlier = moved(ext, -1)
        other = jnp.where(sub_tile == 0, later, jnp.where(sub_tile == 1, earlier, 0.0))
        return jnp.concatenate([moved(ext, 0), other], axis=0)

    def fetch(state, slot):
        clip, place = state
        real = clip < clips
        length = jnp.where(real, length_of(clip), -frames)
        row = pl.ds(jnp.minimum(clip, clips - 1), 1)
        here = (jnp.minimum(place, per_clip - 1), row, slice(None))
        t = place * LANES + lane
        even_ok = 2 * t < length
        odd_ok = 2 * t + 1 < length
        even = jnp.broadcast_to(even_scr[here], (8, LANES))
        odd = jnp.broadcast_to(odd_scr[here], (8, LANES))
        code = jnp.broadcast_to(code_scr[here], (8, LANES))
        live = t < jnp.minimum(lax.shift_right_arithmetic(length + 1, 1) + REAL, half)
        low = jnp.where(live, jnp.bitwise_and(code, LOW - 1), -1).astype(F32)
        high = lax.shift_right_logical(code, 8).astype(F32)
        sig_r[slot] = jnp.where(
            (sub == 0) & even_ok, even, jnp.where((sub == 1) & odd_ok, odd, 0.0)
        )
        msk_r[slot] = jnp.where(((sub == 0) & even_ok) | ((sub == 1) & odd_ok), 1.0, 0.0)
        live_r[slot] = jnp.where(live, 1.0, 0.0)
        me_r[slot] = jnp.where(even_ok, 1.0, 0.0)
        low_r[slot] = stack(low, 2).astype(BF16)
        high_r[slot] = high
        hi_r[slot] = stack(high, 2).astype(BF16)
        done = place + 1 >= blocks_of(length)
        clip = jnp.where(done, jnp.minimum(clip + 1, clips), clip)
        return clip, jnp.where(done, 0, place + 1)

    state = (jnp.int32(0), jnp.int32(0))
    for b in range(per_tile + 1):
        state = fetch(state, b)

    def tile_step(names, i, state):
        def block(lag, b):
            return jnp.bitwise_and(i * per_tile - lag + b, slots - 1)

        def load(ref, lag, first=0, last=per_tile):
            return jnp.concatenate([ref[block(lag, b)] for b in range(first, last)], axis=1)

        def load_ext(ref, lag):
            return load(ref, lag, -1, per_tile + 1)

        def keep(ref, lag, value):
            for b in range(per_tile):
                ref[block(lag, b)] = value[:, b * LANES : (b + 1) * LANES]

        def spread(ext, way):
            return jnp.concatenate([moved(ext, d * way) for d in (-REACH, 0, REACH)], axis=0)

        def strips_step():
            sig_ext, live = load_ext(sig_r, 0), load(live_r, 0)
            yield
            strips = (taps(sig_ext) * stack(live, 2)).astype(BF16)
            keep(strips_r, 0, strips)
            yield
            hidden = nn(edge[0], strips)
            yield
            keep(actu_e_r, 0, relu_bf(hidden))

        def lookup_step():
            low16, hi = load(low_r, 0) - iota16, load(high_r, 0)
            onehot = jnp.concatenate(
                [
                    jnp.where(low16 == float(16 * r), jnp.ones((), BF16), jnp.zeros((), BF16))
                    for r in range(LOW // 16)
                ],
                axis=0,
            )
            keep(onehot_r, 0, onehot)
            yield
            picked = nn(table, onehot)
            yield
            parts = [jnp.zeros((8, TILE), F32) for _ in range(width // 8)]
            for h in range(groups):
                here = hi == float(h)
                parts = [
                    jnp.where(here, picked[h * width + 8 * r : h * width + 8 * r + 8], parts[r])
                    for r in range(width // 8)
                ]
            chosen = jnp.concatenate(parts, axis=0).astype(BF16)
            keep(chosen_r, 0, chosen)
            yield
            decin = nn(point[2], chosen)
            yield
            keep(actu_d_r, 0, relu_bf(decin))

        def encode_step():
            lag = LAG
            around = spread(load_ext(actu_e_r, lag), 1)
            yield
            inner = nn(conv[0], around)
            yield
            actp, strips = relu_bf(inner), load(strips_r, lag)
            keep(actp_e_r, lag, actp)
            yield
            latent = nn(latent_w, jnp.concatenate([actp, actp, strips, strips], axis=0))
            chosen, me = load(chosen_r, lag), load(me_r, lag)
            yield
            gap = (latent.astype(BF16).astype(F32) - chosen.astype(F32)) * stack(me, width // 8)
            keep(gapb_r, lag, (gap * (2.0 * COMMIT)).astype(BF16))
            yield
            square = gap * gap
            rows = square[:8]
            for r in range(1, width // 8):
                rows = rows + square[8 * r : 8 * r + 8]
            add_loss(COMMIT * rows)

        def decode_step():
            lag = LAG
            around = spread(load_ext(actu_d_r, lag), 1)
            yield
            inner = nn(conv[1], around)
            yield
            actp, chosen = relu_bf(inner), load(chosen_r, lag)
            keep(actp_d_r, lag, actp)
            yield
            outs = nn(outs_w, jnp.concatenate([actp, chosen], axis=0))
            yield
            keep(outs_r, lag, outs[:16] + outs[16:])

        def scatter_step():
            lag = LAG + per_tile
            hi, gap = load(hi_r, lag), load(gapb_r, lag)
            terms = []
            for h in range(groups):
                here = hi == float(h)
                terms += [
                    jnp.where(here, gap[16 * r : 16 * r + 16], jnp.zeros((), BF16))
                    for r in range(width // 16)
                ]
            onehot = load(onehot_r, lag)
            yield
            found = nt(jnp.concatenate(terms, axis=0), onehot)
            yield
            g_table[...] += found

        def add_loss(rows):
            total = rows[:, :LANES]
            for j in range(1, per_tile):
                total = total + rows[:, j * LANES : (j + 1) * LANES]
            loss_ref[...] += total

        def error_step():
            lag = 2 * LAG
            outs_ext, live_ext = load_ext(outs_r, lag), load_ext(live_r, lag)
            sig_ext, msk_ext = load_ext(sig_r, lag), load_ext(msk_r, lag)
            outs_ext = outs_ext * stack(live_ext, 2)
            shifted = outs_ext[8:]
            wide = TILE + 2 * LANES
            crossed = jnp.where(
                sub_ext == 0, pltpu.roll(shifted, 1, 1), pltpu.roll(shifted, wide - 1, 1)
            )
            error = (outs_ext[:8] + crossed - sig_ext) * msk_ext
            middle = moved(error, 0)
            add_loss(middle * middle)
            yield
            douts = (2.0 * taps(error) * stack(moved(live_ext, 0), 2)).astype(BF16)
            keep(douts_r, lag, douts)
            yield
            dinner = nn(inner_d_w, jnp.concatenate([douts, douts], axis=0))
            actp = load(actp_d_r, lag)
            yield
            keep(dinner_d_r, lag, jnp.where(actp > 0, dinner.astype(BF16), 0))
            yield
            found = nt(jnp.concatenate([actp, load(chosen_r, lag)], axis=0), douts)
            yield
            g_outs[...] += found

        def middle_step():
            lag = 3 * LAG
            around, douts = spread(load_ext(dinner_d_r, lag), -1), load(douts_r, lag)
            yield
            both = nn(back_d, jnp.concatenate([around, douts], axis=0))
            dres = nn(edge[1], douts)
            actu = load(actu_d_r, lag)
            yield
            ddecin = jnp.where(actu > 0, both.astype(BF16), dres.astype(BF16))
            gap = load(gapb_r, lag)
            yield
            back = nn(back_latent, jnp.concatenate([ddecin, gap], axis=0))
            yield
            dlatent = back.astype(BF16)
            keep(dlatent_r, lag, dlatent)
            yield
            dinner = nn(inner_e_w, jnp.concatenate([dlatent, dlatent], axis=0))
            actp = load(actp_e_r, lag)
            yield
            keep(dinner_e_r, lag, jnp.where(actp > 0, dinner.astype(BF16), 0))
            yield
            found = nt(
                jnp.concatenate([actu, load(chosen_r, lag)], axis=0),
                jnp.concatenate([around, ddecin], axis=0),
            )
            yield
            g_mix[1, :width] += found[:width]
            g_mix[1, width : 2 * width, LANES:] += found[width:, LANES:]

        def last_step():
            lag = 4 * LAG
            around = spread(load_ext(dinner_e_r, lag), -1)
            dlatent = load(dlatent_r, lag)
            yield
            both = nn(back_e, jnp.concatenate([around, dlatent], axis=0))
            denc = nn(point_t[1], dlatent)
            actu = load(actu_e_r, lag)
            yield
            dhidden = jnp.where(actu > 0, both.astype(BF16), denc.astype(BF16))
            strips = load(strips_r, lag)
            yield
            found = nt(
                jnp.concatenate([actu, load(actp_e_r, lag), strips], axis=0),
                jnp.concatenate([around, dlatent], axis=0),
            )
            yield
            g_mix[0, :width] += found[:width]
            g_mix[0, width:, LANES:] += found[width:, LANES:]
            yield
            found = nt(dhidden, strips)
            yield
            g_edge[...] += found

        functions = (
            strips_step,
            lookup_step,
            encode_step,
            decode_step,
            scatter_step,
            error_step,
            middle_step,
            last_step,
        )
        steps = {k: functions[k]() for k in names}
        for k in ORDER:
            if k in steps:
                next(steps[k], None)
        for step in steps.values():
            for _ in step:
                pass
        if 0 in names:
            for b in range(per_tile):
                state = fetch(state, block(-LAG, b))
        return state

    ranges = (
        ((0, 1, 2, 3), 0, HEAD),
        (range(8), HEAD, tiles - 2),
        ((6, 7), tiles - 2, tiles - 1),
        ((7,), tiles - 1, tiles),
    )
    for names, begin, end in ranges:
        state = lax.fori_loop(begin, end, functools.partial(tile_step, names), state)

    loss_row = jnp.sum(loss_ref[...], axis=0, keepdims=True)
    count_row = jnp.where(lane == 0, count, 0).astype(F32)
    stats = jnp.where(
        jnp.bitwise_and(sub, 1) == 0, jnp.broadcast_to(loss_row, (8, LANES)), count_row
    )
    def exact(a, b, axis):
        return lax.dot_general(
            a.astype(F32),
            b.astype(F32),
            (((1,), (axis,)), ((), ())),
            preferred_element_type=F32,
            precision=lax.Precision.HIGHEST,
        )

    by_latent = g_mix[0, width : 2 * width, 3 * width :].T
    by_strips = g_mix[0, 2 * width :, 3 * width :].T
    by_inner, by_chosen = g_outs[:width].T, g_outs[width:].T
    points = (
        (
            exact(point_t[1], by_latent, 0),
            exact(by_latent, point[0], 1) + exact(by_strips, edge[0], 1),
        ),
        (g_mix[1, width : 2 * width, 3 * width :].T, exact(edge[1], by_inner, 0)),
    )
    edges = (g_edge[...].T, exact(by_inner, point[3], 1) + exact(by_chosen, point[2], 1))
    rows = groups // 2 * width
    for part in range(2):
        payload_ref[part, :rows] = g_table[part * rows : (part + 1) * rows, :LANES]
        payload_ref[part, rows : 2 * rows] = g_table[part * rows : (part + 1) * rows, LANES:]
        conv_rows = [g_mix[part, :width, k * width : (k + 1) * width].T for k in range(3)]
        edge_rows = jnp.concatenate([edges[part], jnp.zeros((width - 16, width), F32)], axis=0)
        after = 2 * rows
        for pair in (
            conv_rows[:2],
            (conv_rows[2], edge_rows),
            points[part],
        ):
            payload_ref[part, after : after + width] = jnp.concatenate(pair, axis=1)
            after += width
        payload_ref[part, after : after + 8] = stats
        after += 8
        rest = payload_ref.shape[1] - after
        if rest:
            payload_ref[part, after:] = jnp.zeros((rest, LANES), F32)


def net(rows, lengths, wave, codes, weights):
    sets, per_clip = wave.shape[:2]
    clips = 8 * sets
    width = 64
    table_rows = 2 * (weights.shape[1] - 4 * width - 16)
    slots = SLOTS * TILE // LANES
    vmem = pl.BlockSpec(memory_space=pltpu.VMEM)

    def ring(rows, dtype):
        return pltpu.VMEM((slots, rows, LANES), dtype)

    return pl.pallas_call(
        net_kernel,
        out_shape=jax.ShapeDtypeStruct((2, rows, LANES), F32),
        in_specs=[pl.BlockSpec(memory_space=pl.ANY)] * 4,
        out_specs=vmem,
        scratch_shapes=[
            pltpu.SMEM(lengths.shape, lengths.dtype),
            pltpu.VMEM(wave.shape, wave.dtype),
            pltpu.VMEM(codes.shape, codes.dtype),
            pltpu.VMEM(weights.shape, weights.dtype),
            pltpu.SemaphoreType.DMA((4,)),
            pltpu.VMEM((2, 2 * width + 16, 4 * width), F32),
            pltpu.VMEM((2 * width, 16), F32),
            pltpu.VMEM((width, 16), F32),
            pltpu.VMEM((table_rows, LOW), F32),
            pltpu.VMEM((8, LANES), F32),
            pltpu.VMEM((per_clip, clips, LANES), F32),
            pltpu.VMEM((per_clip, clips, LANES), F32),
            pltpu.VMEM((per_clip, clips, LANES), jnp.int32),
            *(ring(8, F32) for _ in range(4)),
            ring(16, BF16),
            ring(8, F32),
            *(ring(16, BF16) for _ in range(2)),
            ring(LOW, BF16),
            *(ring(width, BF16) for _ in range(6)),
            ring(16, F32),
            ring(16, BF16),
            *(ring(width, BF16) for _ in range(3)),
        ],
        compiler_params=pltpu.CompilerParams(vmem_limit_bytes=60 * 2**20),
    )(lengths, wave, codes, weights)


def remote(src, dst, send, recv, to):
    return pltpu.make_async_remote_copy(
        src_ref=src, dst_ref=dst, send_sem=send, recv_sem=recv, device_id=to, device_id_type=MESH
    )


def share_kernel(items, *refs):
    sources, (len_out, wave_out, ids_out, weight_out), inputs = refs[:7], refs[7:11], refs[11:18]
    len_ref, wave_ref, ids_ref, conv_ref, point_ref, edge_ref, table_ref = inputs
    len_scr, wave_scr, ids_scr, weight_scr, sems, load_sems = refs[18:]
    loads = [
        pltpu.make_async_copy(source, place, load_sems.at[k])
        for k, (source, place) in enumerate(zip(sources, inputs))
    ]
    for load in loads:
        load.start()
    item = lax.axis_index("item")
    pipe = lax.axis_index("pipe")
    partner = (item, 1 - pipe)
    mirror = (items - 1 - item, pipe)
    per_clip = wave_out.shape[1]
    width = conv_ref.shape[1]
    table_rows = weight_scr.shape[1] - 4 * width - 16

    barrier = pltpu.get_barrier_semaphore()
    for other in (partner, mirror):
        pl.semaphore_signal(barrier, inc=1, device_id=other, device_id_type=MESH)

    row_at = lax.broadcasted_iota(jnp.int32, (2 * LANES, 2 * LANES), 0)
    col_at = lax.broadcasted_iota(jnp.int32, (2 * LANES, 2 * LANES), 1)
    wanted = jnp.where(col_at < LANES, 2 * col_at, 2 * (col_at - LANES) + 1)
    split = jnp.where(row_at == wanted, 1.0, 0.0).astype(BF16)
    on_first = pipe == 0
    for load in loads[:3]:
        load.wait()
    lane = lax.broadcasted_iota(jnp.int32, (8, LANES), 1)
    kept = jnp.zeros((8, LANES), jnp.int32)
    given = kept
    for k in range(8):
        kept = jnp.where(lane == k, jnp.where(on_first, len_ref[k], len_ref[8 + k]), kept)
        given = jnp.where(lane == k, jnp.where(on_first, len_ref[24 + k], len_ref[16 + k]), given)
    len_out[:8] = kept
    len_scr[0] = given
    clips = wave_ref.shape[0]
    strips = [wave_ref[:, k * 2 * LANES : (k + 1) * 2 * LANES] for k in range(per_clip)]
    parted = nn(jnp.concatenate(strips, axis=0), split)

    def chosen(values, first, second):
        return jnp.where(on_first, values[8 * first :][:8], values[8 * second :][:8])

    def both(values, first, second):
        pair = [
            chosen(side, first, second) for side in (values[:, :LANES], values[:, LANES:])
        ]
        return jnp.concatenate(pair, axis=0).astype(BF16)

    codes = [ids_ref[:, k * LANES : (k + 1) * LANES] for k in range(per_clip)]
    for k in range(per_clip):
        values = parted[clips * k : clips * (k + 1)]
        wave_scr[0, k] = both(values, 3, 2)
        wave_out[0, k] = both(values, 0, 1)
        ids_out[0, k] = chosen(codes[k], 0, 1)
    for k in range(per_clip // 2):
        pair = [chosen(codes[2 * k + j], 3, 2) for j in range(2)]
        ids_scr[0, k] = jnp.concatenate(pair, axis=0).astype(jnp.int16)

    pl.semaphore_wait(barrier, 2)
    copies = [
        remote(ref.at[0], ref.at[1], sems.at[2 * k], sems.at[2 * k + 1], mirror)
        for k, ref in enumerate((len_scr, wave_scr, ids_scr))
    ]
    for copy in copies:
        copy.start()

    for load in loads[3:]:
        load.wait()
    groups = table_rows // width
    for h in range(groups):
        weight_scr[0, h * width : (h + 1) * width] = table_ref[:, h * LOW : (h + 1) * LOW].astype(
            BF16
        )
    blank = jnp.zeros((width, LOW - 3 * width), F32)
    conv = conv_ref[0]
    conv_t = [conv[:, k * width : (k + 1) * width].T for k in range(3)]
    points = [point_ref[0, 0], point_ref[0, 1]]
    edge = edge_ref[0]
    empty = jnp.zeros((6, width), F32)
    edge_t = jnp.concatenate([edge[1:3], empty, edge[3:], edge[:1], empty], axis=0)
    edge_square = jnp.concatenate([edge_t, jnp.zeros((width - 16, width), F32)], axis=0).T
    after = table_rows
    for pieces in (
        [conv, blank],
        conv_t + [blank],
        points + [value.T for value in points],
        [edge_square, jnp.zeros((width, LOW - width), F32)],
        [edge_t, jnp.zeros((16, LOW - width), F32)],
    ):
        value = jnp.concatenate(pieces, axis=1).astype(BF16)
        weight_scr[0, after : after + value.shape[0]] = value
        after += value.shape[0]
    over = remote(weight_scr.at[0], weight_scr.at[1], sems.at[6], sems.at[7], partner)
    over.start()
    weight_out[pipe] = weight_scr[0]
    over.wait()
    weight_out[1 - pipe] = weight_scr[1]
    for copy in copies:
        copy.wait()
    len_out[8:] = len_scr[1]
    wave_out[1] = wave_scr[1]
    for k in range(per_clip // 2):
        pair = ids_scr[1, k].astype(jnp.int32)
        ids_out[1, 2 * k], ids_out[1, 2 * k + 1] = pair[:8], pair[8:]


def shared(items, lengths, waveform, code_ids, conv, point, edge, table):
    per_clip = code_ids.shape[1] // LANES
    width = conv.shape[1]
    weight_rows = table.shape[1] // LOW * width + 4 * width + 16
    vmem = pl.BlockSpec(memory_space=pltpu.VMEM)
    wave_shape = (2, per_clip, 16, LANES)
    ids_shape = (2, per_clip, 8, LANES)
    weight_shape = (2, weight_rows, LOW)
    return pl.pallas_call(
        functools.partial(share_kernel, items),
        out_shape=(
            jax.ShapeDtypeStruct((16, LANES), jnp.int32),
            jax.ShapeDtypeStruct(wave_shape, BF16),
            jax.ShapeDtypeStruct(ids_shape, jnp.int32),
            jax.ShapeDtypeStruct(weight_shape, BF16),
        ),
        in_specs=[pl.BlockSpec(memory_space=pl.ANY)] * 7,
        out_specs=(vmem,) * 4,
        scratch_shapes=[pltpu.SMEM(lengths.shape, jnp.int32)]
        + [
            pltpu.VMEM(value.shape, value.dtype)
            for value in (waveform, code_ids, conv, point, edge, table)
        ]
        + [
            pltpu.VMEM((2, 8, LANES), jnp.int32),
            pltpu.VMEM(wave_shape, BF16),
            pltpu.VMEM((2, per_clip // 2, 16, LANES), jnp.int16),
            pltpu.VMEM(weight_shape, BF16),
            pltpu.SemaphoreType.DMA((8,)),
            pltpu.SemaphoreType.DMA((7,)),
        ],
        compiler_params=pltpu.CompilerParams(
            collective_id=0, has_side_effects=True, vmem_limit_bytes=60 * 2**20
        ),
    )(lengths, waveform, code_ids, conv, point, edge, table)


def sum_kernel(
    items,
    stats_row,
    payload_ref,
    sum_ref,
    own,
    crossed,
    part,
    landed,
    whole,
    own_sem,
    cross_send,
    cross_recv,
    out_send,
    out_recv,
    back_send,
    back_recv,
):
    item = lax.axis_index("item")
    pipe = lax.axis_index("pipe")
    partner = (item, 1 - pipe)
    piece = part.shape[1]

    def peer(d):
        if items & (items - 1):
            return lax.rem(item + d, items)
        return jnp.bitwise_and(item + d, items - 1)

    def rows_of(k):
        return pl.ds(pl.multiple_of(k * piece, piece), piece)

    load = pltpu.make_async_copy(payload_ref.at[pipe], own, own_sem)
    load.start()
    barrier = pltpu.get_barrier_semaphore()
    pl.semaphore_signal(barrier, inc=1, device_id=partner, device_id_type=MESH)

    @pl.loop(1, items)
    def _(d):
        pl.semaphore_signal(barrier, inc=1, device_id=(peer(d), pipe), device_id_type=MESH)

    pl.semaphore_wait(barrier, items)

    def cross_copy(k):
        return remote(
            payload_ref.at[1 - pipe, rows_of(k)], crossed.at[rows_of(k)],
            cross_send.at[k], cross_recv.at[k], partner,
        )

    @pl.loop(1, items + 1)
    def _(d):
        cross_copy(peer(d)).start()

    load.wait()

    def out_copy(to, place):
        return remote(
            part.at[to], landed.at[place], out_send.at[to], out_recv.at[place], (to, pipe)
        )

    @pl.loop(1, items)
    def _(d):
        to = peer(d)
        cross_copy(to).wait_recv()
        part[to] = (own[rows_of(to)] + crossed[rows_of(to)]).astype(BF16)
        out_copy(to, item).start()

    cross_copy(item).wait_recv()
    total = own[rows_of(item)] + crossed[rows_of(item)]
    stats = own[stats_row : stats_row + 8] + crossed[stats_row : stats_row + 8]
    high = stats.astype(BF16).astype(F32)
    middle = (stats - high).astype(BF16).astype(F32)
    low = stats - high - middle
    sub = lax.broadcasted_iota(jnp.int32, (8, LANES), 0)
    message = jnp.where(sub < 2, high, jnp.where(sub < 4, middle, jnp.where(sub < 6, low, 0.0)))
    whole[item, piece:] = jnp.concatenate([message, jnp.zeros_like(message)], axis=0).astype(BF16)

    def take(d, total):
        source = peer(items - d)
        out_copy(source, source).wait_recv()
        return total + landed[source].astype(F32)

    total = lax.fori_loop(1, items, take, total)
    whole[item, :piece] = total.astype(BF16)

    def back_copy(place, to):
        return remote(
            whole.at[place], whole.at[place], back_send.at[to], back_recv.at[place], (to, pipe)
        )

    @pl.loop(1, items)
    def _(d):
        back_copy(item, peer(d)).start()

    sum_ref[rows_of(item)] = whole[item, :piece].astype(F32)

    @pl.loop(1, items)
    def _(d):
        to = peer(d)
        cross_copy(to).wait_send()
        out_copy(to, item).wait_send()

    cross_copy(item).wait_send()

    def gather(d, stats):
        source = peer(items - d)
        back_copy(source, source).wait_recv()
        sum_ref[rows_of(source)] = whole[source, :piece].astype(F32)
        return stats + whole[source, piece:].astype(F32)[:8]

    stats = lax.fori_loop(1, items, gather, whole[item, piece:].astype(F32)[:8])
    sum_ref[stats_row : stats_row + 8] = stats

    @pl.loop(1, items)
    def _(d):
        back_copy(item, peer(d)).wait_send()


def summed(items, stats_row, payload):
    rows = payload.shape[1]
    piece = rows // items
    vmem = pl.BlockSpec(memory_space=pltpu.VMEM)
    sems = pltpu.SemaphoreType.DMA((items,))
    return pl.pallas_call(
        functools.partial(sum_kernel, items, stats_row),
        out_shape=jax.ShapeDtypeStruct((rows, LANES), F32),
        in_specs=[pl.BlockSpec(memory_space=pl.ANY)],
        out_specs=vmem,
        scratch_shapes=[
            pltpu.VMEM((rows, LANES), F32),
            pltpu.VMEM((rows, LANES), F32),
            pltpu.VMEM((items, piece, LANES), BF16),
            pltpu.VMEM((items, piece, LANES), BF16),
            pltpu.VMEM((items, piece + 16, LANES), BF16),
            pltpu.SemaphoreType.DMA,
        ]
        + [sems] * 6,
        compiler_params=pltpu.CompilerParams(
            collective_id=1, has_side_effects=True, vmem_limit_bytes=16 * 2**20
        ),
    )(payload)


def update_kernel(*refs):
    rate_net, rate_code, sum_ref = refs[:3]
    states = refs[3:15]
    loss_ref = refs[15]
    results = refs[16:]
    width = states[0].shape[1]
    groups = states[3].shape[1] // LOW
    rows = groups * width
    stats_row = 2 * rows + 3 * width
    stats = sum_ref[stats_row : stats_row + 8]
    odd = jnp.bitwise_and(lax.broadcasted_iota(jnp.int32, stats.shape, 0), 1) == 1
    counts = jnp.where(odd, stats, 0.0)
    loss_ref[0] = jnp.sum(jnp.where(odd, 0.0, stats)) / jnp.sum(counts)
    scale = 1.0 / jnp.sum(counts, keepdims=True)

    def step(kind, place, grad, rate):
        weight_ref, moment_ref, average_ref = (states[4 * j + kind] for j in range(3))
        new_ref, moment_new_ref, average_new_ref, copy_ref = results[4 * kind : 4 * kind + 4]
        grad = grad * scale
        moment = MOMENTUM * moment_ref[place] + grad
        weight = weight_ref[place] - rate * (grad + MOMENTUM * moment)
        new_ref[place] = weight
        moment_new_ref[place] = moment
        average_new_ref[place] = AVERAGE * average_ref[place] + (1.0 - AVERAGE) * weight
        copy_ref[place] = weight.astype(BF16)

    for h in range(groups):
        for side in range(LOW // LANES):
            start = h * LOW + side * LANES
            grad = sum_ref[side * rows + h * width : side * rows + (h + 1) * width]
            place = (slice(None), slice(start, start + LANES))
            step(3, place, -grad, rate_code[0])
    first, second, third = (
        sum_ref[2 * rows + k * width : 2 * rows + (k + 1) * width] for k in range(3)
    )
    rate = rate_net[0]
    step(0, 0, jnp.concatenate([first, second[:, :width]], axis=1), rate)
    step(1, (0, 0), third[:, :width], rate)
    step(1, (0, 1), third[:, width:], rate)
    edge = [second[k : k + 1, width:] for k in (9, 0, 1, 8)]
    step(2, 0, jnp.concatenate(edge, axis=0), rate)


def updated(rates, sums, states):
    smem = pl.BlockSpec(memory_space=pltpu.SMEM)
    shapes = [jax.ShapeDtypeStruct((1,), F32)]
    for weight in states[:4]:
        shapes += [jax.ShapeDtypeStruct(weight.shape, F32)] * 3
        shapes += [jax.ShapeDtypeStruct(weight.shape, BF16)]
    def block(value):
        return pl.BlockSpec(value.shape, lambda i: (0,) * len(value.shape))

    return pl.pallas_call(
        update_kernel,
        grid=(1,),
        out_shape=tuple(shapes),
        in_specs=[smem] * 2 + [block(value) for value in (sums, *states)],
        out_specs=(smem,) + tuple(block(value) for value in shapes[1:]),
        compiler_params=pltpu.CompilerParams(vmem_limit_bytes=24 * 2**20),
    )(*rates, sums, *states)


def per_device(
    waveform,
    lengths,
    code_ids,
    conv_w,
    point_w,
    edge_w,
    codebook,
    conv_mom,
    point_mom,
    edge_mom,
    code_mom,
    conv_avg,
    point_avg,
    edge_avg,
    code_avg,
    rate_net,
    rate_code,
):
    width = conv_w.shape[1]
    items = lax.axis_size("item")
    edge_w, edge_mom, edge_avg = (jnp.swapaxes(v, 1, 2) for v in (edge_w, edge_mom, edge_avg))
    codebook, code_mom, code_avg = (v.T for v in (codebook, code_mom, code_avg))
    rows = 2 * (codebook.shape[1] // LOW) * width + 3 * width
    piece = -(-(rows + 8) // (16 * items)) * 16
    own_inputs = shared(items, lengths, waveform, code_ids, conv_w, point_w, edge_w, codebook)
    payload = net(piece * items, *own_inputs)
    sums = summed(items, rows, payload)
    states = (
        conv_w, point_w, edge_w, codebook,
        conv_mom, point_mom, edge_mom, code_mom,
        conv_avg, point_avg, edge_avg, code_avg,
    )
    loss, *rest = updated((rate_net, rate_code), sums, states)
    edges = (jnp.swapaxes(v, 1, 2) for v in rest[8:12])
    return (loss.reshape(()), *rest[:8], *edges, *(v.T for v in rest[12:]))


def solution(mesh):
    weights = (
        P("pipe", None, None),
        P("pipe", None, None, None),
        P("pipe", None, None),
        P("pipe", None),
    )
    return jax.shard_map(
        per_device,
        mesh=mesh,
        in_specs=(P("item", None), P("item"), P("item", None), *weights, *weights, *weights, P(), P()),
        out_specs=(P(),) + tuple(spec for spec in weights for _ in range(4)),
        check_vma=False,
    )
```

```python
import functools

import jax
import jax.numpy as jnp
from jax import lax
from jax.experimental import pallas as pl
from jax.experimental.pallas import tpu as pltpu
from jax.sharding import PartitionSpec as P

REACH = 3
COMMIT = 0.02
MOMENTUM = 0.9
AVERAGE = 0.99

LANES = 128
TILE = 512
SLOTS = 8
LAG = TILE // LANES + 1
HEAD = 2
DEPTH = -(-4 * LAG * LANES // TILE)
LOW = 256
SPARE = 8
REAL = 4

MESH = pl.DeviceIdType.MESH
ORDER = (1, 6, 3, 2, 4, 7, 5, 0, 1, 6, 3, 2, 4, 7, 5, 0, 1, 6, 3, 2, 4, 7, 5, 0, 1, 6, 3, 2, 7, 5, 0, 1, 6, 3, 2, 7, 5, 6, 2, 7, 5, 6, 7, 6, 6)
F32 = jnp.float32
BF16 = jnp.bfloat16


def nn(a, b):
    return lax.dot_general(a, b, (((1,), (0,)), ((), ())), preferred_element_type=F32)


def nt(a, b):
    return lax.dot_general(a, b, (((1,), (1,)), ((), ())), preferred_element_type=F32)


def moved(ext, distance):
    width = ext.shape[1]
    turned = ext if distance == 0 else pltpu.roll(ext, (-distance) % width, 1)
    return turned[:, LANES : width - LANES]


def relu_bf(values):
    return jnp.maximum(values, 0.0).astype(BF16)


def stack(rows, times):
    return jnp.concatenate([rows] * times, axis=0)


def net_kernel(
    len_src,
    wave_src,
    ids_src,
    weight_src,
    payload_ref,
    len_ref,
    wave_ref,
    ids_ref,
    weight_ref,
    load_sems,
    g_mix,
    g_outs,
    g_edge,
    g_table,
    loss_ref,
    even_scr,
    odd_scr,
    code_scr,
    sig_r,
    msk_r,
    live_r,
    me_r,
    low_r,
    high_r,
    hi_r,
    strips_r,
    onehot_r,
    actu_e_r,
    chosen_r,
    actu_d_r,
    actp_e_r,
    actp_d_r,
    gapb_r,
    outs_r,
    douts_r,
    dinner_d_r,
    dlatent_r,
    dinner_e_r,
):
    pairs = (
        (len_src, len_ref), (wave_src, wave_ref), (ids_src, ids_ref), (weight_src, weight_ref)
    )
    loads = [
        pltpu.make_async_copy(source, place, load_sems.at[k])
        for k, (source, place) in enumerate(pairs)
    ]
    for load in loads:
        load.start()
    sets, per_clip = wave_ref.shape[:2]
    half = per_clip * LANES
    frames = 2 * half
    width = 64
    groups = 2 * (weight_ref.shape[1] - 4 * width - 16) // width
    table_rows = groups // 2 * width
    per_tile = TILE // LANES

    rings = (
        sig_r, msk_r, live_r, me_r, low_r, high_r, hi_r, strips_r, onehot_r, actu_e_r, chosen_r,
        actu_d_r, actp_e_r, actp_d_r, gapb_r, outs_r, douts_r, dinner_d_r, dlatent_r, dinner_e_r,
    )
    slots = SLOTS * per_tile

    @pl.loop(slots - (4 * LAG + 1 - HEAD * per_tile), slots)
    def _(slot):
        for ref in rings:
            ref[slot] = jnp.zeros(ref.shape[1:], ref.dtype)

    for ref in (g_mix, g_outs, g_edge, g_table, loss_ref):
        ref[...] = jnp.zeros(ref.shape, ref.dtype)

    for load in loads:
        load.wait()

    def weight(part, start, rows, first, columns):
        start += table_rows
        return weight_ref[part, start : start + rows, first : first + columns]

    conv = [weight(part, 0, width, 0, 3 * width) for part in range(2)]
    conv_t = [weight(part, width, width, 0, 3 * width) for part in range(2)]
    point = [weight(k // 2, 2 * width, width, k % 2 * width, width) for k in range(4)]
    point_t = [weight(k // 2, 2 * width, width, (2 + k % 2) * width, width) for k in range(4)]
    edge = [weight(part, 3 * width, width, 0, 16) for part in range(2)]
    edge_t = [weight(part, 4 * width, 16, 0, width) for part in range(2)]

    def beside(*parts):
        return jnp.concatenate(parts, axis=1)

    same = lax.broadcasted_iota(jnp.int32, (width, width), 0) == lax.broadcasted_iota(
        jnp.int32, (width, width), 1
    )
    same_bf = jnp.where(same, 1.0, 0.0).astype(BF16)

    def halves(value):
        high = value.astype(BF16)
        return high, (value - high.astype(F32)).astype(BF16)

    latent_w = beside(*halves(nn(point[1], point[0])), *halves(nn(point[1], edge[0])))
    outs_w = jnp.concatenate(halves(nn(edge_t[1], beside(point[3], point[2]))), axis=0)
    inner_d_w = beside(*halves(nn(point_t[3], edge[1])))
    inner_e_w = beside(*halves(nn(point_t[0], point_t[1])))
    back_d = beside(conv_t[1], edge[1])
    back_latent = beside(point_t[2], same_bf)
    back_e = beside(conv_t[0], point_t[1])

    for k in range(sets):
        for block in range(per_clip):
            rows = slice(8 * k, 8 * k + 8)
            parted = wave_ref[k, block].astype(F32)
            even_scr[block, rows] = parted[:8]
            odd_scr[block, rows] = parted[8:]
            code_scr[block, rows] = ids_ref[k, block].astype(F32)

    clips = 8 * sets

    def columns_of(length):
        return lax.shift_right_arithmetic(length + 1, 1) + SPARE

    def length_of(clip):
        return len_ref[jnp.bitwise_and(clip, 8), jnp.bitwise_and(clip, 7)]

    def add_clip(c, carry):
        length = length_of(c)
        return carry[0] + columns_of(length), carry[1] + length

    columns, count = lax.fori_loop(0, clips, add_clip, (jnp.int32(0), jnp.int32(0)))
    tiles = lax.div(columns + TILE - 1, jnp.int32(TILE)) + DEPTH

    sub = lax.broadcasted_iota(jnp.int32, (8, LANES), 0)
    lane = lax.broadcasted_iota(jnp.int32, (8, LANES), 1)
    sub_ext = lax.broadcasted_iota(jnp.int32, (8, TILE + 2 * LANES), 0)
    sub_tile = lax.broadcasted_iota(jnp.int32, (8, TILE), 0)
    iota16 = lax.broadcasted_iota(jnp.int32, (16, TILE), 0).astype(F32).astype(BF16)

    table = jnp.concatenate([weight_ref[part, :table_rows] for part in range(2)], axis=0)

    def taps(ext):
        later = moved(ext, 1)
        earlier = moved(ext, -1)
        other = jnp.where(sub_tile == 0, later, jnp.where(sub_tile == 1, earlier, 0.0))
        return jnp.concatenate([moved(ext, 0), other], axis=0)

    def rows_at(clip, place):
        here = (jnp.minimum(place, per_clip - 1), pl.ds(jnp.minimum(clip, clips - 1), 1), slice(None))
        even, odd, code = (
            jnp.broadcast_to(ref[here], (8, LANES)) for ref in (even_scr, odd_scr, code_scr)
        )
        return jnp.where(sub == 0, even, jnp.where(sub == 1, odd, code))

    def known_length(clip):
        return jnp.where(clip < clips, length_of(clip), -frames)

    def fetch(state, slot):
        clip, start = state
        own, following = known_length(clip), known_length(clip + 1)
        cut = jnp.where(clip < clips, columns_of(own), 1 << 20) - start
        inside = lane < cut
        t = jnp.where(inside, start + lane, lane - cut)
        length = jnp.where(inside, own, following)
        turn = jnp.bitwise_and(start, LANES - 1)
        place = lax.shift_right_logical(start, 7)
        ahead = jnp.where(lane >= turn, rows_at(clip, place), rows_at(clip, place + 1))
        ahead = pltpu.roll(ahead, jnp.bitwise_and(LANES - turn, LANES - 1), 1)
        after = pltpu.roll(rows_at(clip + 1, 0), jnp.bitwise_and(cut, LANES - 1), 1)
        values = jnp.where(inside, ahead, after)
        code = jnp.broadcast_to(values[2:3], (8, LANES)).astype(jnp.int32)
        even_ok = 2 * t < length
        odd_ok = 2 * t + 1 < length
        live = t < jnp.minimum(lax.shift_right_arithmetic(length + 1, 1) + REAL, half)
        low = jnp.where(live, jnp.bitwise_and(code, LOW - 1), -1).astype(F32)
        high = lax.shift_right_logical(code, 8).astype(F32)
        known = ((sub == 0) & even_ok) | ((sub == 1) & odd_ok)
        sig_r[slot] = jnp.where(known, values, 0.0)
        msk_r[slot] = jnp.where(known, 1.0, 0.0)
        live_r[slot] = jnp.where(live, 1.0, 0.0)
        me_r[slot] = jnp.where(even_ok, 1.0, 0.0)
        low_r[slot] = stack(low, 2).astype(BF16)
        high_r[slot] = high
        hi_r[slot] = stack(high, 2).astype(BF16)
        done = cut <= LANES
        return jnp.where(done, clip + 1, clip), jnp.where(done, LANES - cut, start + LANES)

    state = (jnp.int32(0), jnp.int32(0))
    for b in range(per_tile + 1):
        state = fetch(state, b)

    def tile_step(names, i, state):
        def block(lag, b):
            return jnp.bitwise_and(i * per_tile - lag + b, slots - 1)

        def load(ref, lag, first=0, last=per_tile):
            return jnp.concatenate([ref[block(lag, b)] for b in range(first, last)], axis=1)

        def load_ext(ref, lag):
            return load(ref, lag, -1, per_tile + 1)

        def keep(ref, lag, value):
            for b in range(per_tile):
                ref[block(lag, b)] = value[:, b * LANES : (b + 1) * LANES]

        def spread(ext, way):
            return jnp.concatenate([moved(ext, d * way) for d in (-REACH, 0, REACH)], axis=0)

        def strips_step():
            sig_ext, live = load_ext(sig_r, 0), load(live_r, 0)
            yield
            strips = (taps(sig_ext) * stack(live, 2)).astype(BF16)
            keep(strips_r, 0, strips)
            yield
            hidden = nn(edge[0], strips)
            yield
            keep(actu_e_r, 0, relu_bf(hidden))

        def lookup_step():
            low16, hi = load(low_r, 0) - iota16, load(high_r, 0)
            onehot = jnp.concatenate(
                [
                    jnp.where(low16 == float(16 * r), jnp.ones((), BF16), jnp.zeros((), BF16))
                    for r in range(LOW // 16)
                ],
                axis=0,
            )
            keep(onehot_r, 0, onehot)
            yield
            picked = nn(table, onehot)
            yield
            parts = [jnp.zeros((8, TILE), F32) for _ in range(width // 8)]
            for h in range(groups):
                here = hi == float(h)
                parts = [
                    jnp.where(here, picked[h * width + 8 * r : h * width + 8 * r + 8], parts[r])
                    for r in range(width // 8)
                ]
            chosen = jnp.concatenate(parts, axis=0).astype(BF16)
            keep(chosen_r, 0, chosen)
            yield
            decin = nn(point[2], chosen)
            yield
            keep(actu_d_r, 0, relu_bf(decin))

        def encode_step():
            lag = LAG
            around = spread(load_ext(actu_e_r, lag), 1)
            yield
            inner = nn(conv[0], around)
            yield
            actp, strips = relu_bf(inner), load(strips_r, lag)
            keep(actp_e_r, lag, actp)
            yield
            latent = nn(latent_w, jnp.concatenate([actp, actp, strips, strips], axis=0))
            chosen, me = load(chosen_r, lag), load(me_r, lag)
            yield
            gap = (latent.astype(BF16).astype(F32) - chosen.astype(F32)) * stack(me, width // 8)
            keep(gapb_r, lag, (gap * (2.0 * COMMIT)).astype(BF16))
            yield
            square = gap * gap
            rows = square[:8]
            for r in range(1, width // 8):
                rows = rows + square[8 * r : 8 * r + 8]
            add_loss(COMMIT * rows)

        def decode_step():
            lag = LAG
            around = spread(load_ext(actu_d_r, lag), 1)
            yield
            inner = nn(conv[1], around)
            yield
            actp, chosen = relu_bf(inner), load(chosen_r, lag)
            keep(actp_d_r, lag, actp)
            yield
            outs = nn(outs_w, jnp.concatenate([actp, chosen], axis=0))
            yield
            keep(outs_r, lag, outs[:16] + outs[16:])

        def scatter_step():
            lag = LAG + per_tile
            hi, gap = load(hi_r, lag), load(gapb_r, lag)
            terms = []
            for h in range(groups):
                here = hi == float(h)
                terms += [
                    jnp.where(here, gap[16 * r : 16 * r + 16], jnp.zeros((), BF16))
                    for r in range(width // 16)
                ]
            onehot = load(onehot_r, lag)
            yield
            found = nt(jnp.concatenate(terms, axis=0), onehot)
            yield
            g_table[...] += found

        def add_loss(rows):
            total = rows[:, :LANES]
            for j in range(1, per_tile):
                total = total + rows[:, j * LANES : (j + 1) * LANES]
            loss_ref[...] += total

        def error_step():
            lag = 2 * LAG
            outs_ext, live_ext = load_ext(outs_r, lag), load_ext(live_r, lag)
            sig_ext, msk_ext = load_ext(sig_r, lag), load_ext(msk_r, lag)
            outs_ext = outs_ext * stack(live_ext, 2)
            shifted = outs_ext[8:]
            wide = TILE + 2 * LANES
            crossed = jnp.where(
                sub_ext == 0, pltpu.roll(shifted, 1, 1), pltpu.roll(shifted, wide - 1, 1)
            )
            error = (outs_ext[:8] + crossed - sig_ext) * msk_ext
            middle = moved(error, 0)
            add_loss(middle * middle)
            yield
            douts = (2.0 * taps(error) * stack(moved(live_ext, 0), 2)).astype(BF16)
            keep(douts_r, lag, douts)
            yield
            dinner = nn(inner_d_w, jnp.concatenate([douts, douts], axis=0))
            actp = load(actp_d_r, lag)
            yield
            keep(dinner_d_r, lag, jnp.where(actp > 0, dinner.astype(BF16), 0))
            yield
            found = nt(jnp.concatenate([actp, load(chosen_r, lag)], axis=0), douts)
            yield
            g_outs[...] += found

        def middle_step():
            lag = 3 * LAG
            around, douts = spread(load_ext(dinner_d_r, lag), -1), load(douts_r, lag)
            yield
            both = nn(back_d, jnp.concatenate([around, douts], axis=0))
            dres = nn(edge[1], douts)
            actu = load(actu_d_r, lag)
            yield
            ddecin = jnp.where(actu > 0, both.astype(BF16), dres.astype(BF16))
            gap = load(gapb_r, lag)
            yield
            back = nn(back_latent, jnp.concatenate([ddecin, gap], axis=0))
            yield
            dlatent = back.astype(BF16)
            keep(dlatent_r, lag, dlatent)
            yield
            dinner = nn(inner_e_w, jnp.concatenate([dlatent, dlatent], axis=0))
            actp = load(actp_e_r, lag)
            yield
            keep(dinner_e_r, lag, jnp.where(actp > 0, dinner.astype(BF16), 0))
            yield
            found = nt(
                jnp.concatenate([actu, load(chosen_r, lag)], axis=0),
                jnp.concatenate([around, ddecin], axis=0),
            )
            yield
            g_mix[1, :width] += found[:width]
            g_mix[1, width : 2 * width, LANES:] += found[width:, LANES:]

        def last_step():
            lag = 4 * LAG
            around = spread(load_ext(dinner_e_r, lag), -1)
            dlatent = load(dlatent_r, lag)
            yield
            both = nn(back_e, jnp.concatenate([around, dlatent], axis=0))
            denc = nn(point_t[1], dlatent)
            actu = load(actu_e_r, lag)
            yield
            dhidden = jnp.where(actu > 0, both.astype(BF16), denc.astype(BF16))
            strips = load(strips_r, lag)
            yield
            found = nt(
                jnp.concatenate([actu, load(actp_e_r, lag), strips], axis=0),
                jnp.concatenate([around, dlatent], axis=0),
            )
            yield
            g_mix[0, :width] += found[:width]
            g_mix[0, width:, LANES:] += found[width:, LANES:]
            yield
            found = nt(dhidden, strips)
            yield
            g_edge[...] += found

        functions = (
            strips_step,
            lookup_step,
            encode_step,
            decode_step,
            scatter_step,
            error_step,
            middle_step,
            last_step,
        )
        steps = {k: functions[k]() for k in names}
        for k in ORDER:
            if k in steps:
                next(steps[k], None)
        for step in steps.values():
            for _ in step:
                pass
        if 0 in names:
            for b in range(per_tile):
                state = fetch(state, block(-LAG, b))
        return state

    ranges = (
        ((0, 1, 2, 3), 0, HEAD),
        (range(8), HEAD, tiles - 2),
        ((6, 7), tiles - 2, tiles - 1),
        ((7,), tiles - 1, tiles),
    )
    for names, begin, end in ranges:
        state = lax.fori_loop(begin, end, functools.partial(tile_step, names), state)

    loss_row = jnp.sum(loss_ref[...], axis=0, keepdims=True)
    count_row = jnp.where(lane == 0, count, 0).astype(F32)
    stats = jnp.where(
        jnp.bitwise_and(sub, 1) == 0, jnp.broadcast_to(loss_row, (8, LANES)), count_row
    )
    def exact(a, b, axis):
        return lax.dot_general(
            a.astype(F32),
            b.astype(F32),
            (((1,), (axis,)), ((), ())),
            preferred_element_type=F32,
            precision=lax.Precision.HIGHEST,
        )

    by_latent = g_mix[0, width : 2 * width, 3 * width :].T
    by_strips = g_mix[0, 2 * width :, 3 * width :].T
    by_inner, by_chosen = g_outs[:width].T, g_outs[width:].T
    points = (
        (
            exact(point_t[1], by_latent, 0),
            exact(by_latent, point[0], 1) + exact(by_strips, edge[0], 1),
        ),
        (g_mix[1, width : 2 * width, 3 * width :].T, exact(edge[1], by_inner, 0)),
    )
    edges = (g_edge[...].T, exact(by_inner, point[3], 1) + exact(by_chosen, point[2], 1))
    rows = groups // 2 * width
    for part in range(2):
        payload_ref[part, :rows] = g_table[part * rows : (part + 1) * rows, :LANES]
        payload_ref[part, rows : 2 * rows] = g_table[part * rows : (part + 1) * rows, LANES:]
        conv_rows = [g_mix[part, :width, k * width : (k + 1) * width].T for k in range(3)]
        edge_rows = jnp.concatenate([edges[part], jnp.zeros((width - 16, width), F32)], axis=0)
        after = 2 * rows
        for pair in (
            conv_rows[:2],
            (conv_rows[2], edge_rows),
            points[part],
        ):
            payload_ref[part, after : after + width] = jnp.concatenate(pair, axis=1)
            after += width
        payload_ref[part, after : after + 8] = stats
        after += 8
        rest = payload_ref.shape[1] - after
        if rest:
            payload_ref[part, after:] = jnp.zeros((rest, LANES), F32)


def net(rows, lengths, wave, codes, weights):
    sets, per_clip = wave.shape[:2]
    clips = 8 * sets
    width = 64
    table_rows = 2 * (weights.shape[1] - 4 * width - 16)
    slots = SLOTS * TILE // LANES
    vmem = pl.BlockSpec(memory_space=pltpu.VMEM)

    def ring(rows, dtype):
        return pltpu.VMEM((slots, rows, LANES), dtype)

    return pl.pallas_call(
        net_kernel,
        out_shape=jax.ShapeDtypeStruct((2, rows, LANES), F32),
        in_specs=[pl.BlockSpec(memory_space=pl.ANY)] * 4,
        out_specs=vmem,
        scratch_shapes=[
            pltpu.SMEM(lengths.shape, lengths.dtype),
            pltpu.VMEM(wave.shape, wave.dtype),
            pltpu.VMEM(codes.shape, codes.dtype),
            pltpu.VMEM(weights.shape, weights.dtype),
            pltpu.SemaphoreType.DMA((4,)),
            pltpu.VMEM((2, 2 * width + 16, 4 * width), F32),
            pltpu.VMEM((2 * width, 16), F32),
            pltpu.VMEM((width, 16), F32),
            pltpu.VMEM((table_rows, LOW), F32),
            pltpu.VMEM((8, LANES), F32),
            pltpu.VMEM((per_clip, clips, LANES), F32),
            pltpu.VMEM((per_clip, clips, LANES), F32),
            pltpu.VMEM((per_clip, clips, LANES), F32),
            *(ring(8, F32) for _ in range(4)),
            ring(16, BF16),
            ring(8, F32),
            *(ring(16, BF16) for _ in range(2)),
            ring(LOW, BF16),
            *(ring(width, BF16) for _ in range(6)),
            ring(16, F32),
            ring(16, BF16),
            *(ring(width, BF16) for _ in range(3)),
        ],
        compiler_params=pltpu.CompilerParams(vmem_limit_bytes=60 * 2**20),
    )(lengths, wave, codes, weights)


def remote(src, dst, send, recv, to):
    return pltpu.make_async_remote_copy(
        src_ref=src, dst_ref=dst, send_sem=send, recv_sem=recv, device_id=to, device_id_type=MESH
    )


def share_kernel(items, *refs):
    sources, (len_out, wave_out, ids_out, weight_out), inputs = refs[:7], refs[7:11], refs[11:18]
    len_ref, wave_ref, ids_ref, conv_ref, point_ref, edge_ref, table_ref = inputs
    len_scr, wave_scr, ids_scr, weight_scr, sems, load_sems = refs[18:]
    loads = [
        pltpu.make_async_copy(source, place, load_sems.at[k])
        for k, (source, place) in enumerate(zip(sources, inputs))
    ]
    for load in loads:
        load.start()
    item = lax.axis_index("item")
    pipe = lax.axis_index("pipe")
    partner = (item, 1 - pipe)
    mirror = (items - 1 - item, pipe)
    per_clip = wave_out.shape[1]
    width = conv_ref.shape[1]
    table_rows = weight_scr.shape[1] - 4 * width - 16

    barrier = pltpu.get_barrier_semaphore()
    for other in (partner, mirror):
        pl.semaphore_signal(barrier, inc=1, device_id=other, device_id_type=MESH)

    row_at = lax.broadcasted_iota(jnp.int32, (2 * LANES, 2 * LANES), 0)
    col_at = lax.broadcasted_iota(jnp.int32, (2 * LANES, 2 * LANES), 1)
    wanted = jnp.where(col_at < LANES, 2 * col_at, 2 * (col_at - LANES) + 1)
    split = jnp.where(row_at == wanted, 1.0, 0.0).astype(BF16)
    on_first = pipe == 0
    for load in loads[:3]:
        load.wait()
    lane = lax.broadcasted_iota(jnp.int32, (8, LANES), 1)
    kept = jnp.zeros((8, LANES), jnp.int32)
    given = kept
    for k in range(8):
        kept = jnp.where(lane == k, jnp.where(on_first, len_ref[k], len_ref[8 + k]), kept)
        given = jnp.where(lane == k, jnp.where(on_first, len_ref[24 + k], len_ref[16 + k]), given)
    len_out[:8] = kept
    len_scr[0] = given
    clips = wave_ref.shape[0]
    strips = [wave_ref[:, k * 2 * LANES : (k + 1) * 2 * LANES] for k in range(per_clip)]
    parted = nn(jnp.concatenate(strips, axis=0), split)

    def chosen(values, first, second):
        return jnp.where(on_first, values[8 * first :][:8], values[8 * second :][:8])

    def both(values, first, second):
        pair = [
            chosen(side, first, second) for side in (values[:, :LANES], values[:, LANES:])
        ]
        return jnp.concatenate(pair, axis=0).astype(BF16)

    codes = [ids_ref[:, k * LANES : (k + 1) * LANES] for k in range(per_clip)]
    for k in range(per_clip):
        values = parted[clips * k : clips * (k + 1)]
        wave_scr[0, k] = both(values, 3, 2)
        wave_out[0, k] = both(values, 0, 1)
        ids_out[0, k] = chosen(codes[k], 0, 1)
    for k in range(per_clip // 2):
        pair = [chosen(codes[2 * k + j], 3, 2) for j in range(2)]
        ids_scr[0, k] = jnp.concatenate(pair, axis=0).astype(jnp.int16)

    pl.semaphore_wait(barrier, 2)
    copies = [
        remote(ref.at[0], ref.at[1], sems.at[2 * k], sems.at[2 * k + 1], mirror)
        for k, ref in enumerate((len_scr, wave_scr, ids_scr))
    ]
    for copy in copies:
        copy.start()

    for load in loads[3:]:
        load.wait()
    groups = table_rows // width
    for h in range(groups):
        weight_scr[0, h * width : (h + 1) * width] = table_ref[:, h * LOW : (h + 1) * LOW].astype(
            BF16
        )
    blank = jnp.zeros((width, LOW - 3 * width), F32)
    conv = conv_ref[0]
    conv_t = [conv[:, k * width : (k + 1) * width].T for k in range(3)]
    points = [point_ref[0, 0], point_ref[0, 1]]
    edge = edge_ref[0]
    empty = jnp.zeros((6, width), F32)
    edge_t = jnp.concatenate([edge[1:3], empty, edge[3:], edge[:1], empty], axis=0)
    edge_square = jnp.concatenate([edge_t, jnp.zeros((width - 16, width), F32)], axis=0).T
    after = table_rows
    for pieces in (
        [conv, blank],
        conv_t + [blank],
        points + [value.T for value in points],
        [edge_square, jnp.zeros((width, LOW - width), F32)],
        [edge_t, jnp.zeros((16, LOW - width), F32)],
    ):
        value = jnp.concatenate(pieces, axis=1).astype(BF16)
        weight_scr[0, after : after + value.shape[0]] = value
        after += value.shape[0]
    over = remote(weight_scr.at[0], weight_scr.at[1], sems.at[6], sems.at[7], partner)
    over.start()
    weight_out[pipe] = weight_scr[0]
    over.wait()
    weight_out[1 - pipe] = weight_scr[1]
    for copy in copies:
        copy.wait()
    len_out[8:] = len_scr[1]
    wave_out[1] = wave_scr[1]
    for k in range(per_clip // 2):
        pair = ids_scr[1, k].astype(jnp.int32)
        ids_out[1, 2 * k], ids_out[1, 2 * k + 1] = pair[:8], pair[8:]


def shared(items, lengths, waveform, code_ids, conv, point, edge, table):
    per_clip = code_ids.shape[1] // LANES
    width = conv.shape[1]
    weight_rows = table.shape[1] // LOW * width + 4 * width + 16
    vmem = pl.BlockSpec(memory_space=pltpu.VMEM)
    wave_shape = (2, per_clip, 16, LANES)
    ids_shape = (2, per_clip, 8, LANES)
    weight_shape = (2, weight_rows, LOW)
    return pl.pallas_call(
        functools.partial(share_kernel, items),
        out_shape=(
            jax.ShapeDtypeStruct((16, LANES), jnp.int32),
            jax.ShapeDtypeStruct(wave_shape, BF16),
            jax.ShapeDtypeStruct(ids_shape, jnp.int32),
            jax.ShapeDtypeStruct(weight_shape, BF16),
        ),
        in_specs=[pl.BlockSpec(memory_space=pl.ANY)] * 7,
        out_specs=(vmem,) * 4,
        scratch_shapes=[pltpu.SMEM(lengths.shape, jnp.int32)]
        + [
            pltpu.VMEM(value.shape, value.dtype)
            for value in (waveform, code_ids, conv, point, edge, table)
        ]
        + [
            pltpu.VMEM((2, 8, LANES), jnp.int32),
            pltpu.VMEM(wave_shape, BF16),
            pltpu.VMEM((2, per_clip // 2, 16, LANES), jnp.int16),
            pltpu.VMEM(weight_shape, BF16),
            pltpu.SemaphoreType.DMA((8,)),
            pltpu.SemaphoreType.DMA((7,)),
        ],
        compiler_params=pltpu.CompilerParams(
            collective_id=0, has_side_effects=True, vmem_limit_bytes=60 * 2**20
        ),
    )(lengths, waveform, code_ids, conv, point, edge, table)


def sum_kernel(
    items,
    stats_row,
    payload_ref,
    sum_ref,
    own,
    crossed,
    part,
    landed,
    whole,
    own_sem,
    cross_send,
    cross_recv,
    out_send,
    out_recv,
    back_send,
    back_recv,
):
    item = lax.axis_index("item")
    pipe = lax.axis_index("pipe")
    partner = (item, 1 - pipe)
    piece = part.shape[1]

    def peer(d):
        if items & (items - 1):
            return lax.rem(item + d, items)
        return jnp.bitwise_and(item + d, items - 1)

    def rows_of(k):
        return pl.ds(pl.multiple_of(k * piece, piece), piece)

    load = pltpu.make_async_copy(payload_ref.at[pipe], own, own_sem)
    load.start()
    barrier = pltpu.get_barrier_semaphore()
    pl.semaphore_signal(barrier, inc=1, device_id=partner, device_id_type=MESH)

    @pl.loop(1, items)
    def _(d):
        pl.semaphore_signal(barrier, inc=1, device_id=(peer(d), pipe), device_id_type=MESH)

    pl.semaphore_wait(barrier, items)

    def cross_copy(k):
        return remote(
            payload_ref.at[1 - pipe, rows_of(k)], crossed.at[rows_of(k)],
            cross_send.at[k], cross_recv.at[k], partner,
        )

    @pl.loop(1, items)
    def _(d):
        cross_copy(peer(d)).start()

    cross_copy(item).start()
    load.wait()

    def out_copy(to, place):
        return remote(
            part.at[to], landed.at[place], out_send.at[to], out_recv.at[place], (to, pipe)
        )

    @pl.loop(1, items)
    def _(d):
        to = peer(d)
        cross_copy(to).wait_recv()
        part[to] = (own[rows_of(to)] + crossed[rows_of(to)]).astype(BF16)
        out_copy(to, item).start()

    cross_copy(item).wait_recv()
    total = own[rows_of(item)] + crossed[rows_of(item)]
    stats = own[stats_row : stats_row + 8] + crossed[stats_row : stats_row + 8]
    high = stats.astype(BF16).astype(F32)
    middle = (stats - high).astype(BF16).astype(F32)
    low = stats - high - middle
    sub = lax.broadcasted_iota(jnp.int32, (8, LANES), 0)
    message = jnp.where(sub < 2, high, jnp.where(sub < 4, middle, jnp.where(sub < 6, low, 0.0)))
    whole[item, piece:] = jnp.concatenate([message, jnp.zeros_like(message)], axis=0).astype(BF16)

    def take(d, total):
        source = peer(d)
        out_copy(source, source).wait_recv()
        return total + landed[source].astype(F32)

    total = lax.fori_loop(1, items, take, total)
    whole[item, :piece] = total.astype(BF16)

    def back_copy(place, to):
        return remote(
            whole.at[place], whole.at[place], back_send.at[to], back_recv.at[place], (to, pipe)
        )

    @pl.loop(1, items)
    def _(d):
        back_copy(item, peer(d)).start()

    sum_ref[rows_of(item)] = whole[item, :piece].astype(F32)

    @pl.loop(1, items)
    def _(d):
        to = peer(d)
        cross_copy(to).wait_send()
        out_copy(to, item).wait_send()

    cross_copy(item).wait_send()

    def gather(d, stats):
        source = peer(d)
        back_copy(source, source).wait_recv()
        sum_ref[rows_of(source)] = whole[source, :piece].astype(F32)
        return stats + whole[source, piece:].astype(F32)[:8]

    stats = lax.fori_loop(1, items, gather, whole[item, piece:].astype(F32)[:8])
    sum_ref[stats_row : stats_row + 8] = stats

    @pl.loop(1, items)
    def _(d):
        back_copy(item, peer(d)).wait_send()


def summed(items, stats_row, payload):
    rows = payload.shape[1]
    piece = rows // items
    vmem = pl.BlockSpec(memory_space=pltpu.VMEM)
    sems = pltpu.SemaphoreType.DMA((items,))
    return pl.pallas_call(
        functools.partial(sum_kernel, items, stats_row),
        out_shape=jax.ShapeDtypeStruct((rows, LANES), F32),
        in_specs=[pl.BlockSpec(memory_space=pl.ANY)],
        out_specs=vmem,
        scratch_shapes=[
            pltpu.VMEM((rows, LANES), F32),
            pltpu.VMEM((rows, LANES), F32),
            pltpu.VMEM((items, piece, LANES), BF16),
            pltpu.VMEM((items, piece, LANES), BF16),
            pltpu.VMEM((items, piece + 16, LANES), BF16),
            pltpu.SemaphoreType.DMA,
        ]
        + [sems] * 6,
        compiler_params=pltpu.CompilerParams(
            collective_id=1, has_side_effects=True, vmem_limit_bytes=16 * 2**20
        ),
    )(payload)


def update_kernel(*refs):
    rate_net, rate_code, sum_ref = refs[:3]
    states = refs[3:15]
    loss_ref = refs[15]
    results = refs[16:]
    width = states[0].shape[1]
    groups = states[3].shape[1] // LOW
    rows = groups * width
    stats_row = 2 * rows + 3 * width
    stats = sum_ref[stats_row : stats_row + 8]
    odd = jnp.bitwise_and(lax.broadcasted_iota(jnp.int32, stats.shape, 0), 1) == 1
    counts = jnp.where(odd, stats, 0.0)
    loss_ref[0] = jnp.sum(jnp.where(odd, 0.0, stats)) / jnp.sum(counts)
    scale = 1.0 / jnp.sum(counts, keepdims=True)

    def step(kind, place, grad, rate):
        weight_ref, moment_ref, average_ref = (states[4 * j + kind] for j in range(3))
        new_ref, moment_new_ref, average_new_ref, copy_ref = results[4 * kind : 4 * kind + 4]
        grad = grad * scale
        moment = MOMENTUM * moment_ref[place] + grad
        weight = weight_ref[place] - rate * (grad + MOMENTUM * moment)
        new_ref[place] = weight
        moment_new_ref[place] = moment
        average_new_ref[place] = AVERAGE * average_ref[place] + (1.0 - AVERAGE) * weight
        copy_ref[place] = weight.astype(BF16)

    for h in range(groups):
        for side in range(LOW // LANES):
            start = h * LOW + side * LANES
            grad = sum_ref[side * rows + h * width : side * rows + (h + 1) * width]
            place = (slice(None), slice(start, start + LANES))
            step(3, place, -grad, rate_code[0])
    first, second, third = (
        sum_ref[2 * rows + k * width : 2 * rows + (k + 1) * width] for k in range(3)
    )
    rate = rate_net[0]
    step(0, 0, jnp.concatenate([first, second[:, :width]], axis=1), rate)
    step(1, (0, 0), third[:, :width], rate)
    step(1, (0, 1), third[:, width:], rate)
    edge = [second[k : k + 1, width:] for k in (9, 0, 1, 8)]
    step(2, 0, jnp.concatenate(edge, axis=0), rate)


def updated(rates, sums, states):
    smem = pl.BlockSpec(memory_space=pltpu.SMEM)
    shapes = [jax.ShapeDtypeStruct((1,), F32)]
    for weight in states[:4]:
        shapes += [jax.ShapeDtypeStruct(weight.shape, F32)] * 3
        shapes += [jax.ShapeDtypeStruct(weight.shape, BF16)]
    def block(value):
        return pl.BlockSpec(value.shape, lambda i: (0,) * len(value.shape))

    return pl.pallas_call(
        update_kernel,
        grid=(1,),
        out_shape=tuple(shapes),
        in_specs=[smem] * 2 + [block(value) for value in (sums, *states)],
        out_specs=(smem,) + tuple(block(value) for value in shapes[1:]),
        compiler_params=pltpu.CompilerParams(vmem_limit_bytes=24 * 2**20),
    )(*rates, sums, *states)


def per_device(
    waveform,
    lengths,
    code_ids,
    conv_w,
    point_w,
    edge_w,
    codebook,
    conv_mom,
    point_mom,
    edge_mom,
    code_mom,
    conv_avg,
    point_avg,
    edge_avg,
    code_avg,
    rate_net,
    rate_code,
):
    width = conv_w.shape[1]
    items = lax.axis_size("item")
    edge_w, edge_mom, edge_avg = (jnp.swapaxes(v, 1, 2) for v in (edge_w, edge_mom, edge_avg))
    codebook, code_mom, code_avg = (v.T for v in (codebook, code_mom, code_avg))
    rows = 2 * (codebook.shape[1] // LOW) * width + 3 * width
    piece = -(-(rows + 8) // (16 * items)) * 16
    own_inputs = shared(items, lengths, waveform, code_ids, conv_w, point_w, edge_w, codebook)
    payload = net(piece * items, *own_inputs)
    sums = summed(items, rows, payload)
    states = (
        conv_w, point_w, edge_w, codebook,
        conv_mom, point_mom, edge_mom, code_mom,
        conv_avg, point_avg, edge_avg, code_avg,
    )
    loss, *rest = updated((rate_net, rate_code), sums, states)
    edges = (jnp.swapaxes(v, 1, 2) for v in rest[8:12])
    return (loss.reshape(()), *rest[:8], *edges, *(v.T for v in rest[12:]))


def solution(mesh):
    weights = (
        P("pipe", None, None),
        P("pipe", None, None, None),
        P("pipe", None, None),
        P("pipe", None),
    )
    return jax.shard_map(
        per_device,
        mesh=mesh,
        in_specs=(P("item", None), P("item"), P("item", None), *weights, *weights, *weights, P(), P()),
        out_specs=(P(),) + tuple(spec for spec in weights for _ in range(4)),
        check_vma=False,
    )
```

```python
import functools

import jax
import jax.numpy as jnp
from jax import lax
from jax.experimental import pallas as pl
from jax.experimental.pallas import tpu as pltpu
from jax.sharding import PartitionSpec as P

REACH = 3
COMMIT = 0.02
MOMENTUM = 0.9
AVERAGE = 0.99

LANES = 128
TILE = 512
SLOTS = 8
LAG = TILE // LANES + 1
HEAD = 2
DEPTH = -(-4 * LAG * LANES // TILE)
LOW = 256
SPARE = 8
REAL = 4

MESH = pl.DeviceIdType.MESH
ORDER = (1, 6, 3, 2, 4, 7, 5, 0, 1, 6, 3, 2, 4, 7, 5, 0, 1, 6, 3, 2, 4, 7, 5, 0, 1, 6, 3, 2, 7, 5, 0, 1, 6, 3, 2, 7, 5, 6, 2, 7, 5, 6, 7, 6, 6)
F32 = jnp.float32
BF16 = jnp.bfloat16


def nn(a, b):
    return lax.dot_general(a, b, (((1,), (0,)), ((), ())), preferred_element_type=F32)


def nt(a, b):
    return lax.dot_general(a, b, (((1,), (1,)), ((), ())), preferred_element_type=F32)


def moved(ext, distance):
    width = ext.shape[1]
    turned = ext if distance == 0 else pltpu.roll(ext, (-distance) % width, 1)
    return turned[:, LANES : width - LANES]


def relu_bf(values):
    return jnp.maximum(values, 0.0).astype(BF16)


def stack(rows, times):
    return jnp.concatenate([rows] * times, axis=0)


def net_kernel(
    len_src,
    wave_src,
    ids_src,
    weight_src,
    payload_ref,
    len_ref,
    wave_ref,
    ids_ref,
    weight_ref,
    load_sems,
    g_mix,
    g_outs,
    g_edge,
    g_table,
    loss_ref,
    even_scr,
    odd_scr,
    code_scr,
    sig_r,
    msk_r,
    live_r,
    me_r,
    low_r,
    high_r,
    hi_r,
    strips_r,
    onehot_r,
    actu_e_r,
    chosen_r,
    actu_d_r,
    actp_e_r,
    actp_d_r,
    gapb_r,
    outs_r,
    douts_r,
    dinner_d_r,
    dlatent_r,
    dinner_e_r,
):
    pairs = (
        (len_src, len_ref), (wave_src, wave_ref), (ids_src, ids_ref), (weight_src, weight_ref)
    )
    loads = [
        pltpu.make_async_copy(source, place, load_sems.at[k])
        for k, (source, place) in enumerate(pairs)
    ]
    for load in loads:
        load.start()
    sets, per_clip = wave_ref.shape[:2]
    half = per_clip * LANES
    frames = 2 * half
    width = 64
    groups = 2 * (weight_ref.shape[1] - 4 * width - 16) // width
    table_rows = groups // 2 * width
    per_tile = TILE // LANES

    rings = (
        sig_r, msk_r, live_r, me_r, low_r, high_r, hi_r, strips_r, onehot_r, actu_e_r, chosen_r,
        actu_d_r, actp_e_r, actp_d_r, gapb_r, outs_r, douts_r, dinner_d_r, dlatent_r, dinner_e_r,
    )
    slots = SLOTS * per_tile

    @pl.loop(slots - (4 * LAG + 1 - HEAD * per_tile), slots)
    def _(slot):
        for ref in rings:
            ref[slot] = jnp.zeros(ref.shape[1:], ref.dtype)

    for ref in (g_mix, g_outs, g_edge, g_table, loss_ref):
        ref[...] = jnp.zeros(ref.shape, ref.dtype)

    for load in loads:
        load.wait()

    def weight(part, start, rows, first, columns):
        start += table_rows
        return weight_ref[part, start : start + rows, first : first + columns]

    conv = [weight(part, 0, width, 0, 3 * width) for part in range(2)]
    conv_t = [weight(part, width, width, 0, 3 * width) for part in range(2)]
    point = [weight(k // 2, 2 * width, width, k % 2 * width, width) for k in range(4)]
    point_t = [weight(k // 2, 2 * width, width, (2 + k % 2) * width, width) for k in range(4)]
    edge = [weight(part, 3 * width, width, 0, 16) for part in range(2)]
    edge_t = [weight(part, 4 * width, 16, 0, width) for part in range(2)]

    def beside(*parts):
        return jnp.concatenate(parts, axis=1)

    same = lax.broadcasted_iota(jnp.int32, (width, width), 0) == lax.broadcasted_iota(
        jnp.int32, (width, width), 1
    )
    same_bf = jnp.where(same, 1.0, 0.0).astype(BF16)

    def halves(value):
        high = value.astype(BF16)
        return high, (value - high.astype(F32)).astype(BF16)

    latent_w = beside(*halves(nn(point[1], point[0])), *halves(nn(point[1], edge[0])))
    outs_w = jnp.concatenate(halves(nn(edge_t[1], beside(point[3], point[2]))), axis=0)
    inner_d_w = beside(*halves(nn(point_t[3], edge[1])))
    inner_e_w = beside(*halves(nn(point_t[0], point_t[1])))
    back_d = beside(conv_t[1], edge[1])
    back_latent = beside(point_t[2], same_bf)
    back_e = beside(conv_t[0], point_t[1])

    for k in range(sets):
        for block in range(per_clip):
            rows = slice(8 * k, 8 * k + 8)
            parted = wave_ref[k, block].astype(F32)
            even_scr[block, rows] = parted[:8]
            odd_scr[block, rows] = parted[8:]
            code_scr[block, rows] = ids_ref[k, block].astype(F32)

    clips = 8 * sets

    def columns_of(length):
        return lax.shift_right_arithmetic(length + 1, 1) + SPARE

    def length_of(clip):
        return len_ref[jnp.bitwise_and(clip, 8), jnp.bitwise_and(clip, 7)]

    def add_clip(c, carry):
        length = length_of(c)
        return carry[0] + columns_of(length), carry[1] + length

    columns, count = lax.fori_loop(0, clips, add_clip, (jnp.int32(0), jnp.int32(0)))
    tiles = lax.div(columns + TILE - 1, jnp.int32(TILE)) + DEPTH

    sub = lax.broadcasted_iota(jnp.int32, (8, LANES), 0)
    lane = lax.broadcasted_iota(jnp.int32, (8, LANES), 1)
    sub_ext = lax.broadcasted_iota(jnp.int32, (8, TILE + 2 * LANES), 0)
    sub_tile = lax.broadcasted_iota(jnp.int32, (8, TILE), 0)
    iota16 = lax.broadcasted_iota(jnp.int32, (16, TILE), 0).astype(F32).astype(BF16)

    table = jnp.concatenate([weight_ref[part, :table_rows] for part in range(2)], axis=0)

    def taps(ext):
        later = moved(ext, 1)
        earlier = moved(ext, -1)
        other = jnp.where(sub_tile == 0, later, jnp.where(sub_tile == 1, earlier, 0.0))
        return jnp.concatenate([moved(ext, 0), other], axis=0)

    def rows_at(clip, place):
        here = (jnp.minimum(place, per_clip - 1), pl.ds(jnp.minimum(clip, clips - 1), 1), slice(None))
        even, odd, code = (
            jnp.broadcast_to(ref[here], (8, LANES)) for ref in (even_scr, odd_scr, code_scr)
        )
        return jnp.where(sub == 0, even, jnp.where(sub == 1, odd, code))

    def known_length(clip):
        return jnp.where(clip < clips, length_of(clip), -frames)

    def fetch(state, slot):
        clip, start = state
        own, following = known_length(clip), known_length(clip + 1)
        cut = jnp.where(clip < clips, columns_of(own), 1 << 20) - start
        inside = lane < cut
        t = jnp.where(inside, start + lane, lane - cut)
        length = jnp.where(inside, own, following)
        turn = jnp.bitwise_and(start, LANES - 1)
        place = lax.shift_right_logical(start, 7)
        ahead = jnp.where(lane >= turn, rows_at(clip, place), rows_at(clip, place + 1))
        ahead = pltpu.roll(ahead, jnp.bitwise_and(LANES - turn, LANES - 1), 1)
        after = pltpu.roll(rows_at(clip + 1, 0), jnp.bitwise_and(cut, LANES - 1), 1)
        values = jnp.where(inside, ahead, after)
        code = jnp.broadcast_to(values[2:3], (8, LANES)).astype(jnp.int32)
        even_ok = 2 * t < length
        odd_ok = 2 * t + 1 < length
        live = t < jnp.minimum(lax.shift_right_arithmetic(length + 1, 1) + REAL, half)
        low = jnp.where(live, jnp.bitwise_and(code, LOW - 1), -1).astype(F32)
        high = lax.shift_right_logical(code, 8).astype(F32)
        known = ((sub == 0) & even_ok) | ((sub == 1) & odd_ok)
        sig_r[slot] = jnp.where(known, values, 0.0)
        msk_r[slot] = jnp.where(known, 1.0, 0.0)
        live_r[slot] = jnp.where(live, 1.0, 0.0)
        me_r[slot] = jnp.where(even_ok, 1.0, 0.0)
        low_r[slot] = stack(low, 2).astype(BF16)
        high_r[slot] = high
        hi_r[slot] = stack(high, 2).astype(BF16)
        done = cut <= LANES
        return jnp.where(done, clip + 1, clip), jnp.where(done, LANES - cut, start + LANES)

    state = (jnp.int32(0), jnp.int32(0))
    for b in range(per_tile + 1):
        state = fetch(state, b)

    def tile_step(names, i, state):
        def block(lag, b):
            return jnp.bitwise_and(i * per_tile - lag + b, slots - 1)

        def load(ref, lag, first=0, last=per_tile):
            return jnp.concatenate([ref[block(lag, b)] for b in range(first, last)], axis=1)

        def load_ext(ref, lag):
            return load(ref, lag, -1, per_tile + 1)

        def keep(ref, lag, value):
            for b in range(per_tile):
                ref[block(lag, b)] = value[:, b * LANES : (b + 1) * LANES]

        def spread(ext, way):
            return jnp.concatenate([moved(ext, d * way) for d in (-REACH, 0, REACH)], axis=0)

        def strips_step():
            sig_ext, live = load_ext(sig_r, 0), load(live_r, 0)
            yield
            strips = (taps(sig_ext) * stack(live, 2)).astype(BF16)
            keep(strips_r, 0, strips)
            yield
            hidden = nn(edge[0], strips)
            yield
            keep(actu_e_r, 0, relu_bf(hidden))

        def lookup_step():
            low16, hi = load(low_r, 0) - iota16, load(high_r, 0)
            onehot = jnp.concatenate(
                [
                    jnp.where(low16 == float(16 * r), jnp.ones((), BF16), jnp.zeros((), BF16))
                    for r in range(LOW // 16)
                ],
                axis=0,
            )
            keep(onehot_r, 0, onehot)
            yield
            picked = nn(table, onehot)
            yield
            parts = [jnp.zeros((8, TILE), F32) for _ in range(width // 8)]
            for h in range(groups):
                here = hi == float(h)
                parts = [
                    jnp.where(here, picked[h * width + 8 * r : h * width + 8 * r + 8], parts[r])
                    for r in range(width // 8)
                ]
            chosen = jnp.concatenate(parts, axis=0).astype(BF16)
            keep(chosen_r, 0, chosen)
            yield
            decin = nn(point[2], chosen)
            yield
            keep(actu_d_r, 0, relu_bf(decin))

        def encode_step():
            lag = LAG
            around = spread(load_ext(actu_e_r, lag), 1)
            yield
            inner = nn(conv[0], around)
            yield
            actp, strips = relu_bf(inner), load(strips_r, lag)
            keep(actp_e_r, lag, actp)
            yield
            latent = nn(latent_w, jnp.concatenate([actp, actp, strips, strips], axis=0))
            chosen, me = load(chosen_r, lag), load(me_r, lag)
            yield
            gap = (latent.astype(BF16).astype(F32) - chosen.astype(F32)) * stack(me, width // 8)
            keep(gapb_r, lag, (gap * (2.0 * COMMIT)).astype(BF16))
            yield
            square = gap * gap
            rows = square[:8]
            for r in range(1, width // 8):
                rows = rows + square[8 * r : 8 * r + 8]
            add_loss(COMMIT * rows)

        def decode_step():
            lag = LAG
            around = spread(load_ext(actu_d_r, lag), 1)
            yield
            inner = nn(conv[1], around)
            yield
            actp, chosen = relu_bf(inner), load(chosen_r, lag)
            keep(actp_d_r, lag, actp)
            yield
            outs = nn(outs_w, jnp.concatenate([actp, chosen], axis=0))
            yield
            keep(outs_r, lag, outs[:16] + outs[16:])

        def scatter_step():
            lag = LAG + per_tile
            hi, gap = load(hi_r, lag), load(gapb_r, lag)
            terms = []
            for h in range(groups):
                here = hi == float(h)
                terms += [
                    jnp.where(here, gap[16 * r : 16 * r + 16], jnp.zeros((), BF16))
                    for r in range(width // 16)
                ]
            onehot = load(onehot_r, lag)
            yield
            found = nt(jnp.concatenate(terms, axis=0), onehot)
            yield
            g_table[...] += found

        def add_loss(rows):
            total = rows[:, :LANES]
            for j in range(1, per_tile):
                total = total + rows[:, j * LANES : (j + 1) * LANES]
            loss_ref[...] += total

        def error_step():
            lag = 2 * LAG
            outs_ext, live_ext = load_ext(outs_r, lag), load_ext(live_r, lag)
            sig_ext, msk_ext = load_ext(sig_r, lag), load_ext(msk_r, lag)
            outs_ext = outs_ext * stack(live_ext, 2)
            shifted = outs_ext[8:]
            wide = TILE + 2 * LANES
            crossed = jnp.where(
                sub_ext == 0, pltpu.roll(shifted, 1, 1), pltpu.roll(shifted, wide - 1, 1)
            )
            error = (outs_ext[:8] + crossed - sig_ext) * msk_ext
            middle = moved(error, 0)
            add_loss(middle * middle)
            yield
            douts = (2.0 * taps(error) * stack(moved(live_ext, 0), 2)).astype(BF16)
            keep(douts_r, lag, douts)
            yield
            dinner = nn(inner_d_w, jnp.concatenate([douts, douts], axis=0))
            actp = load(actp_d_r, lag)
            yield
            keep(dinner_d_r, lag, jnp.where(actp > 0, dinner.astype(BF16), 0))
            yield
            found = nt(jnp.concatenate([actp, load(chosen_r, lag)], axis=0), douts)
            yield
            g_outs[...] += found

        def middle_step():
            lag = 3 * LAG
            around, douts = spread(load_ext(dinner_d_r, lag), -1), load(douts_r, lag)
            yield
            both = nn(back_d, jnp.concatenate([around, douts], axis=0))
            dres = nn(edge[1], douts)
            actu = load(actu_d_r, lag)
            yield
            ddecin = jnp.where(actu > 0, both.astype(BF16), dres.astype(BF16))
            gap = load(gapb_r, lag)
            yield
            back = nn(back_latent, jnp.concatenate([ddecin, gap], axis=0))
            yield
            dlatent = back.astype(BF16)
            keep(dlatent_r, lag, dlatent)
            yield
            dinner = nn(inner_e_w, jnp.concatenate([dlatent, dlatent], axis=0))
            actp = load(actp_e_r, lag)
            yield
            keep(dinner_e_r, lag, jnp.where(actp > 0, dinner.astype(BF16), 0))
            yield
            found = nt(
                jnp.concatenate([actu, load(chosen_r, lag)], axis=0),
                jnp.concatenate([around, ddecin], axis=0),
            )
            yield
            g_mix[1, :width] += found[:width]
            g_mix[1, width : 2 * width, LANES:] += found[width:, LANES:]

        def last_step():
            lag = 4 * LAG
            around = spread(load_ext(dinner_e_r, lag), -1)
            dlatent = load(dlatent_r, lag)
            yield
            both = nn(back_e, jnp.concatenate([around, dlatent], axis=0))
            denc = nn(point_t[1], dlatent)
            actu = load(actu_e_r, lag)
            yield
            dhidden = jnp.where(actu > 0, both.astype(BF16), denc.astype(BF16))
            strips = load(strips_r, lag)
            yield
            found = nt(
                jnp.concatenate([actu, load(actp_e_r, lag), strips], axis=0),
                jnp.concatenate([around, dlatent], axis=0),
            )
            yield
            g_mix[0, :width] += found[:width]
            g_mix[0, width:, LANES:] += found[width:, LANES:]
            yield
            found = nt(dhidden, strips)
            yield
            g_edge[...] += found

        functions = (
            strips_step,
            lookup_step,
            encode_step,
            decode_step,
            scatter_step,
            error_step,
            middle_step,
            last_step,
        )
        steps = {k: functions[k]() for k in names}
        for k in ORDER:
            if k in steps:
                next(steps[k], None)
        for step in steps.values():
            for _ in step:
                pass
        if 0 in names:
            for b in range(per_tile):
                state = fetch(state, block(-LAG, b))
        return state

    ranges = (
        ((0, 1), 0, 1),
        ((0, 1, 2, 3), 1, HEAD),
        (range(8), HEAD, tiles - 4),
        (range(2, 8), tiles - 4, tiles - 3),
        (range(4, 8), tiles - 3, tiles - 2),
        ((6, 7), tiles - 2, tiles - 1),
        ((7,), tiles - 1, tiles),
    )
    for names, begin, end in ranges:
        state = lax.fori_loop(begin, end, functools.partial(tile_step, names), state)

    loss_row = jnp.sum(loss_ref[...], axis=0, keepdims=True)
    count_row = jnp.where(lane == 0, count, 0).astype(F32)
    stats = jnp.where(
        jnp.bitwise_and(sub, 1) == 0, jnp.broadcast_to(loss_row, (8, LANES)), count_row
    )
    def exact(a, b, axis):
        return lax.dot_general(
            a.astype(F32),
            b.astype(F32),
            (((1,), (axis,)), ((), ())),
            preferred_element_type=F32,
            precision=lax.Precision.HIGHEST,
        )

    by_latent = g_mix[0, width : 2 * width, 3 * width :].T
    by_strips = g_mix[0, 2 * width :, 3 * width :].T
    by_inner, by_chosen = g_outs[:width].T, g_outs[width:].T
    points = (
        (
            exact(point_t[1], by_latent, 0),
            exact(by_latent, point[0], 1) + exact(by_strips, edge[0], 1),
        ),
        (g_mix[1, width : 2 * width, 3 * width :].T, exact(edge[1], by_inner, 0)),
    )
    edges = (g_edge[...].T, exact(by_inner, point[3], 1) + exact(by_chosen, point[2], 1))
    rows = groups // 2 * width
    for part in range(2):
        payload_ref[part, :rows] = g_table[part * rows : (part + 1) * rows, :LANES]
        payload_ref[part, rows : 2 * rows] = g_table[part * rows : (part + 1) * rows, LANES:]
        conv_rows = [g_mix[part, :width, k * width : (k + 1) * width].T for k in range(3)]
        edge_rows = jnp.concatenate([edges[part], jnp.zeros((width - 16, width), F32)], axis=0)
        after = 2 * rows
        for pair in (
            conv_rows[:2],
            (conv_rows[2], edge_rows),
            points[part],
        ):
            payload_ref[part, after : after + width] = jnp.concatenate(pair, axis=1)
            after += width
        payload_ref[part, after : after + 8] = stats
        after += 8
        rest = payload_ref.shape[1] - after
        if rest:
            payload_ref[part, after:] = jnp.zeros((rest, LANES), F32)


def net(rows, lengths, wave, codes, weights):
    sets, per_clip = wave.shape[:2]
    clips = 8 * sets
    width = 64
    table_rows = 2 * (weights.shape[1] - 4 * width - 16)
    slots = SLOTS * TILE // LANES
    vmem = pl.BlockSpec(memory_space=pltpu.VMEM)

    def ring(rows, dtype):
        return pltpu.VMEM((slots, rows, LANES), dtype)

    return pl.pallas_call(
        net_kernel,
        out_shape=jax.ShapeDtypeStruct((2, rows, LANES), F32),
        in_specs=[pl.BlockSpec(memory_space=pl.ANY)] * 4,
        out_specs=vmem,
        scratch_shapes=[
            pltpu.SMEM(lengths.shape, lengths.dtype),
            pltpu.VMEM(wave.shape, wave.dtype),
            pltpu.VMEM(codes.shape, codes.dtype),
            pltpu.VMEM(weights.shape, weights.dtype),
            pltpu.SemaphoreType.DMA((4,)),
            pltpu.VMEM((2, 2 * width + 16, 4 * width), F32),
            pltpu.VMEM((2 * width, 16), F32),
            pltpu.VMEM((width, 16), F32),
            pltpu.VMEM((table_rows, LOW), F32),
            pltpu.VMEM((8, LANES), F32),
            pltpu.VMEM((per_clip, clips, LANES), F32),
            pltpu.VMEM((per_clip, clips, LANES), F32),
            pltpu.VMEM((per_clip, clips, LANES), F32),
            *(ring(8, F32) for _ in range(4)),
            ring(16, BF16),
            ring(8, F32),
            *(ring(16, BF16) for _ in range(2)),
            ring(LOW, BF16),
            *(ring(width, BF16) for _ in range(6)),
            ring(16, F32),
            ring(16, BF16),
            *(ring(width, BF16) for _ in range(3)),
        ],
        compiler_params=pltpu.CompilerParams(vmem_limit_bytes=60 * 2**20),
    )(lengths, wave, codes, weights)


def remote(src, dst, send, recv, to):
    return pltpu.make_async_remote_copy(
        src_ref=src, dst_ref=dst, send_sem=send, recv_sem=recv, device_id=to, device_id_type=MESH
    )


def share_kernel(items, *refs):
    sources, (len_out, wave_out, ids_out, weight_out), inputs = refs[:7], refs[7:11], refs[11:18]
    len_ref, wave_ref, ids_ref, conv_ref, point_ref, edge_ref, table_ref = inputs
    len_scr, wave_scr, ids_scr, weight_scr, sems, load_sems = refs[18:]
    loads = [
        pltpu.make_async_copy(source, place, load_sems.at[k])
        for k, (source, place) in enumerate(zip(sources, inputs))
    ]
    for load in loads:
        load.start()
    item = lax.axis_index("item")
    pipe = lax.axis_index("pipe")
    partner = (item, 1 - pipe)
    mirror = (items - 1 - item, pipe)
    per_clip = wave_out.shape[1]
    width = conv_ref.shape[1]
    table_rows = weight_scr.shape[1] - 4 * width - 16

    barrier = pltpu.get_barrier_semaphore()
    for other in (partner, mirror):
        pl.semaphore_signal(barrier, inc=1, device_id=other, device_id_type=MESH)

    row_at = lax.broadcasted_iota(jnp.int32, (2 * LANES, 2 * LANES), 0)
    col_at = lax.broadcasted_iota(jnp.int32, (2 * LANES, 2 * LANES), 1)
    wanted = jnp.where(col_at < LANES, 2 * col_at, 2 * (col_at - LANES) + 1)
    split = jnp.where(row_at == wanted, 1.0, 0.0).astype(BF16)
    on_first = pipe == 0
    for load in loads[:3]:
        load.wait()
    lane = lax.broadcasted_iota(jnp.int32, (8, LANES), 1)
    kept = jnp.zeros((8, LANES), jnp.int32)
    given = kept
    for k in range(8):
        kept = jnp.where(lane == k, jnp.where(on_first, len_ref[k], len_ref[8 + k]), kept)
        given = jnp.where(lane == k, jnp.where(on_first, len_ref[24 + k], len_ref[16 + k]), given)
    len_out[:8] = kept
    len_scr[0] = given
    clips = wave_ref.shape[0]
    strips = [wave_ref[:, k * 2 * LANES : (k + 1) * 2 * LANES] for k in range(per_clip)]
    parted = nn(jnp.concatenate(strips, axis=0), split)

    def chosen(values, first, second):
        return jnp.where(on_first, values[8 * first :][:8], values[8 * second :][:8])

    def both(values, first, second):
        pair = [
            chosen(side, first, second) for side in (values[:, :LANES], values[:, LANES:])
        ]
        return jnp.concatenate(pair, axis=0).astype(BF16)

    codes = [ids_ref[:, k * LANES : (k + 1) * LANES] for k in range(per_clip)]
    for k in range(per_clip):
        values = parted[clips * k : clips * (k + 1)]
        wave_scr[0, k] = both(values, 3, 2)
        wave_out[0, k] = both(values, 0, 1)
        ids_out[0, k] = chosen(codes[k], 0, 1)
    for k in range(per_clip // 2):
        pair = [chosen(codes[2 * k + j], 3, 2) for j in range(2)]
        ids_scr[0, k] = jnp.concatenate(pair, axis=0).astype(jnp.int16)

    pl.semaphore_wait(barrier, 2)
    copies = [
        remote(ref.at[0], ref.at[1], sems.at[2 * k], sems.at[2 * k + 1], mirror)
        for k, ref in enumerate((len_scr, wave_scr, ids_scr))
    ]
    for copy in copies:
        copy.start()

    for load in loads[3:]:
        load.wait()
    groups = table_rows // width
    for h in range(groups):
        weight_scr[0, h * width : (h + 1) * width] = table_ref[:, h * LOW : (h + 1) * LOW].astype(
            BF16
        )
    blank = jnp.zeros((width, LOW - 3 * width), F32)
    conv = conv_ref[0]
    conv_t = [conv[:, k * width : (k + 1) * width].T for k in range(3)]
    points = [point_ref[0, 0], point_ref[0, 1]]
    edge = edge_ref[0]
    empty = jnp.zeros((6, width), F32)
    edge_t = jnp.concatenate([edge[1:3], empty, edge[3:], edge[:1], empty], axis=0)
    edge_square = jnp.concatenate([edge_t, jnp.zeros((width - 16, width), F32)], axis=0).T
    after = table_rows
    for pieces in (
        [conv, blank],
        conv_t + [blank],
        points + [value.T for value in points],
        [edge_square, jnp.zeros((width, LOW - width), F32)],
        [edge_t, jnp.zeros((16, LOW - width), F32)],
    ):
        value = jnp.concatenate(pieces, axis=1).astype(BF16)
        weight_scr[0, after : after + value.shape[0]] = value
        after += value.shape[0]
    over = remote(weight_scr.at[0], weight_scr.at[1], sems.at[6], sems.at[7], partner)
    over.start()
    weight_out[pipe] = weight_scr[0]
    over.wait()
    weight_out[1 - pipe] = weight_scr[1]
    for copy in copies:
        copy.wait()
    len_out[8:] = len_scr[1]
    wave_out[1] = wave_scr[1]
    for k in range(per_clip // 2):
        pair = ids_scr[1, k].astype(jnp.int32)
        ids_out[1, 2 * k], ids_out[1, 2 * k + 1] = pair[:8], pair[8:]


def shared(items, lengths, waveform, code_ids, conv, point, edge, table):
    per_clip = code_ids.shape[1] // LANES
    width = conv.shape[1]
    weight_rows = table.shape[1] // LOW * width + 4 * width + 16
    vmem = pl.BlockSpec(memory_space=pltpu.VMEM)
    wave_shape = (2, per_clip, 16, LANES)
    ids_shape = (2, per_clip, 8, LANES)
    weight_shape = (2, weight_rows, LOW)
    return pl.pallas_call(
        functools.partial(share_kernel, items),
        out_shape=(
            jax.ShapeDtypeStruct((16, LANES), jnp.int32),
            jax.ShapeDtypeStruct(wave_shape, BF16),
            jax.ShapeDtypeStruct(ids_shape, jnp.int32),
            jax.ShapeDtypeStruct(weight_shape, BF16),
        ),
        in_specs=[pl.BlockSpec(memory_space=pl.ANY)] * 7,
        out_specs=(vmem,) * 4,
        scratch_shapes=[pltpu.SMEM(lengths.shape, jnp.int32)]
        + [
            pltpu.VMEM(value.shape, value.dtype)
            for value in (waveform, code_ids, conv, point, edge, table)
        ]
        + [
            pltpu.VMEM((2, 8, LANES), jnp.int32),
            pltpu.VMEM(wave_shape, BF16),
            pltpu.VMEM((2, per_clip // 2, 16, LANES), jnp.int16),
            pltpu.VMEM(weight_shape, BF16),
            pltpu.SemaphoreType.DMA((8,)),
            pltpu.SemaphoreType.DMA((7,)),
        ],
        compiler_params=pltpu.CompilerParams(
            collective_id=0, has_side_effects=True, vmem_limit_bytes=60 * 2**20
        ),
    )(lengths, waveform, code_ids, conv, point, edge, table)


def sum_kernel(
    items,
    stats_row,
    payload_ref,
    sum_ref,
    own,
    crossed,
    part,
    landed,
    whole,
    own_sem,
    cross_send,
    cross_recv,
    out_send,
    out_recv,
    back_send,
    back_recv,
):
    item = lax.axis_index("item")
    pipe = lax.axis_index("pipe")
    partner = (item, 1 - pipe)
    piece = part.shape[1]

    def peer(d):
        if items & (items - 1):
            return lax.rem(item + d, items)
        return jnp.bitwise_and(item + d, items - 1)

    def rows_of(k):
        return pl.ds(pl.multiple_of(k * piece, piece), piece)

    load = pltpu.make_async_copy(payload_ref.at[pipe], own, own_sem)
    load.start()
    barrier = pltpu.get_barrier_semaphore()
    pl.semaphore_signal(barrier, inc=1, device_id=partner, device_id_type=MESH)

    @pl.loop(1, items)
    def _(d):
        pl.semaphore_signal(barrier, inc=1, device_id=(peer(d), pipe), device_id_type=MESH)

    pl.semaphore_wait(barrier, items)

    def cross_copy(k):
        return remote(
            payload_ref.at[1 - pipe, rows_of(k)], crossed.at[rows_of(k)],
            cross_send.at[k], cross_recv.at[k], partner,
        )

    @pl.loop(1, items)
    def _(d):
        cross_copy(peer(d)).start()

    cross_copy(item).start()
    load.wait()

    def out_copy(to, place):
        return remote(
            part.at[to], landed.at[place], out_send.at[to], out_recv.at[place], (to, pipe)
        )

    @pl.loop(1, items)
    def _(d):
        to = peer(d)
        cross_copy(to).wait_recv()
        part[to] = (own[rows_of(to)] + crossed[rows_of(to)]).astype(BF16)
        out_copy(to, item).start()

    cross_copy(item).wait_recv()
    total = own[rows_of(item)] + crossed[rows_of(item)]
    stats = own[stats_row : stats_row + 8] + crossed[stats_row : stats_row + 8]
    high = stats.astype(BF16).astype(F32)
    middle = (stats - high).astype(BF16).astype(F32)
    low = stats - high - middle
    sub = lax.broadcasted_iota(jnp.int32, (8, LANES), 0)
    message = jnp.where(sub < 2, high, jnp.where(sub < 4, middle, jnp.where(sub < 6, low, 0.0)))
    whole[item, piece:] = jnp.concatenate([message, jnp.zeros_like(message)], axis=0).astype(BF16)

    def take(d, total):
        source = peer(d)
        out_copy(source, source).wait_recv()
        return total + landed[source].astype(F32)

    total = lax.fori_loop(1, items, take, total)
    whole[item, :piece] = total.astype(BF16)

    def back_copy(place, to):
        return remote(
            whole.at[place], whole.at[place], back_send.at[to], back_recv.at[place], (to, pipe)
        )

    @pl.loop(1, items)
    def _(d):
        back_copy(item, peer(d)).start()

    sum_ref[rows_of(item)] = whole[item, :piece].astype(F32)

    @pl.loop(1, items)
    def _(d):
        to = peer(d)
        cross_copy(to).wait_send()
        out_copy(to, item).wait_send()

    cross_copy(item).wait_send()

    def gather(d, stats):
        source = peer(d)
        back_copy(source, source).wait_recv()
        sum_ref[rows_of(source)] = whole[source, :piece].astype(F32)
        return stats + whole[source, piece:].astype(F32)[:8]

    stats = lax.fori_loop(1, items, gather, whole[item, piece:].astype(F32)[:8])
    sum_ref[stats_row : stats_row + 8] = stats

    @pl.loop(1, items)
    def _(d):
        back_copy(item, peer(d)).wait_send()


def summed(items, stats_row, payload):
    rows = payload.shape[1]
    piece = rows // items
    vmem = pl.BlockSpec(memory_space=pltpu.VMEM)
    sems = pltpu.SemaphoreType.DMA((items,))
    return pl.pallas_call(
        functools.partial(sum_kernel, items, stats_row),
        out_shape=jax.ShapeDtypeStruct((rows, LANES), F32),
        in_specs=[pl.BlockSpec(memory_space=pl.ANY)],
        out_specs=vmem,
        scratch_shapes=[
            pltpu.VMEM((rows, LANES), F32),
            pltpu.VMEM((rows, LANES), F32),
            pltpu.VMEM((items, piece, LANES), BF16),
            pltpu.VMEM((items, piece, LANES), BF16),
            pltpu.VMEM((items, piece + 16, LANES), BF16),
            pltpu.SemaphoreType.DMA,
        ]
        + [sems] * 6,
        compiler_params=pltpu.CompilerParams(
            collective_id=1, has_side_effects=True, vmem_limit_bytes=16 * 2**20
        ),
    )(payload)


def update_kernel(*refs):
    rate_net, rate_code, sum_ref = refs[:3]
    states = refs[3:15]
    loss_ref = refs[15]
    results = refs[16:]
    width = states[0].shape[1]
    groups = states[3].shape[1] // LOW
    rows = groups * width
    stats_row = 2 * rows + 3 * width
    stats = sum_ref[stats_row : stats_row + 8]
    odd = jnp.bitwise_and(lax.broadcasted_iota(jnp.int32, stats.shape, 0), 1) == 1
    counts = jnp.where(odd, stats, 0.0)
    loss_ref[0] = jnp.sum(jnp.where(odd, 0.0, stats)) / jnp.sum(counts)
    scale = 1.0 / jnp.sum(counts, keepdims=True)

    def step(kind, place, grad, rate):
        weight_ref, moment_ref, average_ref = (states[4 * j + kind] for j in range(3))
        new_ref, moment_new_ref, average_new_ref, copy_ref = results[4 * kind : 4 * kind + 4]
        grad = grad * scale
        moment = MOMENTUM * moment_ref[place] + grad
        weight = weight_ref[place] - rate * (grad + MOMENTUM * moment)
        new_ref[place] = weight
        moment_new_ref[place] = moment
        average_new_ref[place] = AVERAGE * average_ref[place] + (1.0 - AVERAGE) * weight
        copy_ref[place] = weight.astype(BF16)

    for h in range(groups):
        for side in range(LOW // LANES):
            start = h * LOW + side * LANES
            grad = sum_ref[side * rows + h * width : side * rows + (h + 1) * width]
            place = (slice(None), slice(start, start + LANES))
            step(3, place, -grad, rate_code[0])
    first, second, third = (
        sum_ref[2 * rows + k * width : 2 * rows + (k + 1) * width] for k in range(3)
    )
    rate = rate_net[0]
    step(0, 0, jnp.concatenate([first, second[:, :width]], axis=1), rate)
    step(1, (0, 0), third[:, :width], rate)
    step(1, (0, 1), third[:, width:], rate)
    edge = [second[k : k + 1, width:] for k in (9, 0, 1, 8)]
    step(2, 0, jnp.concatenate(edge, axis=0), rate)


def updated(rates, sums, states):
    smem = pl.BlockSpec(memory_space=pltpu.SMEM)
    shapes = [jax.ShapeDtypeStruct((1,), F32)]
    for weight in states[:4]:
        shapes += [jax.ShapeDtypeStruct(weight.shape, F32)] * 3
        shapes += [jax.ShapeDtypeStruct(weight.shape, BF16)]
    def block(value):
        return pl.BlockSpec(value.shape, lambda i: (0,) * len(value.shape))

    return pl.pallas_call(
        update_kernel,
        grid=(1,),
        out_shape=tuple(shapes),
        in_specs=[smem] * 2 + [block(value) for value in (sums, *states)],
        out_specs=(smem,) + tuple(block(value) for value in shapes[1:]),
        compiler_params=pltpu.CompilerParams(vmem_limit_bytes=24 * 2**20),
    )(*rates, sums, *states)


def per_device(
    waveform,
    lengths,
    code_ids,
    conv_w,
    point_w,
    edge_w,
    codebook,
    conv_mom,
    point_mom,
    edge_mom,
    code_mom,
    conv_avg,
    point_avg,
    edge_avg,
    code_avg,
    rate_net,
    rate_code,
):
    width = conv_w.shape[1]
    items = lax.axis_size("item")
    edge_w, edge_mom, edge_avg = (jnp.swapaxes(v, 1, 2) for v in (edge_w, edge_mom, edge_avg))
    codebook, code_mom, code_avg = (v.T for v in (codebook, code_mom, code_avg))
    rows = 2 * (codebook.shape[1] // LOW) * width + 3 * width
    piece = -(-(rows + 8) // (16 * items)) * 16
    own_inputs = shared(items, lengths, waveform, code_ids, conv_w, point_w, edge_w, codebook)
    payload = net(piece * items, *own_inputs)
    sums = summed(items, rows, payload)
    states = (
        conv_w, point_w, edge_w, codebook,
        conv_mom, point_mom, edge_mom, code_mom,
        conv_avg, point_avg, edge_avg, code_avg,
    )
    loss, *rest = updated((rate_net, rate_code), sums, states)
    edges = (jnp.swapaxes(v, 1, 2) for v in rest[8:12])
    return (loss.reshape(()), *rest[:8], *edges, *(v.T for v in rest[12:]))


def solution(mesh):
    weights = (
        P("pipe", None, None),
        P("pipe", None, None, None),
        P("pipe", None, None),
        P("pipe", None),
    )
    return jax.shard_map(
        per_device,
        mesh=mesh,
        in_specs=(P("item", None), P("item"), P("item", None), *weights, *weights, *weights, P(), P()),
        out_specs=(P(),) + tuple(spec for spec in weights for _ in range(4)),
        check_vma=False,
    )
```

```python
import functools

import jax
import jax.numpy as jnp
from jax import lax
from jax.experimental import pallas as pl
from jax.experimental.pallas import tpu as pltpu
from jax.sharding import PartitionSpec as P

REACH = 3
COMMIT = 0.02
MOMENTUM = 0.9
AVERAGE = 0.99

LANES = 128
TILE = 512
SLOTS = 8
LAG = TILE // LANES + 1
HEAD = 2
DEPTH = -(-4 * LAG * LANES // TILE)
LOW = 256
SPARE = 8
REAL = 4

MESH = pl.DeviceIdType.MESH
ORDER = (1, 6, 3, 2, 4, 7, 5, 0, 1, 6, 3, 2, 4, 7, 5, 0, 1, 6, 3, 2, 4, 7, 5, 0, 1, 6, 3, 2, 7, 5, 0, 1, 6, 3, 2, 7, 5, 6, 2, 7, 5, 6, 7, 6, 6)
F32 = jnp.float32
BF16 = jnp.bfloat16


def nn(a, b):
    return lax.dot_general(a, b, (((1,), (0,)), ((), ())), preferred_element_type=F32)


def nt(a, b):
    return lax.dot_general(a, b, (((1,), (1,)), ((), ())), preferred_element_type=F32)


def moved(ext, distance):
    width = ext.shape[1]
    turned = ext if distance == 0 else pltpu.roll(ext, (-distance) % width, 1)
    return turned[:, LANES : width - LANES]


def relu_bf(values):
    return jnp.maximum(values, 0.0).astype(BF16)


def stack(rows, times):
    return jnp.concatenate([rows] * times, axis=0)


def net_kernel(
    len_src,
    wave_src,
    ids_src,
    weight_src,
    payload_ref,
    len_ref,
    wave_ref,
    ids_ref,
    weight_ref,
    load_sems,
    g_mix,
    g_outs,
    g_edge,
    g_table,
    loss_ref,
    even_scr,
    odd_scr,
    code_scr,
    sig_r,
    msk_r,
    live_r,
    me_r,
    low_r,
    high_r,
    hi_r,
    strips_r,
    onehot_r,
    actu_e_r,
    chosen_r,
    actu_d_r,
    actp_e_r,
    actp_d_r,
    gapb_r,
    outs_r,
    douts_r,
    dinner_d_r,
    dlatent_r,
    dinner_e_r,
):
    pairs = (
        (len_src, len_ref), (wave_src, wave_ref), (ids_src, ids_ref), (weight_src, weight_ref)
    )
    loads = [
        pltpu.make_async_copy(source, place, load_sems.at[k])
        for k, (source, place) in enumerate(pairs)
    ]
    for load in loads:
        load.start()
    sets, per_clip = wave_ref.shape[:2]
    half = per_clip * LANES
    frames = 2 * half
    width = 64
    groups = 2 * (weight_ref.shape[1] - 4 * width - 16) // width
    table_rows = groups // 2 * width
    per_tile = TILE // LANES

    rings = (
        sig_r, msk_r, live_r, me_r, low_r, high_r, hi_r, strips_r, onehot_r, actu_e_r, chosen_r,
        actu_d_r, actp_e_r, actp_d_r, gapb_r, outs_r, douts_r, dinner_d_r, dlatent_r, dinner_e_r,
    )
    slots = SLOTS * per_tile

    @pl.loop(slots - (4 * LAG + 1 - HEAD * per_tile), slots)
    def _(slot):
        for ref in rings:
            ref[slot] = jnp.zeros(ref.shape[1:], ref.dtype)

    for ref in (g_mix, g_outs, g_edge, g_table, loss_ref):
        ref[...] = jnp.zeros(ref.shape, ref.dtype)

    for load in loads:
        load.wait()

    def weight(part, start, rows, first, columns):
        start += table_rows
        return weight_ref[part, start : start + rows, first : first + columns]

    conv = [weight(part, 0, width, 0, 3 * width) for part in range(2)]
    conv_t = [weight(part, width, width, 0, 3 * width) for part in range(2)]
    point = [weight(k // 2, 2 * width, width, k % 2 * width, width) for k in range(4)]
    point_t = [weight(k // 2, 2 * width, width, (2 + k % 2) * width, width) for k in range(4)]
    edge = [weight(part, 3 * width, width, 0, 16) for part in range(2)]
    edge_t = [weight(part, 4 * width, 16, 0, width) for part in range(2)]

    def beside(*parts):
        return jnp.concatenate(parts, axis=1)

    same = lax.broadcasted_iota(jnp.int32, (width, width), 0) == lax.broadcasted_iota(
        jnp.int32, (width, width), 1
    )
    same_bf = jnp.where(same, 1.0, 0.0).astype(BF16)

    def halves(value):
        high = value.astype(BF16)
        return high, (value - high.astype(F32)).astype(BF16)

    latent_w = beside(*halves(nn(point[1], point[0])), *halves(nn(point[1], edge[0])))
    outs_w = jnp.concatenate(halves(nn(edge_t[1], beside(point[3], point[2]))), axis=0)
    inner_d_w = beside(*halves(nn(point_t[3], edge[1])))
    inner_e_w = beside(*halves(nn(point_t[0], point_t[1])))
    back_d = beside(conv_t[1], edge[1])
    back_latent = beside(point_t[2], same_bf)
    back_e = beside(conv_t[0], point_t[1])

    for k in range(sets):
        for block in range(per_clip):
            rows = slice(8 * k, 8 * k + 8)
            parted = wave_ref[k, block].astype(F32)
            even_scr[block, rows] = parted[:8]
            odd_scr[block, rows] = parted[8:]
            code_scr[block, rows] = ids_ref[k, block].astype(F32)

    clips = 8 * sets

    def columns_of(length):
        return lax.shift_right_arithmetic(length + 1, 1) + SPARE

    def length_of(clip):
        return len_ref[jnp.bitwise_and(clip, 8), jnp.bitwise_and(clip, 7)]

    def add_clip(c, carry):
        length = length_of(c)
        return carry[0] + columns_of(length), carry[1] + length

    columns, count = lax.fori_loop(0, clips, add_clip, (jnp.int32(0), jnp.int32(0)))
    tiles = lax.div(columns + TILE - 1, jnp.int32(TILE)) + DEPTH

    sub = lax.broadcasted_iota(jnp.int32, (8, LANES), 0)
    lane = lax.broadcasted_iota(jnp.int32, (8, LANES), 1)
    sub_ext = lax.broadcasted_iota(jnp.int32, (8, TILE + 2 * LANES), 0)
    sub_tile = lax.broadcasted_iota(jnp.int32, (8, TILE), 0)
    iota16 = lax.broadcasted_iota(jnp.int32, (16, TILE), 0).astype(F32).astype(BF16)

    table = jnp.concatenate([weight_ref[part, :table_rows] for part in range(2)], axis=0)

    def taps(ext):
        later = moved(ext, 1)
        earlier = moved(ext, -1)
        other = jnp.where(sub_tile == 0, later, jnp.where(sub_tile == 1, earlier, 0.0))
        return jnp.concatenate([moved(ext, 0), other], axis=0)

    def rows_at(clip, place):
        here = (jnp.minimum(place, per_clip - 1), pl.ds(jnp.minimum(clip, clips - 1), 1), slice(None))
        even, odd, code = (
            jnp.broadcast_to(ref[here], (8, LANES)) for ref in (even_scr, odd_scr, code_scr)
        )
        return jnp.where(sub == 0, even, jnp.where(sub == 1, odd, code))

    def known_length(clip):
        return jnp.where(clip < clips, length_of(clip), -frames)

    def fetch(state, slot):
        clip, start = state
        own, following = known_length(clip), known_length(clip + 1)
        cut = jnp.where(clip < clips, columns_of(own), 1 << 20) - start
        inside = lane < cut
        t = jnp.where(inside, start + lane, lane - cut)
        length = jnp.where(inside, own, following)
        turn = jnp.bitwise_and(start, LANES - 1)
        place = lax.shift_right_logical(start, 7)
        ahead = jnp.where(lane >= turn, rows_at(clip, place), rows_at(clip, place + 1))
        ahead = pltpu.roll(ahead, jnp.bitwise_and(LANES - turn, LANES - 1), 1)
        after = pltpu.roll(rows_at(clip + 1, 0), jnp.bitwise_and(cut, LANES - 1), 1)
        values = jnp.where(inside, ahead, after)
        code = jnp.broadcast_to(values[2:3], (8, LANES)).astype(jnp.int32)
        even_ok = 2 * t < length
        odd_ok = 2 * t + 1 < length
        live = t < jnp.minimum(lax.shift_right_arithmetic(length + 1, 1) + REAL, half)
        low = jnp.where(live, jnp.bitwise_and(code, LOW - 1), -1).astype(F32)
        high = lax.shift_right_logical(code, 8).astype(F32)
        known = ((sub == 0) & even_ok) | ((sub == 1) & odd_ok)
        sig_r[slot] = jnp.where(known, values, 0.0)
        msk_r[slot] = jnp.where(known, 1.0, 0.0)
        live_r[slot] = jnp.where(live, 1.0, 0.0)
        me_r[slot] = jnp.where(even_ok, 1.0, 0.0)
        low_r[slot] = stack(low, 2).astype(BF16)
        high_r[slot] = high
        hi_r[slot] = stack(high, 2).astype(BF16)
        done = cut <= LANES
        return jnp.where(done, clip + 1, clip), jnp.where(done, LANES - cut, start + LANES)

    state = (jnp.int32(0), jnp.int32(0))
    for b in range(per_tile + 1):
        state = fetch(state, b)

    def tile_step(names, i, state):
        def block(lag, b):
            return jnp.bitwise_and(i * per_tile - lag + b, slots - 1)

        def load(ref, lag, first=0, last=per_tile):
            return jnp.concatenate([ref[block(lag, b)] for b in range(first, last)], axis=1)

        def load_ext(ref, lag):
            return load(ref, lag, -1, per_tile + 1)

        def keep(ref, lag, value):
            for b in range(per_tile):
                ref[block(lag, b)] = value[:, b * LANES : (b + 1) * LANES]

        def spread(ext, way):
            return jnp.concatenate([moved(ext, d * way) for d in (-REACH, 0, REACH)], axis=0)

        def strips_step():
            sig_ext, live = load_ext(sig_r, 0), load(live_r, 0)
            yield
            strips = (taps(sig_ext) * stack(live, 2)).astype(BF16)
            keep(strips_r, 0, strips)
            yield
            hidden = nn(edge[0], strips)
            yield
            keep(actu_e_r, 0, relu_bf(hidden))

        def lookup_step():
            low16, hi = load(low_r, 0) - iota16, load(high_r, 0)
            onehot = jnp.concatenate(
                [
                    jnp.where(low16 == float(16 * r), jnp.ones((), BF16), jnp.zeros((), BF16))
                    for r in range(LOW // 16)
                ],
                axis=0,
            )
            keep(onehot_r, 0, onehot)
            yield
            picked = nn(table, onehot)
            yield
            parts = [jnp.zeros((8, TILE), F32) for _ in range(width // 8)]
            for h in range(groups):
                here = hi == float(h)
                parts = [
                    jnp.where(here, picked[h * width + 8 * r : h * width + 8 * r + 8], parts[r])
                    for r in range(width // 8)
                ]
            chosen = jnp.concatenate(parts, axis=0).astype(BF16)
            keep(chosen_r, 0, chosen)
            yield
            decin = nn(point[2], chosen)
            yield
            keep(actu_d_r, 0, relu_bf(decin))

        def encode_step():
            lag = LAG
            around = spread(load_ext(actu_e_r, lag), 1)
            yield
            inner = nn(conv[0], around)
            yield
            actp, strips = relu_bf(inner), load(strips_r, lag)
            keep(actp_e_r, lag, actp)
            yield
            latent = nn(latent_w, jnp.concatenate([actp, actp, strips, strips], axis=0))
            chosen, me = load(chosen_r, lag), load(me_r, lag)
            yield
            gap = (latent.astype(BF16).astype(F32) - chosen.astype(F32)) * stack(me, width // 8)
            keep(gapb_r, lag, (gap * (2.0 * COMMIT)).astype(BF16))
            yield
            square = gap * gap
            rows = square[:8]
            for r in range(1, width // 8):
                rows = rows + square[8 * r : 8 * r + 8]
            add_loss(COMMIT * rows)

        def decode_step():
            lag = LAG
            around = spread(load_ext(actu_d_r, lag), 1)
            yield
            inner = nn(conv[1], around)
            yield
            actp, chosen = relu_bf(inner), load(chosen_r, lag)
            keep(actp_d_r, lag, actp)
            yield
            outs = nn(outs_w, jnp.concatenate([actp, chosen], axis=0))
            yield
            keep(outs_r, lag, outs[:16] + outs[16:])

        def scatter_step():
            lag = LAG + per_tile
            hi, gap = load(hi_r, lag), load(gapb_r, lag)
            terms = []
            for h in range(groups):
                here = hi == float(h)
                terms += [
                    jnp.where(here, gap[16 * r : 16 * r + 16], jnp.zeros((), BF16))
                    for r in range(width // 16)
                ]
            onehot = load(onehot_r, lag)
            yield
            found = nt(jnp.concatenate(terms, axis=0), onehot)
            yield
            g_table[...] += found

        def add_loss(rows):
            total = rows[:, :LANES]
            for j in range(1, per_tile):
                total = total + rows[:, j * LANES : (j + 1) * LANES]
            loss_ref[...] += total

        def error_step():
            lag = 2 * LAG
            outs_ext, live_ext = load_ext(outs_r, lag), load_ext(live_r, lag)
            sig_ext, msk_ext = load_ext(sig_r, lag), load_ext(msk_r, lag)
            outs_ext = outs_ext * stack(live_ext, 2)
            shifted = outs_ext[8:]
            wide = TILE + 2 * LANES
            crossed = jnp.where(
                sub_ext == 0, pltpu.roll(shifted, 1, 1), pltpu.roll(shifted, wide - 1, 1)
            )
            error = (outs_ext[:8] + crossed - sig_ext) * msk_ext
            middle = moved(error, 0)
            add_loss(middle * middle)
            yield
            douts = (2.0 * taps(error) * stack(moved(live_ext, 0), 2)).astype(BF16)
            keep(douts_r, lag, douts)
            yield
            dinner = nn(inner_d_w, jnp.concatenate([douts, douts], axis=0))
            actp = load(actp_d_r, lag)
            yield
            keep(dinner_d_r, lag, jnp.where(actp > 0, dinner.astype(BF16), 0))
            yield
            found = nt(jnp.concatenate([actp, load(chosen_r, lag)], axis=0), douts)
            yield
            g_outs[...] += found

        def middle_step():
            lag = 3 * LAG
            around, douts = spread(load_ext(dinner_d_r, lag), -1), load(douts_r, lag)
            yield
            both = nn(back_d, jnp.concatenate([around, douts], axis=0))
            dres = nn(edge[1], douts)
            actu = load(actu_d_r, lag)
            yield
            ddecin = jnp.where(actu > 0, both.astype(BF16), dres.astype(BF16))
            gap = load(gapb_r, lag)
            yield
            back = nn(back_latent, jnp.concatenate([ddecin, gap], axis=0))
            yield
            dlatent = back.astype(BF16)
            keep(dlatent_r, lag, dlatent)
            yield
            dinner = nn(inner_e_w, jnp.concatenate([dlatent, dlatent], axis=0))
            actp = load(actp_e_r, lag)
            yield
            keep(dinner_e_r, lag, jnp.where(actp > 0, dinner.astype(BF16), 0))
            yield
            found = nt(
                jnp.concatenate([actu, load(chosen_r, lag)], axis=0),
                jnp.concatenate([around, ddecin], axis=0),
            )
            yield
            g_mix[1, :width] += found[:width]
            g_mix[1, width : 2 * width, LANES:] += found[width:, LANES:]

        def last_step():
            lag = 4 * LAG
            around = spread(load_ext(dinner_e_r, lag), -1)
            dlatent = load(dlatent_r, lag)
            yield
            both = nn(back_e, jnp.concatenate([around, dlatent], axis=0))
            denc = nn(point_t[1], dlatent)
            actu = load(actu_e_r, lag)
            yield
            dhidden = jnp.where(actu > 0, both.astype(BF16), denc.astype(BF16))
            strips = load(strips_r, lag)
            yield
            found = nt(
                jnp.concatenate([actu, load(actp_e_r, lag), strips], axis=0),
                jnp.concatenate([around, dlatent], axis=0),
            )
            yield
            g_mix[0, :width] += found[:width]
            g_mix[0, width:, LANES:] += found[width:, LANES:]
            yield
            found = nt(dhidden, strips)
            yield
            g_edge[...] += found

        functions = (
            strips_step,
            lookup_step,
            encode_step,
            decode_step,
            scatter_step,
            error_step,
            middle_step,
            last_step,
        )
        steps = {k: functions[k]() for k in names}
        for k in ORDER:
            if k in steps:
                next(steps[k], None)
        for step in steps.values():
            for _ in step:
                pass
        if 0 in names:
            for b in range(per_tile):
                state = fetch(state, block(-LAG, b))
        return state

    ranges = (
        ((0, 1), 0, 1),
        ((0, 1, 2, 3), 1, HEAD),
        (range(8), HEAD, tiles - 4),
        (range(2, 8), tiles - 4, tiles - 3),
        (range(4, 8), tiles - 3, tiles - 2),
        ((6, 7), tiles - 2, tiles - 1),
        ((7,), tiles - 1, tiles),
    )
    for names, begin, end in ranges:
        state = lax.fori_loop(begin, end, functools.partial(tile_step, names), state)

    loss_row = jnp.sum(loss_ref[...], axis=0, keepdims=True)
    count_row = jnp.where(lane == 0, count, 0).astype(F32)
    stats = jnp.where(
        jnp.bitwise_and(sub, 1) == 0, jnp.broadcast_to(loss_row, (8, LANES)), count_row
    )
    def exact(a, b, axis):
        return lax.dot_general(
            a.astype(F32),
            b.astype(F32),
            (((1,), (axis,)), ((), ())),
            preferred_element_type=F32,
            precision=lax.Precision.HIGHEST,
        )

    by_latent = g_mix[0, width : 2 * width, 3 * width :].T
    by_strips = g_mix[0, 2 * width :, 3 * width :].T
    by_inner, by_chosen = g_outs[:width].T, g_outs[width:].T
    points = (
        (
            exact(point_t[1], by_latent, 0),
            exact(by_latent, point[0], 1) + exact(by_strips, edge[0], 1),
        ),
        (g_mix[1, width : 2 * width, 3 * width :].T, exact(edge[1], by_inner, 0)),
    )
    edges = (g_edge[...].T, exact(by_inner, point[3], 1) + exact(by_chosen, point[2], 1))
    rows = groups // 2 * width
    for part in range(2):
        payload_ref[part, :rows] = g_table[part * rows : (part + 1) * rows, :LANES]
        payload_ref[part, rows : 2 * rows] = g_table[part * rows : (part + 1) * rows, LANES:]
        conv_rows = [g_mix[part, :width, k * width : (k + 1) * width].T for k in range(3)]
        edge_rows = jnp.concatenate([edges[part], jnp.zeros((width - 16, width), F32)], axis=0)
        after = 2 * rows
        for pair in (
            conv_rows[:2],
            (conv_rows[2], edge_rows),
            points[part],
        ):
            payload_ref[part, after : after + width] = jnp.concatenate(pair, axis=1)
            after += width
        payload_ref[part, after : after + 8] = stats
        after += 8
        rest = payload_ref.shape[1] - after
        if rest:
            payload_ref[part, after:] = jnp.zeros((rest, LANES), F32)


def net(rows, lengths, wave, codes, weights):
    sets, per_clip = wave.shape[:2]
    clips = 8 * sets
    width = 64
    table_rows = 2 * (weights.shape[1] - 4 * width - 16)
    slots = SLOTS * TILE // LANES
    vmem = pl.BlockSpec(memory_space=pltpu.VMEM)

    def ring(rows, dtype):
        return pltpu.VMEM((slots, rows, LANES), dtype)

    return pl.pallas_call(
        net_kernel,
        out_shape=jax.ShapeDtypeStruct((2, rows, LANES), F32),
        in_specs=[pl.BlockSpec(memory_space=pl.ANY)] * 4,
        out_specs=vmem,
        scratch_shapes=[
            pltpu.SMEM(lengths.shape, lengths.dtype),
            pltpu.VMEM(wave.shape, wave.dtype),
            pltpu.VMEM(codes.shape, codes.dtype),
            pltpu.VMEM(weights.shape, weights.dtype),
            pltpu.SemaphoreType.DMA((4,)),
            pltpu.VMEM((2, 2 * width + 16, 4 * width), F32),
            pltpu.VMEM((2 * width, 16), F32),
            pltpu.VMEM((width, 16), F32),
            pltpu.VMEM((table_rows, LOW), F32),
            pltpu.VMEM((8, LANES), F32),
            pltpu.VMEM((per_clip, clips, LANES), F32),
            pltpu.VMEM((per_clip, clips, LANES), F32),
            pltpu.VMEM((per_clip, clips, LANES), F32),
            *(ring(8, F32) for _ in range(4)),
            ring(16, BF16),
            ring(8, F32),
            *(ring(16, BF16) for _ in range(2)),
            ring(LOW, BF16),
            *(ring(width, BF16) for _ in range(6)),
            ring(16, F32),
            ring(16, BF16),
            *(ring(width, BF16) for _ in range(3)),
        ],
        compiler_params=pltpu.CompilerParams(vmem_limit_bytes=60 * 2**20),
    )(lengths, wave, codes, weights)


def remote(src, dst, send, recv, to):
    return pltpu.make_async_remote_copy(
        src_ref=src, dst_ref=dst, send_sem=send, recv_sem=recv, device_id=to, device_id_type=MESH
    )


def share_kernel(items, *refs):
    sources, (len_out, wave_out, ids_out, weight_out), inputs = refs[:7], refs[7:11], refs[11:18]
    len_ref, wave_ref, ids_ref, conv_ref, point_ref, edge_ref, table_ref = inputs
    len_scr, wave_scr, ids_scr, weight_scr, sems, load_sems = refs[18:]
    loads = [
        pltpu.make_async_copy(source, place, load_sems.at[k])
        for k, (source, place) in enumerate(zip(sources, inputs))
    ]
    for load in loads:
        load.start()
    item = lax.axis_index("item")
    pipe = lax.axis_index("pipe")
    partner = (item, 1 - pipe)
    mirror = (items - 1 - item, pipe)
    per_clip = wave_out.shape[1]
    width = conv_ref.shape[1]
    table_rows = weight_scr.shape[1] - 4 * width - 16

    barrier = pltpu.get_barrier_semaphore()
    for other in (partner, mirror):
        pl.semaphore_signal(barrier, inc=1, device_id=other, device_id_type=MESH)

    row_at = lax.broadcasted_iota(jnp.int32, (2 * LANES, 2 * LANES), 0)
    col_at = lax.broadcasted_iota(jnp.int32, (2 * LANES, 2 * LANES), 1)
    wanted = jnp.where(col_at < LANES, 2 * col_at, 2 * (col_at - LANES) + 1)
    split = jnp.where(row_at == wanted, 1.0, 0.0).astype(BF16)
    on_first = pipe == 0
    for load in loads[:3]:
        load.wait()
    lane = lax.broadcasted_iota(jnp.int32, (8, LANES), 1)
    kept = jnp.zeros((8, LANES), jnp.int32)
    given = kept
    for k in range(8):
        kept = jnp.where(lane == k, jnp.where(on_first, len_ref[k], len_ref[8 + k]), kept)
        given = jnp.where(lane == k, jnp.where(on_first, len_ref[24 + k], len_ref[16 + k]), given)
    len_out[:8] = kept
    len_scr[0] = given
    clips = wave_ref.shape[0]
    strips = [wave_ref[:, k * 2 * LANES : (k + 1) * 2 * LANES] for k in range(per_clip)]
    parted = nn(jnp.concatenate(strips, axis=0), split)

    def chosen(values, first, second):
        return jnp.where(on_first, values[8 * first :][:8], values[8 * second :][:8])

    def both(values, first, second):
        pair = [
            chosen(side, first, second) for side in (values[:, :LANES], values[:, LANES:])
        ]
        return jnp.concatenate(pair, axis=0).astype(BF16)

    codes = [ids_ref[:, k * LANES : (k + 1) * LANES] for k in range(per_clip)]
    for k in range(per_clip):
        values = parted[clips * k : clips * (k + 1)]
        wave_scr[0, k] = both(values, 3, 2)
        wave_out[0, k] = both(values, 0, 1)
        ids_out[0, k] = chosen(codes[k], 0, 1)
    for k in range(per_clip // 2):
        pair = [chosen(codes[2 * k + j], 3, 2) for j in range(2)]
        ids_scr[0, k] = jnp.concatenate(pair, axis=0).astype(jnp.int16)

    pl.semaphore_wait(barrier, 2)
    copies = [
        remote(ref.at[0], ref.at[1], sems.at[2 * k], sems.at[2 * k + 1], mirror)
        for k, ref in enumerate((len_scr, wave_scr, ids_scr))
    ]
    for copy in copies:
        copy.start()

    for load in loads[3:]:
        load.wait()
    groups = table_rows // width
    for h in range(groups):
        weight_scr[0, h * width : (h + 1) * width] = table_ref[:, h * LOW : (h + 1) * LOW].astype(
            BF16
        )
    blank = jnp.zeros((width, LOW - 3 * width), F32)
    conv = conv_ref[0]
    conv_t = [conv[:, k * width : (k + 1) * width].T for k in range(3)]
    points = [point_ref[0, 0], point_ref[0, 1]]
    edge = edge_ref[0]
    empty = jnp.zeros((6, width), F32)
    edge_t = jnp.concatenate([edge[1:3], empty, edge[3:], edge[:1], empty], axis=0)
    edge_square = jnp.concatenate([edge_t, jnp.zeros((width - 16, width), F32)], axis=0).T
    after = table_rows
    for pieces in (
        [conv, blank],
        conv_t + [blank],
        points + [value.T for value in points],
        [edge_square, jnp.zeros((width, LOW - width), F32)],
        [edge_t, jnp.zeros((16, LOW - width), F32)],
    ):
        value = jnp.concatenate(pieces, axis=1).astype(BF16)
        weight_scr[0, after : after + value.shape[0]] = value
        after += value.shape[0]
    over = remote(weight_scr.at[0], weight_scr.at[1], sems.at[6], sems.at[7], partner)
    over.start()
    weight_out[pipe] = weight_scr[0]
    over.wait()
    weight_out[1 - pipe] = weight_scr[1]
    for copy in copies:
        copy.wait()
    len_out[8:] = len_scr[1]
    wave_out[1] = wave_scr[1]
    for k in range(per_clip // 2):
        pair = ids_scr[1, k].astype(jnp.int32)
        ids_out[1, 2 * k], ids_out[1, 2 * k + 1] = pair[:8], pair[8:]


def shared(items, lengths, waveform, code_ids, conv, point, edge, table):
    per_clip = code_ids.shape[1] // LANES
    width = conv.shape[1]
    weight_rows = table.shape[1] // LOW * width + 4 * width + 16
    vmem = pl.BlockSpec(memory_space=pltpu.VMEM)
    wave_shape = (2, per_clip, 16, LANES)
    ids_shape = (2, per_clip, 8, LANES)
    weight_shape = (2, weight_rows, LOW)
    return pl.pallas_call(
        functools.partial(share_kernel, items),
        out_shape=(
            jax.ShapeDtypeStruct((16, LANES), jnp.int32),
            jax.ShapeDtypeStruct(wave_shape, BF16),
            jax.ShapeDtypeStruct(ids_shape, jnp.int32),
            jax.ShapeDtypeStruct(weight_shape, BF16),
        ),
        in_specs=[pl.BlockSpec(memory_space=pl.ANY)] * 7,
        out_specs=(vmem,) * 4,
        scratch_shapes=[pltpu.SMEM(lengths.shape, jnp.int32)]
        + [
            pltpu.VMEM(value.shape, value.dtype)
            for value in (waveform, code_ids, conv, point, edge, table)
        ]
        + [
            pltpu.VMEM((2, 8, LANES), jnp.int32),
            pltpu.VMEM(wave_shape, BF16),
            pltpu.VMEM((2, per_clip // 2, 16, LANES), jnp.int16),
            pltpu.VMEM(weight_shape, BF16),
            pltpu.SemaphoreType.DMA((8,)),
            pltpu.SemaphoreType.DMA((7,)),
        ],
        compiler_params=pltpu.CompilerParams(
            collective_id=0, has_side_effects=True, vmem_limit_bytes=60 * 2**20
        ),
    )(lengths, waveform, code_ids, conv, point, edge, table)


def sum_kernel(
    items,
    stats_row,
    payload_ref,
    sum_ref,
    own,
    crossed,
    part,
    landed,
    whole,
    own_sem,
    cross_send,
    cross_recv,
    out_send,
    out_recv,
    back_send,
    back_recv,
):
    item = lax.axis_index("item")
    pipe = lax.axis_index("pipe")
    partner = (item, 1 - pipe)
    piece = part.shape[1]

    def peer(d):
        if items & (items - 1):
            return lax.rem(item + d, items)
        return jnp.bitwise_xor(item, items - d)

    def peer_back(d):
        return lax.rem(item + d, items)

    def rows_of(k):
        return pl.ds(pl.multiple_of(k * piece, piece), piece)

    load = pltpu.make_async_copy(payload_ref.at[pipe], own, own_sem)
    load.start()
    barrier = pltpu.get_barrier_semaphore()
    pl.semaphore_signal(barrier, inc=1, device_id=partner, device_id_type=MESH)

    @pl.loop(1, items)
    def _(d):
        pl.semaphore_signal(barrier, inc=1, device_id=(peer(d), pipe), device_id_type=MESH)

    pl.semaphore_wait(barrier, items)

    def cross_copy(k):
        return remote(
            payload_ref.at[1 - pipe, rows_of(k)], crossed.at[rows_of(k)],
            cross_send.at[k], cross_recv.at[k], partner,
        )

    @pl.loop(1, items)
    def _(d):
        cross_copy(peer(d)).start()

    cross_copy(item).start()
    load.wait()

    def out_copy(to, place):
        return remote(
            part.at[to], landed.at[place], out_send.at[to], out_recv.at[place], (to, pipe)
        )

    @pl.loop(1, items)
    def _(d):
        to = peer(d)
        cross_copy(to).wait_recv()
        part[to] = (own[rows_of(to)] + crossed[rows_of(to)]).astype(BF16)
        out_copy(to, item).start()

    cross_copy(item).wait_recv()
    total = own[rows_of(item)] + crossed[rows_of(item)]
    stats = own[stats_row : stats_row + 8] + crossed[stats_row : stats_row + 8]
    high = stats.astype(BF16).astype(F32)
    middle = (stats - high).astype(BF16).astype(F32)
    low = stats - high - middle
    sub = lax.broadcasted_iota(jnp.int32, (8, LANES), 0)
    message = jnp.where(sub < 2, high, jnp.where(sub < 4, middle, jnp.where(sub < 6, low, 0.0)))
    whole[item, piece:] = jnp.concatenate([message, jnp.zeros_like(message)], axis=0).astype(BF16)

    def take(d, total):
        source = peer(d)
        out_copy(source, source).wait_recv()
        return total + landed[source].astype(F32)

    total = lax.fori_loop(1, items, take, total)
    whole[item, :piece] = total.astype(BF16)

    def back_copy(place, to):
        return remote(
            whole.at[place], whole.at[place], back_send.at[to], back_recv.at[place], (to, pipe)
        )

    @pl.loop(1, items)
    def _(d):
        back_copy(item, peer_back(d)).start()

    sum_ref[rows_of(item)] = whole[item, :piece].astype(F32)

    @pl.loop(1, items)
    def _(d):
        to = peer(d)
        cross_copy(to).wait_send()
        out_copy(to, item).wait_send()

    cross_copy(item).wait_send()

    def gather(d, stats):
        source = peer_back(d)
        back_copy(source, source).wait_recv()
        sum_ref[rows_of(source)] = whole[source, :piece].astype(F32)
        return stats + whole[source, piece:].astype(F32)[:8]

    stats = lax.fori_loop(1, items, gather, whole[item, piece:].astype(F32)[:8])
    sum_ref[stats_row : stats_row + 8] = stats

    @pl.loop(1, items)
    def _(d):
        back_copy(item, peer(d)).wait_send()


def summed(items, stats_row, payload):
    rows = payload.shape[1]
    piece = rows // items
    vmem = pl.BlockSpec(memory_space=pltpu.VMEM)
    sems = pltpu.SemaphoreType.DMA((items,))
    return pl.pallas_call(
        functools.partial(sum_kernel, items, stats_row),
        out_shape=jax.ShapeDtypeStruct((rows, LANES), F32),
        in_specs=[pl.BlockSpec(memory_space=pl.ANY)],
        out_specs=vmem,
        scratch_shapes=[
            pltpu.VMEM((rows, LANES), F32),
            pltpu.VMEM((rows, LANES), F32),
            pltpu.VMEM((items, piece, LANES), BF16),
            pltpu.VMEM((items, piece, LANES), BF16),
            pltpu.VMEM((items, piece + 16, LANES), BF16),
            pltpu.SemaphoreType.DMA,
        ]
        + [sems] * 6,
        compiler_params=pltpu.CompilerParams(
            collective_id=1, has_side_effects=True, vmem_limit_bytes=16 * 2**20
        ),
    )(payload)


def update_kernel(*refs):
    rate_net, rate_code, sum_ref = refs[:3]
    states = refs[3:15]
    loss_ref = refs[15]
    results = refs[16:]
    width = states[0].shape[1]
    groups = states[3].shape[1] // LOW
    rows = groups * width
    stats_row = 2 * rows + 3 * width
    stats = sum_ref[stats_row : stats_row + 8]
    odd = jnp.bitwise_and(lax.broadcasted_iota(jnp.int32, stats.shape, 0), 1) == 1
    counts = jnp.where(odd, stats, 0.0)
    loss_ref[0] = jnp.sum(jnp.where(odd, 0.0, stats)) / jnp.sum(counts)
    scale = 1.0 / jnp.sum(counts, keepdims=True)

    def step(kind, place, grad, rate):
        weight_ref, moment_ref, average_ref = (states[4 * j + kind] for j in range(3))
        new_ref, moment_new_ref, average_new_ref, copy_ref = results[4 * kind : 4 * kind + 4]
        grad = grad * scale
        moment = MOMENTUM * moment_ref[place] + grad
        weight = weight_ref[place] - rate * (grad + MOMENTUM * moment)
        new_ref[place] = weight
        moment_new_ref[place] = moment
        average_new_ref[place] = AVERAGE * average_ref[place] + (1.0 - AVERAGE) * weight
        copy_ref[place] = weight.astype(BF16)

    for h in range(groups):
        for side in range(LOW // LANES):
            start = h * LOW + side * LANES
            grad = sum_ref[side * rows + h * width : side * rows + (h + 1) * width]
            place = (slice(None), slice(start, start + LANES))
            step(3, place, -grad, rate_code[0])
    first, second, third = (
        sum_ref[2 * rows + k * width : 2 * rows + (k + 1) * width] for k in range(3)
    )
    rate = rate_net[0]
    step(0, 0, jnp.concatenate([first, second[:, :width]], axis=1), rate)
    step(1, (0, 0), third[:, :width], rate)
    step(1, (0, 1), third[:, width:], rate)
    edge = [second[k : k + 1, width:] for k in (9, 0, 1, 8)]
    step(2, 0, jnp.concatenate(edge, axis=0), rate)


def updated(rates, sums, states):
    smem = pl.BlockSpec(memory_space=pltpu.SMEM)
    shapes = [jax.ShapeDtypeStruct((1,), F32)]
    for weight in states[:4]:
        shapes += [jax.ShapeDtypeStruct(weight.shape, F32)] * 3
        shapes += [jax.ShapeDtypeStruct(weight.shape, BF16)]
    def block(value):
        return pl.BlockSpec(value.shape, lambda i: (0,) * len(value.shape))

    return pl.pallas_call(
        update_kernel,
        grid=(1,),
        out_shape=tuple(shapes),
        in_specs=[smem] * 2 + [block(value) for value in (sums, *states)],
        out_specs=(smem,) + tuple(block(value) for value in shapes[1:]),
        compiler_params=pltpu.CompilerParams(vmem_limit_bytes=24 * 2**20),
    )(*rates, sums, *states)


def per_device(
    waveform,
    lengths,
    code_ids,
    conv_w,
    point_w,
    edge_w,
    codebook,
    conv_mom,
    point_mom,
    edge_mom,
    code_mom,
    conv_avg,
    point_avg,
    edge_avg,
    code_avg,
    rate_net,
    rate_code,
):
    width = conv_w.shape[1]
    items = lax.axis_size("item")
    edge_w, edge_mom, edge_avg = (jnp.swapaxes(v, 1, 2) for v in (edge_w, edge_mom, edge_avg))
    codebook, code_mom, code_avg = (v.T for v in (codebook, code_mom, code_avg))
    rows = 2 * (codebook.shape[1] // LOW) * width + 3 * width
    piece = -(-(rows + 8) // (16 * items)) * 16
    own_inputs = shared(items, lengths, waveform, code_ids, conv_w, point_w, edge_w, codebook)
    payload = net(piece * items, *own_inputs)
    sums = summed(items, rows, payload)
    states = (
        conv_w, point_w, edge_w, codebook,
        conv_mom, point_mom, edge_mom, code_mom,
        conv_avg, point_avg, edge_avg, code_avg,
    )
    loss, *rest = updated((rate_net, rate_code), sums, states)
    edges = (jnp.swapaxes(v, 1, 2) for v in rest[8:12])
    return (loss.reshape(()), *rest[:8], *edges, *(v.T for v in rest[12:]))


def solution(mesh):
    weights = (
        P("pipe", None, None),
        P("pipe", None, None, None),
        P("pipe", None, None),
        P("pipe", None),
    )
    return jax.shard_map(
        per_device,
        mesh=mesh,
        in_specs=(P("item", None), P("item"), P("item", None), *weights, *weights, *weights, P(), P()),
        out_specs=(P(),) + tuple(spec for spec in weights for _ in range(4)),
        check_vma=False,
    )
```
